32 devices in a mesh: rep: 8 (over y, x, core), shard: 4 (over z).
Axes of the slice: x: 2, y: 2, z: 4, core: 2. Of those that a mesh axis runs over, the one named last changes fastest.
Arguments:
- inputs: bfloat16 [16384, 1536], P(('rep', 'shard')), may hold values from -6 to 6
- query_key_value_weight: bfloat16 [1536, 2560], P('shard'), may hold values from -0.15625 to 0.15625
- output_weight: bfloat16 [1536, 1536], P('shard'), may hold values from -1.25 to 1.25
- attention_gain: bfloat16 [1536], P('shard'), may hold values from 0.25 to 1.75
- feed_gain: bfloat16 [1536], P('shard'), may hold values from 0.25 to 1.75
- router_weight: bfloat16 [1536, 16], P('shard'), may hold values from -0.078125 to 0.078125
- expert_weight: bfloat16 [16, 1536, 1536], P('shard'), may hold values from -3 to 3, as said below
- routes: int32 [16384, 8], P(('rep', 'shard')), may hold values from 0 to 15, all different within a row; in each aligned block of 512 rows (0 to 511, 512 to 1023, ...) at most 320 rows name the same one
- cotangent: bfloat16 [16384, 1536], P(('rep', 'shard')), may hold values from -6 to 6
Outputs:
- activations: bfloat16 [16384, 1536], P(('rep', 'shard'))
- input_grad: bfloat16 [16384, 1536], P(('rep', 'shard'))
- attend_grad: float32 [1536, 2560], P('shard')
- output_grad: float32 [1536, 1536], P('shard')
- attention_gain_grad: float32 [1536], P('shard')
- feed_gain_grad: float32 [1536], P('shard')
- router_grad: float32 [1536, 16], P('shard')
- expert_grad: float32 [16, 1536, 1536], P('shard')
The draws below stay inside these ranges and needn't reach their ends.
Inputs may be any that keep to these rules, and one draw needn't show every extreme that they name: `routes`: each row names 8 different experts. Among the rows of one device no expert is named more than 320 times, and in some device's rows an expert is named exactly 320 times. `expert_weight`: columns 0 to 1023 of each expert's matrix are its gate then up projection, the last 512 columns its down projection transposed.
All inputs are finite; a program needn't handle non-finite values.
Results may differ from the reference program's by a relative error of at most 0.02.
Values may be sent and summed in bfloat16 or wider, within the bound.
No kernel may reach another device: no remote copies, remote signals or barrier semaphores. Data moves between devices by JAX's collectives and lax.ppermute only.
A program may use at most 576 MiB of HBM per device.

```python
import math
import jax
import jax.numpy as jnp
import numpy as np
from jax import lax

MODEL_WIDTH = 1536
QUERY_HEADS = 24
KEY_VALUE_HEADS = 8
HEAD_WIDTH = 64
FF = 512
TOPK = 8
EXPERTS = 16
TOK_DEV = 512
CAP = 320
TOKENS = 16384


def draw_expert_weight(key, part):
    key = jax.random.fold_in(key, 11)
    base = jax.random.truncated_normal(key, -4.0, 4.0, (EXPERTS, MODEL_WIDTH, 3 * FF), jnp.float32)
    columns = jnp.arange(3 * FF)
    scale = jnp.where(columns < 2 * FF, MODEL_WIDTH ** (-0.5), 4.0 * FF ** (-0.5)).astype(jnp.float32)
    return (base * scale[None, None, :]).astype(jnp.bfloat16)


def shard_levels(rng, shape, shards, least, top_value):
    loudness = 1.0
    for position, parts in shards:
        draws = jax.random.uniform(jax.random.fold_in(jax.random.fold_in(rng, 6), position), (parts,), jnp.float32, least / len(shards), top_value / len(shards))
        loudness = loudness * jnp.repeat(jnp.exp(draws), shape[position] // parts).reshape((-1,) + (1,) * (len(shape) - 1 - position))
    return loudness


def shared_out(key, own, number, rows, count, top, most, lean):
    ranking = jax.random.permutation(key, count)
    heavy_load, usual = portions_of(count, rows * top, most, lean, True), portions_of(count, rows * top, most, lean, False)
    places = jnp.arange(count)

    def named(sizes, rotation):
        used = int((sizes > 0).sum())
        fixed = max(1, used // 4)
        shifted = fixed + (places - fixed + rotation * (used - fixed)) % max(1, count - fixed)
        return jnp.zeros((count,), jnp.int32).at[ranking[jnp.where(places < fixed, places, shifted)]].set(jnp.asarray(sizes, jnp.int32))

    sizes = jnp.where(number % 4 == 0, named(heavy_load, number // 4), named(usual, number - number // 4 - 1))
    mixed = jax.random.permutation(jax.random.fold_in(own, 3), count)
    donor, taker = mixed[0:count // 2 * 2:2], mixed[1:count // 2 * 2:2]
    slack = jnp.minimum(sizes[donor] - 1, most - sizes[taker]) // 2
    slack = jnp.where((donor == ranking[0]) | (taker == ranking[0]) | (sizes[taker] == 0), 0, jnp.maximum(slack, 0))
    shifted = jax.random.randint(jax.random.fold_in(own, 4), (count // 2,), 0, 1 << 20) % (slack + 1)
    sizes = sizes.at[donor].add(-shifted).at[taker].add(shifted)
    items = jnp.searchsorted(jnp.cumsum(sizes), jnp.arange(rows * top), side="right").astype(jnp.int32)
    listing = items.reshape(top, rows).T
    listing = listing[jax.random.permutation(jax.random.fold_in(own, 1), rows)]
    rotation = jax.random.randint(jax.random.fold_in(own, 2), (rows, 1), 0, top)
    return jnp.take_along_axis(listing, (jnp.arange(top)[None, :] + rotation) % top, axis=1)


def portions_of(count, total, reach, slope, full):
    portions = [(1 << 20) // math.isqrt(grade ** slope) + 1 for grade in range(1, count + 1)]
    largest = reach if full else min(reach, max(-(-total // count), total * portions[0] // sum(portions)))
    least = 1 if total - largest >= count - 1 else 0
    given, rest = [largest] + [least] * (count - 1), total - largest - least * (count - 1)
    while rest > 0:
        candidates = [i for i in range(1, count) if given[i] < largest] or [i for i in range(1, count) if given[i] < reach]
        pool, left = sum([portions[i] for i in candidates]), rest
        for i in candidates:
            more = min(reach - given[i], max(1, left * portions[i] // pool), rest)
            given[i] = given[i] + more
            rest = rest - more
    return np.array(given)


def gaussian(rng, dims, width, limit, shards=(), kind=jnp.bfloat16):
    values = width * jax.random.normal(rng, dims, jnp.float32)
    if shards:
        values = values * shard_levels(rng, dims, shards, -0.22, 0.18)
    return jnp.clip(values, -limit, limit).astype(kind)


def setup_inputs(seed: int = 0) -> dict:
    streams_of = jax.random.split(jax.random.key(seed), 10)
    inputs = gaussian(streams_of[0], (TOKENS, MODEL_WIDTH), 1.0, 6.0, ((0, 32),))
    query_key_value_weight = gaussian(streams_of[1], (MODEL_WIDTH, (QUERY_HEADS + 2 * KEY_VALUE_HEADS) * HEAD_WIDTH), MODEL_WIDTH ** -0.5, 0.15625, ((0, 4),))
    output_weight = gaussian(streams_of[2], (MODEL_WIDTH, QUERY_HEADS * HEAD_WIDTH), (QUERY_HEADS * HEAD_WIDTH // 64) ** -0.5, 1.25, ((0, 4),))
    attention_gain = jnp.clip(1.0 + 0.15 * jax.random.normal(streams_of[3], (MODEL_WIDTH,), jnp.float32), 0.25, 1.75).astype(jnp.bfloat16)
    feed_gain = jnp.clip(1.0 + 0.15 * jax.random.normal(streams_of[4], (MODEL_WIDTH,), jnp.float32), 0.25, 1.75).astype(jnp.bfloat16)
    router_weight = gaussian(streams_of[5], (MODEL_WIDTH, EXPERTS), (4 * MODEL_WIDTH) ** -0.5, 0.078125, ((0, 4),))
    expert_weight = draw_expert_weight(jax.random.fold_in(streams_of[9], 71), 0)
    routes_keys = jax.random.split(jax.random.fold_in(streams_of[7], 1), TOKENS // TOK_DEV)
    routes_turns = jax.random.permutation(jax.random.fold_in(streams_of[7], 3), TOKENS // TOK_DEV)
    routes = jax.vmap(lambda own, number: shared_out(jax.random.fold_in(streams_of[7], 2), own, number, TOK_DEV, EXPERTS, TOPK, CAP, 1))(routes_keys, routes_turns).reshape((TOKENS, TOPK))
    cotangent = gaussian(streams_of[8], (TOKENS, MODEL_WIDTH), 1.0, 6.0, ((0, 32),))
    return dict(inputs=inputs, query_key_value_weight=query_key_value_weight, output_weight=output_weight, attention_gain=attention_gain, feed_gain=feed_gain, router_weight=router_weight, expert_weight=expert_weight, routes=routes, cotangent=cotangent)


@jax.custom_vjp
def lower_part(v):
    return lax.optimization_barrier(v.astype(jnp.bfloat16)).astype(jnp.float32)

@jax.custom_vjp
def low_back(v):
    return v

def low_keep(v):
    return (lower_part(v), None)

def low_pass(kept, grad):
    return (grad,)

def back_keep(v):
    return (v, None)

def back_low(kept, grad):
    return (lower_part(grad),)
lower_part.defvjp(low_keep, low_pass)
low_back.defvjp(back_keep, back_low)
EPSILON = 1e-06
MASKED = -1e+30
HIGHEST = lax.Precision.HIGHEST

def rms_scaled(value_rows):
    return value_rows * lax.rsqrt(lax.optimization_barrier(jnp.mean(value_rows * value_rows, axis=-1, keepdims=True)) + EPSILON)

def rotary_tables(sequence_length, head_size):
    half_size = head_size // 2
    frequency = 10000.0 ** (-2.0 * jnp.arange(half_size, dtype=jnp.float32) / head_size)
    angles = jnp.arange(sequence_length, dtype=jnp.float32)[:, None] * frequency[None, :]
    return (jnp.cos(angles)[:, None, :], jnp.sin(angles)[:, None, :])

def apply_rotation(value_rows, cosine_table, sine_values):
    half_size = value_rows.shape[-1] // 2
    lower_half = value_rows[..., :half_size]
    upper_half = value_rows[..., half_size:]
    return jnp.concatenate([lower_half * cosine_table - upper_half * sine_values, upper_half * cosine_table + lower_half * sine_values], axis=-1)

def slot_tables(routes):
    sequence_length = routes.shape[0]
    listed = routes.reshape(-1).astype(jnp.int32)
    hits = (listed[:, None] == jnp.arange(EXPERTS, dtype=jnp.int32)[None, :]).astype(jnp.int32)
    earlier = (jnp.cumsum(hits, axis=0).astype(jnp.int32) - hits).astype(jnp.int32)
    places = lax.optimization_barrier(jnp.sum(earlier * hits, axis=1)).astype(jnp.int32)
    flat_slot = (listed * CAP + places).astype(jnp.int32)
    owners = (jnp.arange(sequence_length * TOPK, dtype=jnp.int32) // TOPK).astype(jnp.int32)
    slot_token = jnp.zeros((EXPERTS * CAP,), jnp.int32).at[flat_slot].set(owners)
    filled = jnp.zeros((EXPERTS * CAP,), jnp.int32).at[flat_slot].set(1) > 0
    return (slot_token, filled, flat_slot.reshape(sequence_length, TOPK))

def attend(query_matrix, key_rows, value_rows):
    sequence_length = query_matrix.shape[0]
    rows_per_block = min(sequence_length, 512)
    head_groups = QUERY_HEADS // KEY_VALUE_HEADS
    query_block_count = query_matrix.reshape(sequence_length // rows_per_block, rows_per_block, KEY_VALUE_HEADS, head_groups, HEAD_WIDTH)
    offsets = jnp.arange(sequence_length // rows_per_block, dtype=jnp.int32) * rows_per_block
    key_place = jnp.arange(sequence_length, dtype=jnp.int32)

    def attend_block(block_inputs):
        query_rows, offset = block_inputs
        scores = low_back(jnp.einsum('qkgd,skd->kgqs', query_rows, key_rows, precision=HIGHEST) * HEAD_WIDTH ** (-0.5))
        allowed = key_place[None, :] <= offset + jnp.arange(rows_per_block, dtype=jnp.int32)[:, None]
        scores = jnp.where(allowed, scores, MASKED)
        probability = lower_part(jax.nn.softmax(scores, axis=-1))
        return jnp.einsum('kgqs,skd->qkgd', probability, value_rows, precision=HIGHEST)
    mixed = lax.map(jax.checkpoint(attend_block), (query_block_count, offsets))
    return mixed.reshape(sequence_length, QUERY_HEADS * HEAD_WIDTH)

def block_forward(inputs, query_key_value_weight, output_weight, attention_gain, feed_gain, router_weight, expert_weight, routes, tables):
    slot_token, filled, flat_slot = tables
    sequence_length = inputs.shape[0]
    query_total_width = QUERY_HEADS * HEAD_WIDTH
    key_total_width = KEY_VALUE_HEADS * HEAD_WIDTH
    cosine_table, sine_values = rotary_tables(sequence_length, HEAD_WIDTH)
    normed = lower_part(rms_scaled(inputs) * attention_gain)
    projected_rows = low_back(jnp.dot(normed, query_key_value_weight, precision=HIGHEST))
    query_matrix = lower_part(apply_rotation(projected_rows[:, :query_total_width].reshape(sequence_length, QUERY_HEADS, HEAD_WIDTH), cosine_table, sine_values))
    key_rows = lower_part(apply_rotation(projected_rows[:, query_total_width:query_total_width + key_total_width].reshape(sequence_length, KEY_VALUE_HEADS, HEAD_WIDTH), cosine_table, sine_values))
    value_rows = lower_part(projected_rows[:, query_total_width + key_total_width:].reshape(sequence_length, KEY_VALUE_HEADS, HEAD_WIDTH))
    mixed = lower_part(low_back(attend(query_matrix, key_rows, value_rows)))
    branch = jnp.dot(mixed, output_weight.T, precision=HIGHEST)
    middle = inputs + branch
    fed = lower_part(rms_scaled(middle) * feed_gain)
    logits = low_back(jnp.dot(fed, router_weight, precision=HIGHEST))
    gates = jax.nn.softmax(jnp.take_along_axis(logits, routes, axis=1), axis=-1)
    dispatched = low_back(jnp.where(filled[:, None], fed[slot_token], 0.0)).reshape(EXPERTS, CAP, MODEL_WIDTH)
    gate_up = jnp.einsum('ecd,edf->ecf', dispatched, expert_weight[:, :, :2 * FF], precision=HIGHEST)
    gate_up = low_back(gate_up)
    hidden = lower_part(jax.nn.silu(gate_up[..., :FF]) * gate_up[..., FF:])
    produced = jnp.einsum('ecf,edf->ecd', hidden, expert_weight[:, :, 2 * FF:], precision=HIGHEST)
    produced = lower_part(low_back(produced)).reshape(EXPERTS * CAP, MODEL_WIDTH)
    return middle + lax.optimization_barrier(jnp.sum(gates[:, :, None] * produced[flat_slot], axis=1))

def reference(inputs, query_key_value_weight, output_weight, attention_gain, feed_gain, router_weight, expert_weight, routes, cotangent):
    params = tuple((matrix.astype(jnp.float32) for matrix in (query_key_value_weight, output_weight, attention_gain, feed_gain, router_weight, expert_weight)))
    sequences = inputs.astype(jnp.float32).reshape(-1, TOK_DEV, MODEL_WIDTH)
    cotangents = cotangent.astype(jnp.float32).reshape(-1, TOK_DEV, MODEL_WIDTH)
    route_rows = routes.reshape(-1, TOK_DEV, TOPK)

    def sequence_step(totals, sequence_items):
        sequence, sequence_cot, sequence_routes = sequence_items
        tables = slot_tables(sequence_routes)

        def forward(sequence_in, attend_matrix, output_matrix, attention_vector, feed_vector, router_matrix, expert_matrix):
            return block_forward(sequence_in, attend_matrix, output_matrix, attention_vector, feed_vector, router_matrix, expert_matrix, sequence_routes, tables)
        result, pullback = jax.vjp(forward, sequence, params[0], params[1], params[2], params[3], params[4], params[5])
        gradients = pullback(sequence_cot)
        totals = tuple((running + update for running, update in zip(totals, gradients[1:])))
        return (totals, (result.astype(jnp.bfloat16), gradients[0].astype(jnp.bfloat16)))
    initial = tuple((jnp.zeros_like(matrix) for matrix in params))
    totals, (outputs, input_grads) = lax.scan(sequence_step, initial, (sequences, cotangents, route_rows))
    return (outputs.reshape(-1, MODEL_WIDTH), input_grads.reshape(-1, MODEL_WIDTH), totals[0], totals[1], totals[2], totals[3], totals[4], totals[5])
```

```python
import functools

import jax
import jax.numpy as jnp
from jax import lax
from jax.experimental import pallas as pl
from jax.experimental.pallas import tpu as pltpu
from jax.sharding import PartitionSpec as P

QUERY_HEADS = 24
KEY_VALUE_HEADS = 8
HEAD_WIDTH = 64
FF = 512
EXPERTS = 16

EPSILON = 1e-06
MASKED = -1e30

GROUP = QUERY_HEADS // KEY_VALUE_HEADS
PAIRS = KEY_VALUE_HEADS // 2
PAIR_QUERY = 2 * GROUP * HEAD_WIDTH
PAIR_KEY = 2 * HEAD_WIDTH
PAIR_WIDTH = PAIR_QUERY + 2 * PAIR_KEY
BLOCK = 256
LANES = 128
VMEM = 60 * 2**20


def cost(flops, moved):
    return pl.CostEstimate(flops=int(flops), bytes_accessed=int(moved), transcendentals=0)

bf16 = jnp.bfloat16
f32 = jnp.float32


def dot(left, right):
    return jnp.dot(left, right, preferred_element_type=f32)


def contract_rows(left, right):
    return lax.dot_general(left, right, (((0,), (0,)), ((), ())), preferred_element_type=f32)


def times_transposed(left, right):
    return lax.dot_general(left, right, (((1,), (1,)), ((), ())), preferred_element_type=f32)


def norm_rows(value_rows):
    inverse = lax.rsqrt(jnp.mean(value_rows * value_rows, axis=-1, keepdims=True) + EPSILON)
    return (value_rows * inverse, inverse)


def norm_back(scaled, inverse, upstream):
    return inverse * (upstream - scaled * jnp.mean(upstream * scaled, axis=-1, keepdims=True))


def rotary_tables(length, width):
    half = HEAD_WIDTH // 2
    frequency = 10000.0 ** (-2.0 * jnp.arange(half, dtype=f32) / HEAD_WIDTH)
    angles = jnp.arange(length, dtype=f32)[:, None] * frequency[None, :]
    cosine, sine = jnp.cos(angles), jnp.sin(angles)
    heads = width // HEAD_WIDTH
    return (
        jnp.tile(jnp.concatenate([cosine, cosine], axis=1), (1, heads)),
        jnp.tile(jnp.concatenate([-sine, sine], axis=1), (1, heads)),
    )


def rotate(values, cosine, sine):
    width = values.shape[1]
    half = HEAD_WIDTH // 2
    lane = lax.broadcasted_iota(jnp.int32, values.shape, 1)
    swapped = jnp.where(
        lane % HEAD_WIDTH < half,
        pltpu.roll(values, width - half, 1),
        pltpu.roll(values, half, 1),
    )
    return values * cosine + swapped * sine


def causal_block():
    shape = (BLOCK, BLOCK)
    return lax.broadcasted_iota(jnp.int32, shape, 0) <= lax.broadcasted_iota(jnp.int32, shape, 1)


def stack_rows(parts):
    return parts[0] if len(parts) == 1 else jnp.concatenate(parts, axis=0)


def attend_forward_kernel(
    own_ref, other_ref, own_weight_ref, other_weight_ref, cosine_ref, sine_ref, mixed_ref, qkv_ref, lse_ref
):
    length = own_ref.shape[0]
    keep = causal_block()
    projected = dot(own_ref[...], own_weight_ref[...].reshape(-1, PAIR_WIDTH)) + dot(
        other_ref[...], other_weight_ref[...].reshape(-1, PAIR_WIDTH)
    )
    rotated = rotate(projected[:, : PAIR_QUERY + PAIR_KEY], cosine_ref[...], sine_ref[...])
    query = (rotated[:, :PAIR_QUERY] * HEAD_WIDTH**-0.5).astype(bf16)
    key = rotated[:, PAIR_QUERY:].astype(bf16)
    value = projected[:, PAIR_QUERY + PAIR_KEY :].astype(bf16)
    qkv_ref[:, :PAIR_QUERY] = query
    qkv_ref[:, PAIR_QUERY : PAIR_QUERY + PAIR_KEY] = key
    qkv_ref[:, PAIR_QUERY + PAIR_KEY :] = value
    value_columns = value.T
    outs = []
    for head in range(2 * GROUP):
        kv = (head // GROUP) * HEAD_WIDTH
        columns = []
        for block in range(length // BLOCK):
            start, stop = block * BLOCK, (block + 1) * BLOCK
            scores = times_transposed(
                key[:stop, kv : kv + HEAD_WIDTH],
                query[start:stop, head * HEAD_WIDTH : (head + 1) * HEAD_WIDTH],
            )
            parts = [scores[:start]] if block else []
            scores = stack_rows(parts + [jnp.where(keep, scores[start:], MASKED)])
            top = jnp.max(scores, axis=0, keepdims=True)
            powers = jnp.exp(scores - top)
            total = jnp.sum(powers, axis=0, keepdims=True)
            probability = (powers * (1.0 / total)).astype(bf16)
            columns.append(dot(value_columns[kv : kv + HEAD_WIDTH, :stop], probability))
            lse_ref[head, start:stop] = (top + jnp.log(total))[0]
        outs.append(jnp.concatenate(columns, axis=1))
    mixed_ref[...] = jnp.concatenate(outs, axis=0).T.astype(bf16)


def attend_forward(halves, weights, cosine, sine):
    length = halves[0].shape[0]
    return pl.pallas_call(
        attend_forward_kernel,
        out_shape=[
            jax.ShapeDtypeStruct((length, PAIR_QUERY), bf16),
            jax.ShapeDtypeStruct((length, PAIR_WIDTH), bf16),
            jax.ShapeDtypeStruct((8, length), f32),
        ],
        compiler_params=pltpu.CompilerParams(vmem_limit_bytes=VMEM),
        cost_estimate=cost(5e9, 5e6),
    )(*halves, *weights, cosine, sine)


def output_kernel(*refs):
    mixed, own, other = refs[:PAIRS], refs[PAIRS : 2 * PAIRS], refs[2 * PAIRS : 3 * PAIRS]
    for out_ref, weights in zip(refs[3 * PAIRS :], (own, other)):
        total = None
        for m in range(PAIRS):
            added = times_transposed(mixed[m][...], weights[m][...].reshape(-1, PAIR_QUERY))
            total = added if total is None else total + added
        out_ref[...] = total


def output_product(mixed, weights):
    length = mixed[0].shape[0]
    half = weights[0][0].shape[0] * weights[0][0].shape[1]
    return pl.pallas_call(
        output_kernel,
        out_shape=[jax.ShapeDtypeStruct((length, half), f32)] * 2,
        compiler_params=pltpu.CompilerParams(vmem_limit_bytes=VMEM),
        cost_estimate=cost(2.4e9, 1e7),
    )(*mixed, *[w[0] for w in weights], *[w[1] for w in weights])


def attend_backward_kernel(
    own_branch_ref,
    other_branch_ref,
    own_output_ref,
    other_output_ref,
    qkv_ref,
    lse_ref,
    mixed_ref,
    own_normed_ref,
    other_normed_ref,
    own_weight_ref,
    other_weight_ref,
    cosine_ref,
    sine_ref,
    own_total_ref,
    other_total_ref,
    own_term_ref,
    other_term_ref,
    own_grad_ref,
    other_grad_ref,
):
    length = own_branch_ref.shape[0]
    keep = causal_block()
    blocks = length // BLOCK
    mixed_grad = (
        dot(own_branch_ref[...], own_output_ref[...].reshape(-1, PAIR_QUERY))
        + dot(other_branch_ref[...], other_output_ref[...].reshape(-1, PAIR_QUERY))
    ).astype(bf16)
    query = qkv_ref[:, :PAIR_QUERY]
    key = qkv_ref[:, PAIR_QUERY : PAIR_QUERY + PAIR_KEY]
    value = qkv_ref[:, PAIR_QUERY + PAIR_KEY :]
    scaled_key = (key.astype(f32) * HEAD_WIDTH**-0.5).T.astype(bf16)
    query_grads, key_grads, value_grads = [], [], []
    for side in range(2):
        kv = side * HEAD_WIDTH
        key_part = key[:, kv : kv + HEAD_WIDTH]
        value_part = value[:, kv : kv + HEAD_WIDTH]
        key_grad, value_grad = [None] * blocks, [None] * blocks
        for head in range(side * GROUP, (side + 1) * GROUP):
            column = head * HEAD_WIDTH
            columns = []
            for block in range(blocks):
                start, stop = block * BLOCK, (block + 1) * BLOCK
                query_rows = query[start:stop, column : column + HEAD_WIDTH]
                upstream = mixed_grad[start:stop, column : column + HEAD_WIDTH]
                scores = times_transposed(key_part[:stop], query_rows)
                prob_grad = times_transposed(value_part[:stop], upstream)
                probability = jnp.exp(scores - lse_ref[head, start:stop][None, :])
                parts = [probability[:start]] if block else []
                probability = stack_rows(parts + [jnp.where(keep, probability[start:], 0.0)])
                shift = jnp.sum(probability * prob_grad, axis=0, keepdims=True)
                score_grad = (probability * (prob_grad - shift)).astype(bf16)
                value_add = dot(probability.astype(bf16), upstream)
                key_add = dot(score_grad, query_rows)
                for j in range(block + 1):
                    rows = slice(j * BLOCK, (j + 1) * BLOCK)
                    value_grad[j] = (
                        value_add[rows] if value_grad[j] is None else value_grad[j] + value_add[rows]
                    )
                    key_grad[j] = (
                        key_add[rows] if key_grad[j] is None else key_grad[j] + key_add[rows]
                    )
                columns.append(dot(scaled_key[kv : kv + HEAD_WIDTH, :stop], score_grad))
            query_grads.append(jnp.concatenate(columns, axis=1))
        key_grads.append(stack_rows(key_grad))
        value_grads.append(stack_rows(value_grad))
    turned = rotate(
        jnp.concatenate([jnp.concatenate(query_grads, axis=0).T] + key_grads, axis=1),
        cosine_ref[...],
        -sine_ref[...],
    )
    projected_grad = jnp.concatenate([turned] + value_grads, axis=1).astype(bf16)
    for normed_ref, branch_ref, term_ref in (
        (own_normed_ref, own_branch_ref, own_term_ref),
        (other_normed_ref, other_branch_ref, other_term_ref),
    ):
        term_ref[:, :PAIR_WIDTH] = contract_rows(normed_ref[...], projected_grad).astype(bf16)
        term_ref[:, PAIR_WIDTH:] = contract_rows(branch_ref[...], mixed_ref[...]).astype(bf16)
    for total_ref, weight_ref, grad_ref in (
        (own_total_ref, own_weight_ref, own_grad_ref),
        (other_total_ref, other_weight_ref, other_grad_ref),
    ):
        added = times_transposed(projected_grad, weight_ref[...].reshape(-1, PAIR_WIDTH))
        grad_ref[...] = total_ref[...] + added


def attend_backward(branch, output, saved, normed, weights, tables, totals):
    length, half = branch[0].shape
    term = jax.ShapeDtypeStruct((half, PAIR_WIDTH + PAIR_QUERY), bf16)
    return pl.pallas_call(
        attend_backward_kernel,
        out_shape=[term, term] + [jax.ShapeDtypeStruct((length, half), f32)] * 2,
        input_output_aliases={13: 2, 14: 3},
        compiler_params=pltpu.CompilerParams(vmem_limit_bytes=VMEM),
        cost_estimate=cost(9e9, 1.5e7),
    )(
        *branch,
        *output,
        *saved,
        *normed,
        *weights,
        *tables,
        *totals,
    )


def expert_kernel(
    first_ref,
    fed_ref,
    upstream_ref,
    chosen_ref,
    router_ref,
    weight_ref,
    row_ref,
    combined_ref,
    gate_grad_ref,
    pair_ref,
    gated_ref,
    gates_ref,
    row_total,
    combined_total,
):
    step, steps = pl.program_id(0), pl.num_programs(0)
    index = first_ref[0] + step
    lane = lax.broadcasted_iota(jnp.int32, gates_ref.shape, 1)

    @pl.when(step == 0)
    def _():
        logits = dot(fed_ref[...], router_ref[...])
        chosen = chosen_ref[0] > 0.0
        logits = jnp.where(chosen, logits, MASKED)
        powers = jnp.where(chosen, jnp.exp(logits - jnp.max(logits, axis=1, keepdims=True)), 0.0)
        gates_ref[...] = powers / jnp.sum(powers, axis=1, keepdims=True)
        gate_grad_ref[...] = jnp.zeros_like(gate_grad_ref)

    gate = jnp.sum(jnp.where(lane == index, gates_ref[...], 0.0), axis=1, keepdims=True)
    gate_grad = None
    width = FF // 2
    for start in range(0, FF, width):
        stop = start + width
        gate_part = dot(fed_ref[...], weight_ref[0, :, start:stop])
        up_part = dot(fed_ref[...], weight_ref[0, :, FF + start : FF + stop])
        raw_grad = dot(upstream_ref[0], weight_ref[0, :, 2 * FF + start : 2 * FF + stop])
        sigma = jax.nn.sigmoid(gate_part)
        activated = gate_part * sigma
        hidden = activated * up_part
        part = jnp.sum(hidden * raw_grad, axis=1, keepdims=True)
        gate_grad = part if gate_grad is None else gate_grad + part
        hidden_grad = gate * raw_grad
        slope = sigma * (1.0 + gate_part * (1.0 - sigma))
        pair_ref[0, :, start:stop] = (hidden_grad * up_part * slope).astype(bf16)
        pair_ref[0, :, FF + start : FF + stop] = (hidden_grad * activated).astype(bf16)
        gated_ref[0, :, start:stop] = (gate * hidden).astype(bf16)
    gate_grad_ref[...] += jnp.where(lane == index, gate_grad, 0.0)
    combined = times_transposed(gated_ref[0], weight_ref[0, :, 2 * FF :])
    row = times_transposed(pair_ref[0], weight_ref[0, :, : 2 * FF])

    @pl.when(step == 0)
    def _():
        combined_total[...] = combined
        row_total[...] = row

    @pl.when(step > 0)
    def _():
        combined_total[...] += combined
        row_total[...] += row

    @pl.when(step == steps - 1)
    def _():
        row_ref[...] = row_total[...].astype(bf16)
        combined_ref[...] = combined_total[...].astype(bf16)


def expert_slot(places, fed, upstream, chosen, router, weights):
    length, features = fed.shape
    count = weights.shape[0]
    full = lambda *shape: pl.BlockSpec(shape, lambda e, at: (0,) * len(shape))
    each = lambda *shape: pl.BlockSpec((1,) + shape, lambda e, at: (e,) + (0,) * len(shape))
    there = lambda *shape: pl.BlockSpec((1,) + shape, lambda e, at: (at[1],) + (0,) * len(shape))
    return pl.pallas_call(
        expert_kernel,
        grid_spec=pltpu.PrefetchScalarGridSpec(
            num_scalar_prefetch=1,
            grid=(count,),
            in_specs=[
                full(length, features),
                there(length, features),
                there(length, LANES),
                full(features, LANES),
                each(features, 3 * FF),
            ],
            out_specs=[
                full(length, features),
                full(length, features),
                full(length, LANES),
                each(length, 2 * FF),
                each(length, FF),
            ],
            scratch_shapes=[
                pltpu.VMEM((length, LANES), f32),
                pltpu.VMEM((length, features), f32),
                pltpu.VMEM((length, features), f32),
            ],
        ),
        out_shape=[
            jax.ShapeDtypeStruct((length, features), bf16),
            jax.ShapeDtypeStruct((length, features), bf16),
            jax.ShapeDtypeStruct((length, LANES), f32),
            jax.ShapeDtypeStruct((count, length, 2 * FF), bf16),
            jax.ShapeDtypeStruct((count, length, FF), bf16),
        ],
        compiler_params=pltpu.CompilerParams(vmem_limit_bytes=VMEM),
        cost_estimate=cost(12 * count * length * features * FF, 3.2e7),
    )(places, fed, upstream, chosen, router, weights)


def expert_grad_kernel(places_ref, *refs):
    slots = (len(refs) - 1) // 4
    fed, upstream, pair, gated = (refs[i * slots : (i + 1) * slots] for i in range(4))
    out_ref = refs[-1]
    inner = outer = None
    for k in range(slots):
        add_inner = contract_rows(fed[k][...], pair[k][0])
        add_outer = contract_rows(upstream[k][0], gated[k][0])
        inner = add_inner if inner is None else inner + add_inner
        outer = add_outer if outer is None else outer + add_outer
    out_ref[0, :, : 2 * FF] = inner.astype(out_ref.dtype)
    out_ref[0, :, 2 * FF :] = outer.astype(out_ref.dtype)


def expert_grads(places, fed, upstream, pairs, gated):
    length, features = fed[0].shape
    slots, count = len(pairs), pairs[0].shape[0]
    rows = features // 2
    column = pl.BlockSpec((length, rows), lambda e, i, at: (0, i))
    there = lambda k: pl.BlockSpec((1, length, rows), lambda e, i, at: (at[k], 0, i))
    each = lambda width: pl.BlockSpec((1, length, width), lambda e, i, at: (e, 0, 0))
    return pl.pallas_call(
        expert_grad_kernel,
        grid_spec=pltpu.PrefetchScalarGridSpec(
            num_scalar_prefetch=1,
            grid=(count, features // rows),
            in_specs=[column] * slots
            + [there(k) for k in range(slots)]
            + [each(2 * FF)] * slots
            + [each(FF)] * slots,
            out_specs=pl.BlockSpec((1, rows, 3 * FF), lambda e, i, at: (e, i, 0)),
        ),
        out_shape=jax.ShapeDtypeStruct((count, features, 3 * FF), bf16),
        compiler_params=pltpu.CompilerParams(vmem_limit_bytes=VMEM),
        cost_estimate=cost(6 * slots * count * length * features * FF, 8e7),
    )(places, *fed, *[upstream] * slots, *pairs, *gated)


def exchange(value, k):
    return lax.ppermute(value, "shard", [(i, i ^ k) for i in range(4)])


def inside(place):
    return (place == 1) | (place == 2)


def sources(place, count):
    if count != 4:
        return [place ^ k for k in range(count)]
    middle = inside(place)
    order = ((1, 3), (2, 1), (3, 2))
    return [place] + [place ^ jnp.where(middle, mid, out) for out, mid in order]


def after(value, *earlier):
    return lax.optimization_barrier((value, earlier))[0]


def line_gather(rows, place, count):
    if count != 4:
        everything = lax.all_gather(rows, "shard", axis=0)
        for source in sources(place, count):
            yield pick(everything, source)
            yield
        return
    middle = inside(place)
    near = exchange(rows, 1)
    across = lax.ppermute(rows, "shard", [(1, 2), (2, 1)])
    made = yield rows
    yield
    near_on, across_on = after((near, across), made)
    second_inside = lax.ppermute(near_on, "shard", [(1, 2), (2, 1)])
    second_outside = lax.ppermute(across_on, "shard", [(1, 0), (2, 3)])
    made = yield jnp.where(middle, across, near)
    yield
    third_outside = lax.ppermute(after(second_inside, made), "shard", [(1, 0), (2, 3)])
    yield jnp.where(middle, near, second_outside)
    yield
    yield jnp.where(middle, second_inside, third_outside)
    yield


def line_scatter(parts, place, count):
    if count != 4:
        stacked = jnp.stack(parts)
        ordered = jnp.stack([pick(stacked, place ^ d) for d in range(count)])
        return lax.psum_scatter(ordered, "shard", scatter_dimension=0, tiled=False), []
    return parts[0], [come for k in range(1, 4) for come in line_send(parts[k], k)]


def line_send(part, k):
    ways = {
        1: ([(0, 1), (3, 2)], [(1, 2), (2, 1)]),
        2: ([(0, 2), (3, 1)], [(1, 0), (2, 3)]),
        3: ([(0, 3), (3, 0)], [(1, 3), (2, 0)]),
    }
    return [lax.ppermute(part, "shard", way) for way in ways[k]]


def total_of(kept, arrived):
    total = kept.astype(f32)
    for part in arrived:
        total = total + part.astype(f32)
    return total


def hop(value, bit):
    return lax.ppermute(value, "rep", [(i, i ^ bit) for i in range(8)])


def pick(stacked, index, axis=0):
    return lax.dynamic_index_in_dim(stacked, index, axis, False)


def gather_near(local, core, spot):
    mine = local(spot, core)
    return jnp.stack([exchange(mine, k) for k in range(1, 4)])


def send_pairs(near):
    return [hop(near, 2 * m) for m in range(1, 4)]


def join_pair(local, part, m, core, spot):
    own = jnp.concatenate([local(spot ^ m, core)[None], part])
    return own, hop(own, 1)


def halve_columns(rows, places, base, core):
    length, features = rows.shape
    parts = rows.reshape(length, places, 2, -1).transpose(2, 1, 0, 3)
    parts = jnp.stack([pick(parts, base ^ k, 1) for k in range(places)], axis=1)
    return [
        pick(parts, side).transpose(1, 0, 2).reshape(length, features // 2)
        for side in (core, 1 - core)
    ]


def join_columns(halves, places, base, core):
    length, width = halves[0].shape
    parts = jnp.stack(halves).reshape(2, length, places, -1).transpose(2, 0, 1, 3)
    parts = jnp.stack([pick(parts, base ^ k) for k in range(places)])
    parts = jnp.stack([pick(parts, core, 1), pick(parts, 1 - core, 1)], axis=1)
    return parts.transpose(2, 0, 1, 3).reshape(length, 2 * width)


def join_chip(term, special):
    kept, given = term
    return (kept.astype(f32) + hop(given, 1).astype(f32)).astype(bf16) if special else kept


def reduce_plane(terms, core, spot):
    kept, given = pick(terms, core, 2), pick(terms, 1 - core, 2)
    chip = (kept.astype(f32) + hop(given, 1).astype(f32)).astype(terms.dtype)
    total = pick(chip, spot).astype(f32)
    for m in range(1, 4):
        total = total + hop(pick(chip, spot ^ m), 2 * m).astype(f32)
    return total.astype(terms.dtype)


def finish_pairs(plane, core, spot):
    piece = plane[0].astype(f32)
    for k in range(1, 4):
        piece = piece + exchange(plane[k], k).astype(f32)
    piece = piece.astype(plane.dtype)
    mine = jnp.stack([piece] + [hop(piece, 2 * m) for m in range(1, 4)])
    other = hop(mine, 1)
    both = jnp.stack(
        [jnp.where(core == 0, mine, other), jnp.where(core == 0, other, mine)], axis=1
    )
    return jnp.stack([pick(both, spot ^ p) for p in range(4)])


def reduce_terms(terms, place, core, spot, special):
    if not special:
        part = lax.psum_scatter(terms, "shard", scatter_dimension=1, tiled=False)
        return lax.psum(part, "rep")
    plane = reduce_plane(terms, core, spot)
    plane = jnp.stack([pick(plane, place ^ k) for k in range(4)])
    return finish_pairs(plane, core, spot)


def body(
    inputs,
    query_key_value_weight,
    output_weight,
    attention_gain,
    feed_gain,
    router_weight,
    expert_weight,
    routes,
    cotangent,
    *,
    places,
    ranks,
):
    length, features = inputs.shape
    own = query_key_value_weight.shape[0]
    local = expert_weight.shape[0]
    query_width = QUERY_HEADS * HEAD_WIDTH
    key_width = KEY_VALUE_HEADS * HEAD_WIDTH
    place, rank = lax.axis_index("shard"), lax.axis_index("rep")

    special = places == 4 and ranks == 8
    half = own // 2
    base, core, spot = (place, rank % 2, rank // 2) if special else (0, 0, 0)

    projection = query_key_value_weight

    def projection_share(pair, side):
        rows = lax.dynamic_slice_in_dim(projection, side * half, half, 0)
        return jnp.concatenate(
            [
                lax.dynamic_slice_in_dim(rows, pair * PAIR_QUERY, PAIR_QUERY, 1),
                lax.dynamic_slice_in_dim(rows, query_width + pair * PAIR_KEY, PAIR_KEY, 1),
                lax.dynamic_slice_in_dim(
                    rows, query_width + key_width + pair * PAIR_KEY, PAIR_KEY, 1
                ),
            ],
            axis=1,
        )

    def output_share(weight, pair, side):
        return lax.dynamic_slice(
            weight, (side * half, pair * PAIR_QUERY), (half, PAIR_QUERY)
        )

    chosen_own = jnp.sum(
        (routes[:, :, None] == jnp.arange(EXPERTS, dtype=jnp.int32)).astype(f32), axis=1
    )
    small = jnp.concatenate(
        [feed_gain.reshape(-1), router_weight.reshape(-1), chosen_own.astype(bf16).reshape(-1)]
    )
    if special:
        projection_near = gather_near(projection_share, core, spot)
        projection_sent = send_pairs(projection_near)
        held, _ = lax.optimization_barrier((output_weight, projection_near))
        output_near = gather_near(functools.partial(output_share, held), core, spot)
        output_sent = send_pairs(lax.optimization_barrier((output_near, projection_sent))[0])

        def attend_weights(m, outs):
            part = after(projection_sent[m - 1], outs[0]) if m else projection_near
            return join_pair(projection_share, part, m, core, spot)

        output_weights = [
            join_pair(functools.partial(output_share, output_weight), part, m, core, spot)
            for m, part in enumerate([output_near] + output_sent)
        ]
        cotangent_sent, _ = lax.optimization_barrier((cotangent, projection_near))
        gains = jnp.stack([attention_gain] + [exchange(attention_gain, k) for k in range(1, 4)])
        gains = jnp.stack([pick(gains, place ^ k) for k in range(4)])
        small_slots = jnp.stack([small] + [exchange(small, k) for k in range(1, 4)])
        small_all = jnp.stack([pick(small_slots, place ^ k) for k in range(4)])
    else:
        whole = lax.all_gather(projection, "shard", axis=0)
        whole_output = lax.all_gather(output_weight, "shard", axis=0)
        attend_weights, output_weights = [], []
        for p in range(PAIRS):
            columns = jnp.concatenate(
                [
                    whole[:, :, p * PAIR_QUERY : (p + 1) * PAIR_QUERY],
                    whole[:, :, query_width + p * PAIR_KEY : query_width + (p + 1) * PAIR_KEY],
                    whole[:, :, query_width + key_width + p * PAIR_KEY :][:, :, :PAIR_KEY],
                ],
                axis=2,
            )
            attend_weights.append((columns[:, :half], columns[:, half:]))
            columns = whole_output[:, :, p * PAIR_QUERY : (p + 1) * PAIR_QUERY]
            output_weights.append((columns[:, :half], columns[:, half:]))
        gains = lax.all_gather(attention_gain, "shard", axis=0)
        small_all = lax.all_gather(small, "shard", axis=0)
        cotangent_sent = cotangent

    upstream_all = lax.all_gather(cotangent_sent, "shard", axis=0)

    cosine, sine = rotary_tables(length, PAIR_QUERY + PAIR_KEY)
    residual = inputs.astype(f32)
    scaled_in, inverse_in = norm_rows(residual)
    attention_scale = gains.reshape(features).astype(f32)
    normed = (scaled_in * attention_scale).astype(bf16)
    pair_outs, joined = [], []
    normed_halves = halve_columns(normed, places, base, core)
    for m in range(PAIRS):
        weights = attend_weights(m, pair_outs) if special else attend_weights[m]
        pair_outs.append(attend_forward(normed_halves, weights, cosine, sine))
        joined.append(weights)
    attend_weights = joined
    branch = output_product([out[0] for out in pair_outs], output_weights)
    middle = residual + join_columns(branch, places, base, core)
    scaled_mid, inverse_mid = norm_rows(middle)
    feed_scale = small_all[:, :own].reshape(features).astype(f32)
    router_full = small_all[:, own : (1 + EXPERTS) * own].reshape(features, EXPERTS)
    chosen_all = small_all[:, (1 + EXPERTS) * own :].reshape(places, length, EXPERTS).astype(f32)
    fed = (scaled_mid * feed_scale).astype(bf16)

    router_wide = jnp.pad(router_full, ((0, 0), (0, LANES - EXPERTS)))
    chosen_wide = jnp.pad(chosen_all, ((0, 0), (0, 0), (0, LANES - EXPERTS)))
    rows, combined, gate_grads, pair_grads, gated = [], [], [], [], []
    order = sources(place, places)
    fed_slots, arriving = [], line_gather(fed, place, places)
    rows_come = []
    for k, source in enumerate(order):
        fed_k = next(arriving)
        if special and k == 3:
            fed_k = after(fed_k, rows_come)
        fed_slots.append(fed_k)
        at = jnp.stack([place * local, source]).astype(jnp.int32)
        slot = expert_slot(
            at, fed_slots[k], upstream_all, chosen_wide, router_wide, expert_weight
        )
        for held, value in zip((rows, combined, gate_grads, pair_grads, gated), slot):
            held.append(value)
        arriving.send(slot[0])
        if special and k:
            rows_come += line_send(slot[0], k)
    expert_term = expert_grads(
        jnp.stack(order).astype(jnp.int32),
        after(fed_slots, rows_come[2:4]),
        upstream_all,
        pair_grads,
        gated,
    )
    expert_total = lax.psum(expert_term, "rep").astype(f32)

    row_sum = total_of(rows[0], rows_come) if special else total_of(*line_scatter(rows, place, places))
    row_sum = after(row_sum, expert_term)
    gate_grad = total_of(
        *line_scatter([g[:, :EXPERTS].T for g in gate_grads], place, places)
    ).T
    upstream = cotangent.astype(f32)
    logits = dot(fed, router_full)
    gates = jax.nn.softmax(jnp.where(chosen_own > 0.0, logits, -jnp.inf), axis=-1)
    logit_grad = (
        gates * (gate_grad - jnp.sum(gates * gate_grad, axis=-1, keepdims=True))
    ).astype(bf16)
    router_term = contract_rows(fed, logit_grad)
    fed_grad = times_transposed(logit_grad, router_full) + row_sum
    feed_term = jnp.sum(fed_grad * scaled_mid, axis=0)
    middle_grad = upstream + norm_back(scaled_mid, inverse_mid, fed_grad * feed_scale)
    branch_grad = middle_grad.astype(bf16)

    branch_halves = halve_columns(branch_grad, places, base, core)
    combined_kept, combined_come = line_scatter(after(combined, row_sum), place, places)
    totals = [jnp.zeros((length, features // 2), f32)] * 2
    terms, chips = [None] * PAIRS, [None] * PAIRS
    waits = {1: combined_come[:2], 2: [], 0: combined_come[2:4]}
    sent = []
    for m in (3, 1, 2, 0):
        if m == 2:
            chips[3] = join_chip(terms[3], special)
            waits[2] = [chips[3]]
        if m == 0:
            chips[1] = join_chip(terms[1], special)
            waits[0] = waits[0] + [chips[1]]
        own_term, other_term, *totals = attend_backward(
            after(branch_halves, *waits.get(m, [])),
            output_weights[m],
            (pair_outs[m][1], pair_outs[m][2], pair_outs[m][0]),
            normed_halves,
            attend_weights[m],
            (cosine, sine),
            totals,
        )
        terms[m] = (own_term, other_term)
    if special:
        chips[2], chips[0] = join_chip(terms[2], special), join_chip(terms[0], special)
        plane = chips[0].astype(f32)
        for m in (3, 1, 2):
            plane = plane + hop(chips[m], 2 * m).astype(f32)
        plane = plane.astype(bf16).reshape(places, half, -1)
        weight_sums = finish_pairs(after(plane, *combined_come[4:]), core, spot)
    else:
        stacked = jnp.stack([jnp.stack(term) for term in terms])
        stacked = stacked.reshape(PAIRS, 2, places, half, -1).transpose(0, 2, 1, 3, 4)
        weight_sums = reduce_terms(stacked, place, core, spot, special)
    weight_sums = weight_sums.reshape(PAIRS, own, -1).transpose(1, 0, 2).astype(f32)
    attend_total = jnp.concatenate(
        [
            weight_sums[:, :, :PAIR_QUERY].reshape(own, query_width),
            weight_sums[:, :, PAIR_QUERY : PAIR_QUERY + PAIR_KEY].reshape(own, key_width),
            weight_sums[:, :, PAIR_QUERY + PAIR_KEY : PAIR_WIDTH].reshape(own, key_width),
        ],
        axis=1,
    )
    output_total = weight_sums[:, :, PAIR_WIDTH:].reshape(own, query_width)

    normed_grad = join_columns(totals, places, base, core)
    attention_term = jnp.sum(normed_grad * scaled_in, axis=0)
    input_grad = (
        middle_grad + norm_back(scaled_in, inverse_in, normed_grad * attention_scale)
    ).astype(bf16)

    small_terms = jnp.concatenate([attention_term[None], feed_term[None], router_term.T], axis=0)
    count = (EXPERTS + 2) * own
    tiles = -(-count // (2 * PAIRS * 8 * LANES)) * 8
    small_terms = small_terms.reshape(EXPERTS + 2, places, own).transpose(1, 0, 2)
    small_terms = jnp.pad(
        small_terms.reshape(places, count), ((0, 0), (0, 2 * PAIRS * tiles * LANES - count))
    )
    small_terms = small_terms.reshape(places, PAIRS, 2, tiles, LANES).transpose(1, 0, 2, 3, 4)
    small_sums = reduce_terms(small_terms, place, core, spot, special)
    small_sums = small_sums.reshape(-1)[:count].reshape(EXPERTS + 2, own)

    combined_sum = total_of(combined_kept, combined_come)
    activations = (middle + combined_sum).astype(bf16)
    return (
        activations,
        input_grad,
        attend_total,
        output_total,
        small_sums[0],
        small_sums[1],
        small_sums[2:].T,
        expert_total,
    )


def solution(mesh):
    in_specs = (
        P(("rep", "shard"), None),
        P("shard", None),
        P("shard", None),
        P("shard"),
        P("shard"),
        P("shard", None),
        P("shard", None, None),
        P(("rep", "shard"), None),
        P(("rep", "shard"), None),
    )
    out_specs = (
        P(("rep", "shard"), None),
        P(("rep", "shard"), None),
        P("shard", None),
        P("shard", None),
        P("shard"),
        P("shard"),
        P("shard", None),
        P("shard", None, None),
    )
    run = functools.partial(body, places=mesh.shape["shard"], ranks=mesh.shape["rep"])
    return jax.shard_map(run, mesh=mesh, in_specs=in_specs, out_specs=out_specs, check_vma=False)
```

```python
import functools

import jax
import jax.numpy as jnp
from jax import lax
from jax.experimental import pallas as pl
from jax.experimental.pallas import tpu as pltpu
from jax.sharding import PartitionSpec as P

QUERY_HEADS = 24
KEY_VALUE_HEADS = 8
HEAD_WIDTH = 64
FF = 512
EXPERTS = 16

EPSILON = 1e-06
MASKED = -1e30

GROUP = QUERY_HEADS // KEY_VALUE_HEADS
PAIRS = KEY_VALUE_HEADS // 2
PAIR_QUERY = 2 * GROUP * HEAD_WIDTH
PAIR_KEY = 2 * HEAD_WIDTH
PAIR_WIDTH = PAIR_QUERY + 2 * PAIR_KEY
BLOCK = 256
LANES = 128
VMEM = 60 * 2**20


def cost(flops, moved):
    return pl.CostEstimate(flops=int(flops), bytes_accessed=int(moved), transcendentals=0)

bf16 = jnp.bfloat16
f32 = jnp.float32


def dot(left, right):
    return jnp.dot(left, right, preferred_element_type=f32)


def contract_rows(left, right):
    return lax.dot_general(left, right, (((0,), (0,)), ((), ())), preferred_element_type=f32)


def times_transposed(left, right):
    return lax.dot_general(left, right, (((1,), (1,)), ((), ())), preferred_element_type=f32)


def norm_rows(value_rows):
    inverse = lax.rsqrt(jnp.mean(value_rows * value_rows, axis=-1, keepdims=True) + EPSILON)
    return (value_rows * inverse, inverse)


def norm_back(scaled, inverse, upstream):
    return inverse * (upstream - scaled * jnp.mean(upstream * scaled, axis=-1, keepdims=True))


def rotary_tables(length, width):
    half = HEAD_WIDTH // 2
    frequency = 10000.0 ** (-2.0 * jnp.arange(half, dtype=f32) / HEAD_WIDTH)
    angles = jnp.arange(length, dtype=f32)[:, None] * frequency[None, :]
    cosine, sine = jnp.cos(angles), jnp.sin(angles)
    heads = width // HEAD_WIDTH
    return (
        jnp.tile(jnp.concatenate([cosine, cosine], axis=1), (1, heads)),
        jnp.tile(jnp.concatenate([-sine, sine], axis=1), (1, heads)),
    )


def rotate(values, cosine, sine):
    width = values.shape[1]
    half = HEAD_WIDTH // 2
    lane = lax.broadcasted_iota(jnp.int32, values.shape, 1)
    swapped = jnp.where(
        lane % HEAD_WIDTH < half,
        pltpu.roll(values, width - half, 1),
        pltpu.roll(values, half, 1),
    )
    return values * cosine + swapped * sine


def causal_block():
    shape = (BLOCK, BLOCK)
    return lax.broadcasted_iota(jnp.int32, shape, 0) <= lax.broadcasted_iota(jnp.int32, shape, 1)


def stack_rows(parts):
    return parts[0] if len(parts) == 1 else jnp.concatenate(parts, axis=0)


def natural(at_ref, own_ref, other_ref, held_ref):
    shards, half = own_ref.shape[1:3]
    for k in range(shards):
        for side, ref in enumerate((own_ref, other_ref)):
            start = (at_ref[0] ^ k) * (2 * half) + (at_ref[1] ^ side) * half
            held_ref[pl.ds(pl.multiple_of(start, half), half), :] = ref[0, k]


def attend_forward_kernel(
    at_ref, normed_ref, own_ref, other_ref, cosine_ref, sine_ref, mixed_ref, qkv_ref, lse_ref, weight_ref
):
    length = normed_ref.shape[0]
    natural(at_ref, own_ref, other_ref, weight_ref)
    keep = causal_block()
    projected = dot(normed_ref[...], weight_ref[...])
    rotated = rotate(projected[:, : PAIR_QUERY + PAIR_KEY], cosine_ref[...], sine_ref[...])
    query = (rotated[:, :PAIR_QUERY] * HEAD_WIDTH**-0.5).astype(bf16)
    key = rotated[:, PAIR_QUERY:].astype(bf16)
    value = projected[:, PAIR_QUERY + PAIR_KEY :].astype(bf16)
    qkv_ref[0, :, :PAIR_QUERY] = query
    qkv_ref[0, :, PAIR_QUERY : PAIR_QUERY + PAIR_KEY] = key
    qkv_ref[0, :, PAIR_QUERY + PAIR_KEY :] = value
    value_columns = value.T
    outs = []
    for head in range(2 * GROUP):
        kv = (head // GROUP) * HEAD_WIDTH
        columns = []
        for block in range(length // BLOCK):
            start, stop = block * BLOCK, (block + 1) * BLOCK
            scores = times_transposed(
                key[:stop, kv : kv + HEAD_WIDTH],
                query[start:stop, head * HEAD_WIDTH : (head + 1) * HEAD_WIDTH],
            )
            parts = [scores[:start]] if block else []
            scores = stack_rows(parts + [jnp.where(keep, scores[start:], MASKED)])
            top = jnp.max(scores, axis=0, keepdims=True)
            powers = jnp.exp(scores - top)
            total = jnp.sum(powers, axis=0, keepdims=True)
            probability = (powers * (1.0 / total)).astype(bf16)
            columns.append(dot(value_columns[kv : kv + HEAD_WIDTH, :stop], probability))
            lse_ref[0, head, start:stop] = (top + jnp.log(total))[0]
        outs.append(jnp.concatenate(columns, axis=1))
    mixed_ref[0] = jnp.concatenate(outs, axis=0).T.astype(bf16)


def whole(array):
    return pl.BlockSpec(array.shape, lambda *_: (0,) * array.ndim)


def entry(array, index=None):
    rest = (0,) * (array.ndim - 1)
    return pl.BlockSpec(
        (1,) + array.shape[1:], lambda p, at: ((p if index is None else index),) + rest
    )


def attend_forward(at, normed, weights, tables):
    length, features = normed.shape
    shapes = [
        jax.ShapeDtypeStruct((PAIRS, length, PAIR_QUERY), bf16),
        jax.ShapeDtypeStruct((PAIRS, length, PAIR_WIDTH), bf16),
        jax.ShapeDtypeStruct((PAIRS, 8, length), f32),
    ]
    return pl.pallas_call(
        attend_forward_kernel,
        grid_spec=pltpu.PrefetchScalarGridSpec(
            num_scalar_prefetch=1,
            grid=(PAIRS,),
            in_specs=[whole(normed)] + [entry(w) for w in weights] + [whole(t) for t in tables],
            out_specs=[entry(shape) for shape in shapes],
            scratch_shapes=[pltpu.VMEM((features, PAIR_WIDTH), bf16)],
        ),
        out_shape=shapes,
        compiler_params=pltpu.CompilerParams(vmem_limit_bytes=VMEM),
        cost_estimate=cost(2e10, 2e7),
    )(at, normed, *weights, *tables)


def middle_kernel(
    at_ref, mixed_ref, own_ref, other_ref, input_ref, gain_ref, middle_ref, fed_ref, weight_ref
):
    step = pl.program_id(0)
    natural(at_ref, own_ref, other_ref, weight_ref)
    added = times_transposed(mixed_ref[0], weight_ref[...])

    @pl.when(step == 0)
    def _():
        middle_ref[...] = input_ref[...].astype(f32) + added

    @pl.when(step > 0)
    def _():
        middle_ref[...] += added

    @pl.when(step == pl.num_programs(0) - 1)
    def _():
        fed_ref[...] = (norm_rows(middle_ref[...])[0] * gain_ref[...]).astype(bf16)


def middle_rows(at, mixed, weights, inputs, gain):
    length, features = inputs.shape
    shapes = [jax.ShapeDtypeStruct((length, features), kind) for kind in (f32, bf16)]
    return pl.pallas_call(
        middle_kernel,
        grid_spec=pltpu.PrefetchScalarGridSpec(
            num_scalar_prefetch=1,
            grid=(PAIRS,),
            in_specs=[entry(mixed)] + [entry(w) for w in weights] + [whole(inputs), whole(gain)],
            out_specs=[whole(shape) for shape in shapes],
            scratch_shapes=[pltpu.VMEM((features, PAIR_QUERY), bf16)],
        ),
        out_shape=shapes,
        compiler_params=pltpu.CompilerParams(vmem_limit_bytes=VMEM),
        cost_estimate=cost(2.4e9, 1e7),
    )(at, mixed, *weights, inputs, gain)


def attend_backward_kernel(
    at_ref,
    branch_ref,
    own_output_ref,
    other_output_ref,
    mixed_ref,
    qkv_ref,
    lse_ref,
    normed_ref,
    own_weight_ref,
    other_weight_ref,
    cosine_ref,
    sine_ref,
    total_ref,
    own_term_ref,
    other_term_ref,
    grad_ref,
    output_ref,
    weight_ref,
    term_ref,
):
    length = branch_ref.shape[0]
    natural(at_ref, own_output_ref, other_output_ref, output_ref)
    natural(at_ref, own_weight_ref, other_weight_ref, weight_ref)
    keep = causal_block()
    blocks = length // BLOCK
    mixed_grad = dot(branch_ref[...], output_ref[...]).astype(bf16)
    query = qkv_ref[0, :, :PAIR_QUERY]
    key = qkv_ref[0, :, PAIR_QUERY : PAIR_QUERY + PAIR_KEY]
    value = qkv_ref[0, :, PAIR_QUERY + PAIR_KEY :]
    scaled_key = (key.astype(f32) * HEAD_WIDTH**-0.5).T.astype(bf16)
    query_grads, key_grads, value_grads = [], [], []
    for side in range(2):
        kv = side * HEAD_WIDTH
        key_part = key[:, kv : kv + HEAD_WIDTH]
        value_part = value[:, kv : kv + HEAD_WIDTH]
        key_grad, value_grad = [None] * blocks, [None] * blocks
        for head in range(side * GROUP, (side + 1) * GROUP):
            column = head * HEAD_WIDTH
            columns = []
            for block in range(blocks):
                start, stop = block * BLOCK, (block + 1) * BLOCK
                query_rows = query[start:stop, column : column + HEAD_WIDTH]
                upstream = mixed_grad[start:stop, column : column + HEAD_WIDTH]
                scores = times_transposed(key_part[:stop], query_rows)
                prob_grad = times_transposed(value_part[:stop], upstream)
                probability = jnp.exp(scores - lse_ref[0, head, start:stop][None, :])
                parts = [probability[:start]] if block else []
                probability = stack_rows(parts + [jnp.where(keep, probability[start:], 0.0)])
                shift = jnp.sum(probability * prob_grad, axis=0, keepdims=True)
                score_grad = (probability * (prob_grad - shift)).astype(bf16)
                value_add = dot(probability.astype(bf16), upstream)
                key_add = dot(score_grad, query_rows)
                for j in range(block + 1):
                    rows = slice(j * BLOCK, (j + 1) * BLOCK)
                    value_grad[j] = (
                        value_add[rows] if value_grad[j] is None else value_grad[j] + value_add[rows]
                    )
                    key_grad[j] = (
                        key_add[rows] if key_grad[j] is None else key_grad[j] + key_add[rows]
                    )
                columns.append(dot(scaled_key[kv : kv + HEAD_WIDTH, :stop], score_grad))
            query_grads.append(jnp.concatenate(columns, axis=1))
        key_grads.append(stack_rows(key_grad))
        value_grads.append(stack_rows(value_grad))
    turned = rotate(
        jnp.concatenate([jnp.concatenate(query_grads, axis=0).T] + key_grads, axis=1),
        cosine_ref[...],
        -sine_ref[...],
    )
    projected_grad = jnp.concatenate([turned] + value_grads, axis=1).astype(bf16)
    term_ref[:, :PAIR_WIDTH] = contract_rows(normed_ref[...], projected_grad).astype(bf16)
    term_ref[:, PAIR_WIDTH:] = contract_rows(branch_ref[...], mixed_ref[0]).astype(bf16)
    shards, half = own_weight_ref.shape[1:3]
    for k in range(shards):
        for side, ref in enumerate((own_term_ref, other_term_ref)):
            start = (at_ref[0] ^ k) * (2 * half) + (at_ref[1] ^ side) * half
            ref[k] = term_ref[pl.ds(pl.multiple_of(start, half), half), :]
    grad_ref[...] = total_ref[...] + times_transposed(projected_grad, weight_ref[...])


def attend_backward(at, m, branch_grad, output, saved, normed, weights, tables, total):
    length, features = branch_grad.shape
    shards, half = weights[0].shape[1:3]
    width = PAIR_WIDTH + PAIR_QUERY
    term = jax.ShapeDtypeStruct((shards, half, width), bf16)
    shapes = [term, term, jax.ShapeDtypeStruct((length, features), f32)]
    ones = [*output, *saved]
    operands = [branch_grad, *ones, normed, *weights, *tables, total]
    specs = [whole(branch_grad)] + [entry(one, m) for one in ones] + [whole(normed)]
    specs += [entry(w, m) for w in weights] + [whole(t) for t in tables] + [whole(total)]
    return pl.pallas_call(
        attend_backward_kernel,
        grid_spec=pltpu.PrefetchScalarGridSpec(
            num_scalar_prefetch=1,
            grid=(1,),
            in_specs=specs,
            out_specs=[whole(shape) for shape in shapes],
            scratch_shapes=[
                pltpu.VMEM((features, PAIR_QUERY), bf16),
                pltpu.VMEM((features, PAIR_WIDTH), bf16),
                pltpu.VMEM((features, width), bf16),
            ],
        ),
        out_shape=shapes,
        input_output_aliases={len(operands): 2},
        compiler_params=pltpu.CompilerParams(vmem_limit_bytes=VMEM),
        cost_estimate=cost(9e9, 1.5e7),
    )(at, *operands)


def expert_kernel(
    first_ref,
    inner_ref,
    outer_ref,
    upstream_ref,
    chosen_ref,
    router_ref,
    weight_ref,
    _,
    fed_ref,
    row_ref,
    combined_ref,
    pair_ref,
    gated_ref,
    gates_ref,
    gate_grad_ref,
    row_total,
    combined_total,
):
    step, steps = pl.program_id(0), pl.num_programs(0)
    index = first_ref[0] + step
    lane = lax.broadcasted_iota(jnp.int32, gates_ref.shape, 1)

    @pl.when(step == 0)
    def _():
        @pl.when(first_ref[3] > 0)
        def _():
            fed_ref[...] = inner_ref[...]

        @pl.when(first_ref[3] == 0)
        def _():
            fed_ref[...] = outer_ref[...]

        logits = dot(fed_ref[...], router_ref[...])
        chosen = chosen_ref[0] > 0.0
        logits = jnp.where(chosen, logits, MASKED)
        powers = jnp.where(chosen, jnp.exp(logits - jnp.max(logits, axis=1, keepdims=True)), 0.0)
        gates_ref[...] = powers / jnp.sum(powers, axis=1, keepdims=True)
        gate_grad_ref[...] = jnp.zeros_like(gate_grad_ref)

    gate = jnp.sum(jnp.where(lane == index, gates_ref[...], 0.0), axis=1, keepdims=True)
    gate_grad = None
    width = FF // 2
    for start in range(0, FF, width):
        stop = start + width
        gate_part = dot(fed_ref[...], weight_ref[0, :, start:stop])
        up_part = dot(fed_ref[...], weight_ref[0, :, FF + start : FF + stop])
        raw_grad = dot(upstream_ref[0], weight_ref[0, :, 2 * FF + start : 2 * FF + stop])
        sigma = jax.nn.sigmoid(gate_part)
        activated = gate_part * sigma
        hidden = activated * up_part
        part = jnp.sum(hidden * raw_grad, axis=1, keepdims=True)
        gate_grad = part if gate_grad is None else gate_grad + part
        hidden_grad = gate * raw_grad
        slope = sigma * (1.0 + gate_part * (1.0 - sigma))
        pair_ref[0, :, start:stop] = (hidden_grad * up_part * slope).astype(bf16)
        pair_ref[0, :, FF + start : FF + stop] = (hidden_grad * activated).astype(bf16)
        gated_ref[0, :, start:stop] = (gate * hidden).astype(bf16)
    gate_grad_ref[...] += jnp.where(lane == index, gate_grad, 0.0)
    combined = times_transposed(gated_ref[0], weight_ref[0, :, 2 * FF :])
    row = times_transposed(pair_ref[0], weight_ref[0, :, : 2 * FF])

    @pl.when(step == 0)
    def _():
        combined_total[...] = combined
        row_total[...] = row

    @pl.when(step > 0)
    def _():
        combined_total[...] += combined
        row_total[...] += row

    @pl.when(step == steps - 1)
    def _():
        features = row_total.shape[1]
        row_ref[:, :features] = row_total[...].astype(bf16)
        high = gate_grad_ref[...].astype(bf16)
        low = gate_grad_ref[...] - high.astype(f32)
        row_ref[:, features:] = (high.astype(f32) + pltpu.roll(low, LANES // 2, 1)).astype(bf16)
        combined_ref[0] = combined_total[...].astype(bf16)


def expert_slot(at, choices, upstream, chosen, router, weights, combined):
    length, features = choices[0].shape
    count = weights.shape[0]
    full = lambda *shape: pl.BlockSpec(shape, lambda e, at: (0,) * len(shape))
    each = lambda *shape: pl.BlockSpec((1,) + shape, lambda e, at: (e,) + (0,) * len(shape))
    there = lambda i, *shape: pl.BlockSpec(
        (1,) + shape, lambda e, at: (at[i],) + (0,) * len(shape)
    )
    return pl.pallas_call(
        expert_kernel,
        grid_spec=pltpu.PrefetchScalarGridSpec(
            num_scalar_prefetch=1,
            grid=(count,),
            in_specs=[
                full(length, features),
                full(length, features),
                there(1, length, features),
                there(2, length, LANES),
                full(features, LANES),
                each(features, 3 * FF),
                pl.BlockSpec(memory_space=pl.ANY),
            ],
            out_specs=[
                full(length, features),
                full(length, features + LANES),
                there(2, length, features),
                each(length, 2 * FF),
                each(length, FF),
            ],
            scratch_shapes=[
                pltpu.VMEM((length, LANES), f32),
                pltpu.VMEM((length, LANES), f32),
                pltpu.VMEM((length, features), f32),
                pltpu.VMEM((length, features), f32),
            ],
        ),
        out_shape=[
            jax.ShapeDtypeStruct((length, features), bf16),
            jax.ShapeDtypeStruct((length, features + LANES), bf16),
            jax.ShapeDtypeStruct(combined.shape, bf16),
            jax.ShapeDtypeStruct((count, length, 2 * FF), bf16),
            jax.ShapeDtypeStruct((count, length, FF), bf16),
        ],
        input_output_aliases={7: 2},
        compiler_params=pltpu.CompilerParams(vmem_limit_bytes=VMEM),
        cost_estimate=cost(12 * count * length * features * FF, 3.2e7),
    )(at, *choices, upstream, chosen, router, weights, combined)


def fed_grad_kernel(*refs):
    arrived = refs[:-10]
    (
        fed_ref,
        middle_ref,
        upstream_ref,
        chosen_ref,
        router_ref,
        gain_ref,
        middle_grad_ref,
        branch_ref,
        router_grad_ref,
        gain_grad_ref,
    ) = refs[-10:]
    step = pl.program_id(0)
    total = arrived[0][...].astype(f32)
    for ref in arrived[1:]:
        total = total + ref[...].astype(f32)
    features = fed_ref.shape[1]
    parts = total[:, features:]
    gate_grad = parts + pltpu.roll(parts, LANES // 2, 1)
    chosen = chosen_ref[...] > 0.0
    logits = jnp.where(chosen, dot(fed_ref[...], router_ref[...]), MASKED)
    powers = jnp.where(chosen, jnp.exp(logits - jnp.max(logits, axis=1, keepdims=True)), 0.0)
    gates = powers / jnp.sum(powers, axis=1, keepdims=True)
    gate_grad = jnp.where(chosen, gate_grad, 0.0)
    mean = jnp.sum(gates * gate_grad, axis=1, keepdims=True)
    logit_grad = (gates * (gate_grad - mean)).astype(bf16)
    fed_grad = times_transposed(logit_grad, router_ref[...]) + total[:, :features]
    scaled, inverse = norm_rows(middle_ref[...])
    back = norm_back(scaled, inverse, fed_grad * gain_ref[...])
    middle_grad = upstream_ref[...].astype(f32) + back
    middle_grad_ref[...] = middle_grad
    branch_ref[...] = middle_grad.astype(bf16)
    router_grad = contract_rows(logit_grad, fed_ref[...])
    gain_grad = jnp.sum(fed_grad * scaled, axis=0, keepdims=True)

    @pl.when(step == 0)
    def _():
        router_grad_ref[...] = router_grad
        gain_grad_ref[...] = gain_grad

    @pl.when(step > 0)
    def _():
        router_grad_ref[...] += router_grad
        gain_grad_ref[...] += gain_grad


def fed_grads(arrived, fed, middle, upstream, chosen, router, gain):
    length, features = fed.shape
    rows = length // 4
    split = lambda array: pl.BlockSpec((rows, array.shape[1]), lambda i: (i, 0))
    shapes = [
        jax.ShapeDtypeStruct((length, features), f32),
        jax.ShapeDtypeStruct((length, features), bf16),
        jax.ShapeDtypeStruct((LANES, features), f32),
        jax.ShapeDtypeStruct((1, features), f32),
    ]
    operands = [*arrived, fed, middle, upstream, chosen, router, gain]
    return pl.pallas_call(
        fed_grad_kernel,
        grid=(4,),
        in_specs=[split(a) for a in operands[:-2]] + [whole(router), whole(gain)],
        out_specs=[split(shapes[0]), split(shapes[1]), whole(shapes[2]), whole(shapes[3])],
        out_shape=shapes,
        compiler_params=pltpu.CompilerParams(vmem_limit_bytes=VMEM),
        cost_estimate=cost(1e8, 2e7),
    )(*operands)


def expert_grad_kernel(places_ref, *refs):
    slots = (len(refs) - 1) // 4
    fed, upstream, pair, gated = (refs[i * slots : (i + 1) * slots] for i in range(4))
    out_ref = refs[-1]
    inner = outer = None
    for k in range(slots):
        add_inner = contract_rows(fed[k][...], pair[k][0])
        add_outer = contract_rows(upstream[k][0], gated[k][0])
        inner = add_inner if inner is None else inner + add_inner
        outer = add_outer if outer is None else outer + add_outer
    out_ref[0, :, : 2 * FF] = inner.astype(out_ref.dtype)
    out_ref[0, :, 2 * FF :] = outer.astype(out_ref.dtype)


def expert_grads(places, fed, upstream, pairs, gated):
    length, features = fed[0].shape
    slots, count = len(pairs), pairs[0].shape[0]
    rows = features // 2
    column = pl.BlockSpec((length, rows), lambda e, i, at: (0, i))
    there = lambda k: pl.BlockSpec((1, length, rows), lambda e, i, at: (at[k], 0, i))
    each = lambda width: pl.BlockSpec((1, length, width), lambda e, i, at: (e, 0, 0))
    return pl.pallas_call(
        expert_grad_kernel,
        grid_spec=pltpu.PrefetchScalarGridSpec(
            num_scalar_prefetch=1,
            grid=(count, features // rows),
            in_specs=[column] * slots
            + [there(k) for k in range(slots)]
            + [each(2 * FF)] * slots
            + [each(FF)] * slots,
            out_specs=pl.BlockSpec((1, rows, 3 * FF), lambda e, i, at: (e, i, 0)),
        ),
        out_shape=jax.ShapeDtypeStruct((count, features, 3 * FF), bf16),
        compiler_params=pltpu.CompilerParams(vmem_limit_bytes=VMEM),
        cost_estimate=cost(6 * slots * count * length * features * FF, 8e7),
    )(places, *fed, *[upstream] * slots, *pairs, *gated)


def exchange(value, k):
    return lax.ppermute(value, "shard", [(i, i ^ k) for i in range(4)])


def inside(place):
    return (place == 1) | (place == 2)


def sources(place, count):
    if count != 4:
        return [place ^ k for k in range(count)]
    middle = inside(place)
    order = ((1, 3), (2, 1), (3, 2))
    return [place] + [place ^ jnp.where(middle, mid, out) for out, mid in order]


def after(value, *earlier):
    return lax.optimization_barrier((value, earlier))[0]


def line_gather(rows, place, count):
    if count != 4:
        everything = lax.all_gather(rows, "shard", axis=0)
        for source in sources(place, count):
            yield (pick(everything, source),) * 2
            yield
        return
    middle = inside(place)
    near = exchange(rows, 1)
    across = lax.ppermute(rows, "shard", [(1, 2), (2, 1)])
    made = yield rows, rows
    yield
    near_on, across_on = after((near, across), made)
    second_inside = lax.ppermute(near_on, "shard", [(1, 2), (2, 1)])
    second_outside = lax.ppermute(across_on, "shard", [(1, 0), (2, 3)])
    yield across, near
    yield
    third_outside = lax.ppermute(second_inside, "shard", [(1, 0), (2, 3)])
    yield near, second_outside
    yield
    yield second_inside, third_outside
    yield


def scatter_all(parts, place, count):
    stacked = jnp.stack(parts)
    ordered = jnp.stack([pick(stacked, place ^ d) for d in range(count)])
    return lax.psum_scatter(ordered, "shard", scatter_dimension=0, tiled=False)


def line_send(part, k):
    ways = {
        1: ([(0, 1), (3, 2)], [(1, 2), (2, 1)]),
        2: ([(0, 2), (3, 1)], [(1, 0), (2, 3)]),
        3: ([(0, 3), (3, 0)], [(1, 3), (2, 0)]),
    }
    return [lax.ppermute(part, "shard", way) for way in ways[k]]


def total_of(kept, arrived):
    total = kept.astype(f32)
    for part in arrived:
        total = total + part.astype(f32)
    return total


def hop(value, bit):
    return lax.ppermute(value, "rep", [(i, i ^ bit) for i in range(8)])


def pick(stacked, index, axis=0):
    return lax.dynamic_index_in_dim(stacked, index, axis, False)


def gather_near(mine):
    return jnp.stack([exchange(mine, k) for k in range(1, 4)])


def send_pairs(near):
    return [hop(near, 2 * m) for m in range(1, 4)]


def join_pairs(local, parts, core, spot):
    own = jnp.stack(
        [
            jnp.concatenate([local(spot ^ m, core)[None], part])
            for m, part in enumerate(parts)
        ]
    )
    return own, hop(own, 1)


def join_chip(term, special):
    kept, given = term
    return (kept.astype(f32) + hop(given, 1).astype(f32)).astype(bf16) if special else kept


def place_kernel(at_ref, own_ref, other_ref, attend_ref, output_ref):
    half = own_ref.shape[1]
    query, key = QUERY_HEADS * HEAD_WIDTH, KEY_VALUE_HEADS * HEAD_WIDTH
    for m in range(PAIRS):
        pair = at_ref[0] ^ m
        for side, ref in enumerate((own_ref, other_ref)):
            rows = pl.ds(pl.multiple_of((at_ref[1] ^ side) * half, half), half)
            start = 0
            for out_ref, base, width in (
                (attend_ref, 0, PAIR_QUERY),
                (attend_ref, query, PAIR_KEY),
                (attend_ref, query + key, PAIR_KEY),
                (output_ref, 0, PAIR_QUERY),
            ):
                columns = pl.ds(pl.multiple_of(base + pair * width, LANES), width)
                out_ref[rows, columns] = ref[m, :, start : start + width].astype(f32)
                start += width


def finish_pairs(plane, core, spot):
    piece = plane[0].astype(f32)
    for k in range(1, 4):
        piece = piece + exchange(plane[k], k).astype(f32)
    piece = piece.astype(plane.dtype)
    mine = jnp.stack([piece] + [hop(piece, 2 * m) for m in range(1, 4)])
    other = hop(mine, 1)
    rows = 2 * piece.shape[0]
    return pl.pallas_call(
        place_kernel,
        grid_spec=pltpu.PrefetchScalarGridSpec(
            num_scalar_prefetch=1,
            grid=(1,),
            in_specs=[whole(mine), whole(other)],
            out_specs=[
                pl.BlockSpec((rows, PAIRS * PAIR_WIDTH), lambda i, at: (0, 0)),
                pl.BlockSpec((rows, PAIRS * PAIR_QUERY), lambda i, at: (0, 0)),
            ],
        ),
        out_shape=[
            jax.ShapeDtypeStruct((rows, PAIRS * PAIR_WIDTH), f32),
            jax.ShapeDtypeStruct((rows, PAIRS * PAIR_QUERY), f32),
        ],
        compiler_params=pltpu.CompilerParams(vmem_limit_bytes=VMEM),
        cost_estimate=cost(1e6, 1e7),
    )(jnp.stack([spot, core]).astype(jnp.int32), mine, other)


def reduce_terms(terms):
    part = lax.psum_scatter(terms, "shard", scatter_dimension=1, tiled=False)
    return lax.psum(part, "rep")


def body(
    inputs,
    query_key_value_weight,
    output_weight,
    attention_gain,
    feed_gain,
    router_weight,
    expert_weight,
    routes,
    cotangent,
    *,
    places,
    ranks,
):
    length, features = inputs.shape
    own = query_key_value_weight.shape[0]
    local = expert_weight.shape[0]
    query_width = QUERY_HEADS * HEAD_WIDTH
    key_width = KEY_VALUE_HEADS * HEAD_WIDTH
    place, rank = lax.axis_index("shard"), lax.axis_index("rep")

    special = places == 4 and ranks == 8
    half = own // 2
    base, core, spot = (place, rank % 2, rank // 2) if special else (0, 0, 0)

    projection = query_key_value_weight

    def projection_share(pair, side):
        rows = lax.dynamic_slice_in_dim(projection, side * half, half, 0)
        return jnp.concatenate(
            [
                lax.dynamic_slice_in_dim(rows, pair * PAIR_QUERY, PAIR_QUERY, 1),
                lax.dynamic_slice_in_dim(rows, query_width + pair * PAIR_KEY, PAIR_KEY, 1),
                lax.dynamic_slice_in_dim(
                    rows, query_width + key_width + pair * PAIR_KEY, PAIR_KEY, 1
                ),
            ],
            axis=1,
        )

    def output_share(pair, side):
        return lax.dynamic_slice(
            output_weight, (side * half, pair * PAIR_QUERY), (half, PAIR_QUERY)
        )

    chosen_own = jnp.sum(
        (routes[:, :, None] == jnp.arange(EXPERTS, dtype=jnp.int32)).astype(f32), axis=1
    )
    small = jnp.concatenate(
        [
            attention_gain.reshape(-1),
            feed_gain.reshape(-1),
            router_weight.reshape(-1),
            chosen_own.astype(bf16).reshape(-1),
        ]
    )
    if special:
        extra = -(-small.size // (16 * PAIR_WIDTH)) * 16
        below = jnp.pad(small, (0, extra * PAIR_WIDTH - small.size)).reshape(extra, PAIR_WIDTH)
        near = gather_near(jnp.concatenate([projection_share(spot, core), below]))
        projection_near = near[:, :half]
        small_slots = jnp.concatenate(
            [small[None], near[:, half:].reshape(3, -1)[:, : small.size]]
        )
        small_all = jnp.stack([pick(small_slots, place ^ k) for k in range(4)])
        projection_sent = send_pairs(projection_near)
        output_near = gather_near(after(output_share(spot, core), near))
        output_sent = send_pairs(after(output_near, projection_sent))
        attend_weights = join_pairs(
            projection_share, [projection_near] + projection_sent, core, spot
        )
        output_weights = join_pairs(output_share, [output_near] + output_sent, core, spot)
        cotangent_sent = after(cotangent, near)
    else:
        gathered = lax.all_gather(projection, "shard", axis=0)
        gathered_output = lax.all_gather(output_weight, "shard", axis=0)
        columns = jnp.concatenate(
            [
                gathered[:, :, :query_width].reshape(places, own, PAIRS, PAIR_QUERY),
                gathered[:, :, query_width : query_width + key_width].reshape(
                    places, own, PAIRS, PAIR_KEY
                ),
                gathered[:, :, query_width + key_width :].reshape(places, own, PAIRS, PAIR_KEY),
            ],
            axis=3,
        ).transpose(2, 0, 1, 3)
        attend_weights = (columns[:, :, :half], columns[:, :, half:])
        columns = gathered_output.reshape(places, own, PAIRS, PAIR_QUERY).transpose(2, 0, 1, 3)
        output_weights = (columns[:, :, :half], columns[:, :, half:])
        small_all = lax.all_gather(small, "shard", axis=0)
        cotangent_sent = cotangent

    upstream_all = lax.all_gather(cotangent_sent, "shard", axis=0)

    tables = rotary_tables(length, PAIR_QUERY + PAIR_KEY)
    residual = inputs.astype(f32)
    scaled_in, inverse_in = norm_rows(residual)
    attention_scale = small_all[:, :own].reshape(features).astype(f32)
    feed_scale = small_all[:, own : 2 * own].reshape(features).astype(f32)
    router_full = small_all[:, 2 * own : (2 + EXPERTS) * own].reshape(features, EXPERTS)
    chosen_all = small_all[:, (2 + EXPERTS) * own :].reshape(places, length, EXPERTS).astype(f32)
    normed = (scaled_in * attention_scale).astype(bf16)
    where = jnp.stack([base, core]).astype(jnp.int32)
    mixed, qkv, lse = attend_forward(where, normed, attend_weights, tables)
    middle, fed = middle_rows(where, mixed, output_weights, inputs, feed_scale[None])
    router_wide = jnp.pad(router_full, ((0, 0), (0, LANES - EXPERTS)))
    chosen_wide = jnp.pad(chosen_all, ((0, 0), (0, 0), (0, LANES - EXPERTS)))
    rows, pair_grads, gated = [], [], []
    combined = jnp.zeros((places, length, features), bf16)
    order = sources(place, places)
    middle_place = inside(place).astype(jnp.int32)
    fed_slots, rows_come, arriving = [], [], line_gather(fed, place, places)
    for k, source in enumerate(order):
        index = jnp.zeros_like(source) if k == 0 else source
        at = jnp.stack([place * local, index, source, middle_place]).astype(jnp.int32)
        rows_up = cotangent[None] if k == 0 else upstream_all
        fed_k, row, combined, *kept = expert_slot(
            at, next(arriving), rows_up, chosen_wide, router_wide, expert_weight, combined
        )
        for held, value in zip((fed_slots, rows, pair_grads, gated), (fed_k, row, *kept)):
            held.append(value)
        arriving.send((row, upstream_all))
        if special and k:
            rows_come += line_send(row, k)
    expert_term = expert_grads(
        jnp.stack(order).astype(jnp.int32),
        fed_slots,
        upstream_all,
        pair_grads,
        gated,
    )
    expert_total = lax.psum(expert_term, "rep").astype(f32)

    if special:
        arrived = [rows[0], *rows_come]
    else:
        arrived = [scatter_all(rows, place, places)]
    arrived = after(arrived, expert_term)

    combined = lax.all_to_all(after(combined, arrived), "shard", 0, 0)

    def rest():
        chosen = jnp.pad(chosen_own, ((0, 0), (0, LANES - EXPERTS)))
        middle_grad, branch_grad, router_term, feed_term = fed_grads(
            arrived, fed, middle, cotangent, chosen, router_wide, feed_scale[None]
        )
        normed_grad = jnp.zeros((length, features), f32)
        terms, chips = [None] * PAIRS, [None] * PAIRS
        steps = (3, 1, 2, 0)
        for i, m in enumerate(steps):
            ready = [chips[steps[i - 2]]] if i >= 2 else []
            own_term, other_term, normed_grad = attend_backward(
                where,
                m,
                after(branch_grad, *ready),
                output_weights,
                (mixed, qkv, lse),
                normed,
                attend_weights,
                tables,
                normed_grad,
            )
            terms[m] = (own_term, other_term)
            if i >= 1:
                chips[steps[i - 1]] = join_chip(terms[steps[i - 1]], special)
        if special:
            chips[0] = join_chip(terms[0], special)
            plane = chips[0].astype(f32)
            for m in (3, 1, 2):
                plane = plane + hop(chips[m], 2 * m).astype(f32)
            attend_total, output_total = finish_pairs(plane.astype(bf16), core, spot)
        else:
            stacked = jnp.stack([jnp.stack(term) for term in terms])
            weight_sums = reduce_terms(stacked.transpose(0, 2, 1, 3, 4))
            weight_sums = weight_sums.reshape(PAIRS, own, -1).transpose(1, 0, 2).astype(f32)
            attend_total = jnp.concatenate(
                [
                    weight_sums[:, :, :PAIR_QUERY].reshape(own, query_width),
                    weight_sums[:, :, PAIR_QUERY : PAIR_QUERY + PAIR_KEY].reshape(own, key_width),
                    weight_sums[:, :, PAIR_QUERY + PAIR_KEY : PAIR_WIDTH].reshape(own, key_width),
                ],
                axis=1,
            )
            output_total = weight_sums[:, :, PAIR_WIDTH:].reshape(own, query_width)

        attention_term = jnp.sum(normed_grad * scaled_in, axis=0)
        input_grad = (
            middle_grad + norm_back(scaled_in, inverse_in, normed_grad * attention_scale)
        ).astype(bf16)

        small_terms = jnp.concatenate(
            [attention_term[None], feed_term, router_term[:EXPERTS]], axis=0
        )
        if special:
            for axis, bit in (("rep", 1), ("rep", 2), ("rep", 4), ("shard", 1), ("shard", 2)):
                size = 8 if axis == "rep" else 4
                pairs = [(i, i ^ bit) for i in range(size)]
                small_terms = small_terms + lax.ppermute(small_terms, axis, pairs)
        else:
            small_terms = lax.psum(small_terms, ("rep", "shard"))
        small_sums = lax.dynamic_slice_in_dim(small_terms, place * own, own, 1)
        return (
            input_grad,
            attend_total,
            output_total,
            small_sums[0],
            small_sums[1],
            small_sums[2:].T,
        )

    shapes = (
        ((length, features), bf16),
        (query_key_value_weight.shape, f32),
        (output_weight.shape, f32),
        ((own,), f32),
        ((own,), f32),
        ((own, EXPERTS), f32),
    )
    empty = lambda: tuple(jnp.zeros(*shape) for shape in shapes)
    grads = lax.cond(routes[0, 0] >= 0, rest, empty)
    activations = (middle + jnp.sum(combined.astype(f32), axis=0)).astype(bf16)
    return (activations, *grads, expert_total)


def solution(mesh):
    in_specs = (
        P(("rep", "shard"), None),
        P("shard", None),
        P("shard", None),
        P("shard"),
        P("shard"),
        P("shard", None),
        P("shard", None, None),
        P(("rep", "shard"), None),
        P(("rep", "shard"), None),
    )
    out_specs = (
        P(("rep", "shard"), None),
        P(("rep", "shard"), None),
        P("shard", None),
        P("shard", None),
        P("shard"),
        P("shard"),
        P("shard", None),
        P("shard", None, None),
    )
    run = functools.partial(body, places=mesh.shape["shard"], ranks=mesh.shape["rep"])
    return jax.shard_map(run, mesh=mesh, in_specs=in_specs, out_specs=out_specs, check_vma=False)
```

```python
import functools

import jax
import jax.numpy as jnp
from jax import lax
from jax.experimental import pallas as pl
from jax.experimental.pallas import tpu as pltpu
from jax.sharding import PartitionSpec as P

QUERY_HEADS = 24
KEY_VALUE_HEADS = 8
HEAD_WIDTH = 64
FF = 512
EXPERTS = 16

EPSILON = 1e-06
MASKED = -1e30

GROUP = QUERY_HEADS // KEY_VALUE_HEADS
PAIRS = KEY_VALUE_HEADS // 2
PAIR_QUERY = 2 * GROUP * HEAD_WIDTH
PAIR_KEY = 2 * HEAD_WIDTH
PAIR_WIDTH = PAIR_QUERY + 2 * PAIR_KEY
BLOCK = 256
LANES = 128
VMEM = 60 * 2**20


def cost(flops, moved):
    return pl.CostEstimate(flops=int(flops), bytes_accessed=int(moved), transcendentals=0)

bf16 = jnp.bfloat16
f32 = jnp.float32


def dot(left, right):
    return jnp.dot(left, right, preferred_element_type=f32)


def contract_rows(left, right):
    return lax.dot_general(left, right, (((0,), (0,)), ((), ())), preferred_element_type=f32)


def times_transposed(left, right):
    return lax.dot_general(left, right, (((1,), (1,)), ((), ())), preferred_element_type=f32)


def norm_rows(value_rows):
    inverse = lax.rsqrt(jnp.mean(value_rows * value_rows, axis=-1, keepdims=True) + EPSILON)
    return (value_rows * inverse, inverse)


def norm_back(scaled, inverse, upstream):
    return inverse * (upstream - scaled * jnp.mean(upstream * scaled, axis=-1, keepdims=True))


def rotary_tables(length, width):
    half = HEAD_WIDTH // 2
    frequency = 10000.0 ** (-2.0 * jnp.arange(half, dtype=f32) / HEAD_WIDTH)
    angles = jnp.arange(length, dtype=f32)[:, None] * frequency[None, :]
    cosine, sine = jnp.cos(angles), jnp.sin(angles)
    heads = width // HEAD_WIDTH
    return (
        jnp.tile(jnp.concatenate([cosine, cosine], axis=1), (1, heads)),
        jnp.tile(jnp.concatenate([-sine, sine], axis=1), (1, heads)),
    )


def rotate(values, cosine, sine):
    width = values.shape[1]
    half = HEAD_WIDTH // 2
    lane = lax.broadcasted_iota(jnp.int32, values.shape, 1)
    swapped = jnp.where(
        lane % HEAD_WIDTH < half,
        pltpu.roll(values, width - half, 1),
        pltpu.roll(values, half, 1),
    )
    return values * cosine + swapped * sine


def causal_block():
    shape = (BLOCK, BLOCK)
    return lax.broadcasted_iota(jnp.int32, shape, 0) <= lax.broadcasted_iota(jnp.int32, shape, 1)


def stack_rows(parts):
    return parts[0] if len(parts) == 1 else jnp.concatenate(parts, axis=0)


def natural(at_ref, own_ref, other_ref, held_ref):
    shards, half = own_ref.shape[1:3]
    for k in range(shards):
        for side, ref in enumerate((own_ref, other_ref)):
            start = (at_ref[0] ^ k) * (2 * half) + (at_ref[1] ^ side) * half
            held_ref[pl.ds(pl.multiple_of(start, half), half), :] = ref[0, k]


def attend_forward_kernel(
    at_ref, normed_ref, own_ref, other_ref, cosine_ref, sine_ref, mixed_ref, qkv_ref, lse_ref, weight_ref
):
    length = normed_ref.shape[0]
    natural(at_ref, own_ref, other_ref, weight_ref)
    keep = causal_block()
    projected = dot(normed_ref[...], weight_ref[...])
    rotated = rotate(projected[:, : PAIR_QUERY + PAIR_KEY], cosine_ref[...], sine_ref[...])
    query = (rotated[:, :PAIR_QUERY] * HEAD_WIDTH**-0.5).astype(bf16)
    key = rotated[:, PAIR_QUERY:].astype(bf16)
    value = projected[:, PAIR_QUERY + PAIR_KEY :].astype(bf16)
    qkv_ref[0, :, :PAIR_QUERY] = query
    qkv_ref[0, :, PAIR_QUERY : PAIR_QUERY + PAIR_KEY] = key
    qkv_ref[0, :, PAIR_QUERY + PAIR_KEY :] = value
    value_columns = value.T
    outs = []
    for head in range(2 * GROUP):
        kv = (head // GROUP) * HEAD_WIDTH
        columns = []
        for block in range(length // BLOCK):
            start, stop = block * BLOCK, (block + 1) * BLOCK
            scores = times_transposed(
                key[:stop, kv : kv + HEAD_WIDTH],
                query[start:stop, head * HEAD_WIDTH : (head + 1) * HEAD_WIDTH],
            )
            parts = [scores[:start]] if block else []
            scores = stack_rows(parts + [jnp.where(keep, scores[start:], MASKED)])
            top = jnp.max(scores, axis=0, keepdims=True)
            powers = jnp.exp(scores - top)
            total = jnp.sum(powers, axis=0, keepdims=True)
            probability = (powers * (1.0 / total)).astype(bf16)
            columns.append(dot(value_columns[kv : kv + HEAD_WIDTH, :stop], probability))
            lse_ref[0, head, start:stop] = (top + jnp.log(total))[0]
        outs.append(jnp.concatenate(columns, axis=1))
    mixed_ref[0] = jnp.concatenate(outs, axis=0).T.astype(bf16)


def whole(array):
    return pl.BlockSpec(array.shape, lambda *_: (0,) * array.ndim)


def entry(array, index=None):
    rest = (0,) * (array.ndim - 1)
    return pl.BlockSpec(
        (1,) + array.shape[1:], lambda p, at: ((p if index is None else index),) + rest
    )


def attend_forward(at, normed, weights, tables):
    length, features = normed.shape
    shapes = [
        jax.ShapeDtypeStruct((PAIRS, length, PAIR_QUERY), bf16),
        jax.ShapeDtypeStruct((PAIRS, length, PAIR_WIDTH), bf16),
        jax.ShapeDtypeStruct((PAIRS, 8, length), f32),
    ]
    return pl.pallas_call(
        attend_forward_kernel,
        grid_spec=pltpu.PrefetchScalarGridSpec(
            num_scalar_prefetch=1,
            grid=(PAIRS,),
            in_specs=[whole(normed)] + [entry(w) for w in weights] + [whole(t) for t in tables],
            out_specs=[entry(shape) for shape in shapes],
            scratch_shapes=[pltpu.VMEM((features, PAIR_WIDTH), bf16)],
        ),
        out_shape=shapes,
        compiler_params=pltpu.CompilerParams(vmem_limit_bytes=VMEM),
        cost_estimate=cost(2e10, 2e7),
    )(at, normed, *weights, *tables)


def middle_kernel(
    at_ref, mixed_ref, own_ref, other_ref, input_ref, gain_ref, middle_ref, fed_ref, weight_ref
):
    step = pl.program_id(0)
    natural(at_ref, own_ref, other_ref, weight_ref)
    added = times_transposed(mixed_ref[0], weight_ref[...])

    @pl.when(step == 0)
    def _():
        middle_ref[...] = input_ref[...].astype(f32) + added

    @pl.when(step > 0)
    def _():
        middle_ref[...] += added

    @pl.when(step == pl.num_programs(0) - 1)
    def _():
        fed_ref[...] = (norm_rows(middle_ref[...])[0] * gain_ref[...]).astype(bf16)


def middle_rows(at, mixed, weights, inputs, gain):
    length, features = inputs.shape
    shapes = [jax.ShapeDtypeStruct((length, features), kind) for kind in (f32, bf16)]
    return pl.pallas_call(
        middle_kernel,
        grid_spec=pltpu.PrefetchScalarGridSpec(
            num_scalar_prefetch=1,
            grid=(PAIRS,),
            in_specs=[entry(mixed)] + [entry(w) for w in weights] + [whole(inputs), whole(gain)],
            out_specs=[whole(shape) for shape in shapes],
            scratch_shapes=[pltpu.VMEM((features, PAIR_QUERY), bf16)],
        ),
        out_shape=shapes,
        compiler_params=pltpu.CompilerParams(vmem_limit_bytes=VMEM),
        cost_estimate=cost(2.4e9, 1e7),
    )(at, mixed, *weights, inputs, gain)


def attend_backward_kernel(
    at_ref,
    branch_ref,
    own_output_ref,
    other_output_ref,
    mixed_ref,
    qkv_ref,
    lse_ref,
    normed_ref,
    own_weight_ref,
    other_weight_ref,
    cosine_ref,
    sine_ref,
    total_ref,
    own_term_ref,
    other_term_ref,
    grad_ref,
    output_ref,
    weight_ref,
    term_ref,
):
    length = branch_ref.shape[0]
    natural(at_ref, own_output_ref, other_output_ref, output_ref)
    natural(at_ref, own_weight_ref, other_weight_ref, weight_ref)
    keep = causal_block()
    blocks = length // BLOCK
    mixed_grad = dot(branch_ref[...], output_ref[...]).astype(bf16)
    query = qkv_ref[0, :, :PAIR_QUERY]
    key = qkv_ref[0, :, PAIR_QUERY : PAIR_QUERY + PAIR_KEY]
    value = qkv_ref[0, :, PAIR_QUERY + PAIR_KEY :]
    scaled_key = (key.astype(f32) * HEAD_WIDTH**-0.5).T.astype(bf16)
    query_grads, key_grads, value_grads = [], [], []
    for side in range(2):
        kv = side * HEAD_WIDTH
        key_part = key[:, kv : kv + HEAD_WIDTH]
        value_part = value[:, kv : kv + HEAD_WIDTH]
        key_grad, value_grad = [None] * blocks, [None] * blocks
        for head in range(side * GROUP, (side + 1) * GROUP):
            column = head * HEAD_WIDTH
            columns = []
            for block in range(blocks):
                start, stop = block * BLOCK, (block + 1) * BLOCK
                query_rows = query[start:stop, column : column + HEAD_WIDTH]
                upstream = mixed_grad[start:stop, column : column + HEAD_WIDTH]
                scores = times_transposed(key_part[:stop], query_rows)
                prob_grad = times_transposed(value_part[:stop], upstream)
                probability = jnp.exp(scores - lse_ref[0, head, start:stop][None, :])
                parts = [probability[:start]] if block else []
                probability = stack_rows(parts + [jnp.where(keep, probability[start:], 0.0)])
                shift = jnp.sum(probability * prob_grad, axis=0, keepdims=True)
                score_grad = (probability * (prob_grad - shift)).astype(bf16)
                value_add = dot(probability.astype(bf16), upstream)
                key_add = dot(score_grad, query_rows)
                for j in range(block + 1):
                    rows = slice(j * BLOCK, (j + 1) * BLOCK)
                    value_grad[j] = (
                        value_add[rows] if value_grad[j] is None else value_grad[j] + value_add[rows]
                    )
                    key_grad[j] = (
                        key_add[rows] if key_grad[j] is None else key_grad[j] + key_add[rows]
                    )
                columns.append(dot(scaled_key[kv : kv + HEAD_WIDTH, :stop], score_grad))
            query_grads.append(jnp.concatenate(columns, axis=1))
        key_grads.append(stack_rows(key_grad))
        value_grads.append(stack_rows(value_grad))
    turned = rotate(
        jnp.concatenate([jnp.concatenate(query_grads, axis=0).T] + key_grads, axis=1),
        cosine_ref[...],
        -sine_ref[...],
    )
    projected_grad = jnp.concatenate([turned] + value_grads, axis=1).astype(bf16)
    term_ref[:, :PAIR_WIDTH] = contract_rows(normed_ref[...], projected_grad).astype(bf16)
    term_ref[:, PAIR_WIDTH:] = contract_rows(branch_ref[...], mixed_ref[0]).astype(bf16)
    shards, half = own_weight_ref.shape[1:3]
    for k in range(shards):
        for side, ref in enumerate((own_term_ref, other_term_ref)):
            start = (at_ref[0] ^ k) * (2 * half) + (at_ref[1] ^ side) * half
            ref[k] = term_ref[pl.ds(pl.multiple_of(start, half), half), :]
    grad_ref[...] = total_ref[...] + times_transposed(projected_grad, weight_ref[...])


def attend_backward(at, m, branch_grad, output, saved, normed, weights, tables, total):
    length, features = branch_grad.shape
    shards, half = weights[0].shape[1:3]
    width = PAIR_WIDTH + PAIR_QUERY
    term = jax.ShapeDtypeStruct((shards, half, width), bf16)
    shapes = [term, term, jax.ShapeDtypeStruct((length, features), f32)]
    ones = [*output, *saved]
    operands = [branch_grad, *ones, normed, *weights, *tables, total]
    specs = [whole(branch_grad)] + [entry(one, m) for one in ones] + [whole(normed)]
    specs += [entry(w, m) for w in weights] + [whole(t) for t in tables] + [whole(total)]
    return pl.pallas_call(
        attend_backward_kernel,
        grid_spec=pltpu.PrefetchScalarGridSpec(
            num_scalar_prefetch=1,
            grid=(1,),
            in_specs=specs,
            out_specs=[whole(shape) for shape in shapes],
            scratch_shapes=[
                pltpu.VMEM((features, PAIR_QUERY), bf16),
                pltpu.VMEM((features, PAIR_WIDTH), bf16),
                pltpu.VMEM((features, width), bf16),
            ],
        ),
        out_shape=shapes,
        input_output_aliases={len(operands): 2},
        compiler_params=pltpu.CompilerParams(vmem_limit_bytes=VMEM),
        cost_estimate=cost(9e9, 1.5e7),
    )(at, *operands)


def expert_kernel(
    first_ref,
    inner_ref,
    outer_ref,
    upstream_ref,
    chosen_ref,
    router_ref,
    weight_ref,
    *refs,
):
    (
        fed_ref,
        row_ref,
        combined_ref,
        pair_ref,
        gated_ref,
        gates_ref,
        gate_grad_ref,
        row_total,
        combined_total,
    ) = refs[-9:]
    step, steps = pl.program_id(0), pl.num_programs(0)
    index = first_ref[0] + step
    lane = lax.broadcasted_iota(jnp.int32, gates_ref.shape, 1)

    @pl.when(step == 0)
    def _():
        @pl.when(first_ref[3] > 0)
        def _():
            fed_ref[...] = inner_ref[...]

        @pl.when(first_ref[3] == 0)
        def _():
            fed_ref[...] = outer_ref[...]

        logits = dot(fed_ref[...], router_ref[...])
        chosen = chosen_ref[0] > 0.0
        logits = jnp.where(chosen, logits, MASKED)
        powers = jnp.where(chosen, jnp.exp(logits - jnp.max(logits, axis=1, keepdims=True)), 0.0)
        gates_ref[...] = powers / jnp.sum(powers, axis=1, keepdims=True)
        gate_grad_ref[...] = jnp.zeros_like(gate_grad_ref)

    gate = jnp.sum(jnp.where(lane == index, gates_ref[...], 0.0), axis=1, keepdims=True)
    gate_grad = None
    width = FF // 2
    for start in range(0, FF, width):
        stop = start + width
        gate_part = dot(fed_ref[...], weight_ref[0, :, start:stop])
        up_part = dot(fed_ref[...], weight_ref[0, :, FF + start : FF + stop])
        raw_grad = dot(upstream_ref[0], weight_ref[0, :, 2 * FF + start : 2 * FF + stop])
        sigma = jax.nn.sigmoid(gate_part)
        activated = gate_part * sigma
        hidden = activated * up_part
        part = jnp.sum(hidden * raw_grad, axis=1, keepdims=True)
        gate_grad = part if gate_grad is None else gate_grad + part
        hidden_grad = gate * raw_grad
        slope = sigma * (1.0 + gate_part * (1.0 - sigma))
        pair_ref[0, :, start:stop] = (hidden_grad * up_part * slope).astype(bf16)
        pair_ref[0, :, FF + start : FF + stop] = (hidden_grad * activated).astype(bf16)
        gated_ref[0, :, start:stop] = (gate * hidden).astype(bf16)
    gate_grad_ref[...] += jnp.where(lane == index, gate_grad, 0.0)
    combined = times_transposed(gated_ref[0], weight_ref[0, :, 2 * FF :])
    row = times_transposed(pair_ref[0], weight_ref[0, :, : 2 * FF])

    @pl.when(step == 0)
    def _():
        combined_total[...] = combined
        row_total[...] = row

    @pl.when(step > 0)
    def _():
        combined_total[...] += combined
        row_total[...] += row

    @pl.when(step == steps - 1)
    def _():
        features = row_total.shape[1]
        row_ref[:, :features] = row_total[...].astype(bf16)
        high = gate_grad_ref[...].astype(bf16)
        low = gate_grad_ref[...] - high.astype(f32)
        row_ref[:, features:] = (high.astype(f32) + pltpu.roll(low, LANES // 2, 1)).astype(bf16)
        combined_ref[0] = combined_total[...].astype(bf16)


def expert_slot(at, choices, upstream, chosen, router, weights, combined):
    length, features = choices[0].shape
    count = weights.shape[0]
    held = [] if isinstance(combined, int) else [combined]
    sequences = combined if isinstance(combined, int) else combined.shape[0]
    full = lambda *shape: pl.BlockSpec(shape, lambda e, at: (0,) * len(shape))
    each = lambda *shape: pl.BlockSpec((1,) + shape, lambda e, at: (e,) + (0,) * len(shape))
    there = lambda i, *shape: pl.BlockSpec(
        (1,) + shape, lambda e, at: (at[i],) + (0,) * len(shape)
    )
    return pl.pallas_call(
        expert_kernel,
        grid_spec=pltpu.PrefetchScalarGridSpec(
            num_scalar_prefetch=1,
            grid=(count,),
            in_specs=[
                full(length, features),
                full(length, features),
                there(1, length, features),
                there(2, length, LANES),
                full(features, LANES),
                each(features, 3 * FF),
            ]
            + [pl.BlockSpec(memory_space=pl.ANY)] * len(held),
            out_specs=[
                full(length, features),
                full(length, features + LANES),
                there(2, length, features),
                each(length, 2 * FF),
                each(length, FF),
            ],
            scratch_shapes=[
                pltpu.VMEM((length, LANES), f32),
                pltpu.VMEM((length, LANES), f32),
                pltpu.VMEM((length, features), f32),
                pltpu.VMEM((length, features), f32),
            ],
        ),
        out_shape=[
            jax.ShapeDtypeStruct((length, features), bf16),
            jax.ShapeDtypeStruct((length, features + LANES), bf16),
            jax.ShapeDtypeStruct((sequences, length, features), bf16),
            jax.ShapeDtypeStruct((count, length, 2 * FF), bf16),
            jax.ShapeDtypeStruct((count, length, FF), bf16),
        ],
        input_output_aliases={7: 2} if held else {},
        compiler_params=pltpu.CompilerParams(vmem_limit_bytes=VMEM),
        cost_estimate=cost(12 * count * length * features * FF, 3.2e7),
    )(at, *choices, upstream, chosen, router, weights, *held)


def fed_grad_kernel(*refs):
    arrived = refs[:-10]
    (
        fed_ref,
        middle_ref,
        upstream_ref,
        chosen_ref,
        router_ref,
        gain_ref,
        middle_grad_ref,
        branch_ref,
        router_grad_ref,
        gain_grad_ref,
    ) = refs[-10:]
    step = pl.program_id(0)
    total = arrived[0][...].astype(f32)
    for ref in arrived[1:]:
        total = total + ref[...].astype(f32)
    features = fed_ref.shape[1]
    parts = total[:, features:]
    gate_grad = parts + pltpu.roll(parts, LANES // 2, 1)
    chosen = chosen_ref[...] > 0.0
    logits = jnp.where(chosen, dot(fed_ref[...], router_ref[...]), MASKED)
    powers = jnp.where(chosen, jnp.exp(logits - jnp.max(logits, axis=1, keepdims=True)), 0.0)
    gates = powers / jnp.sum(powers, axis=1, keepdims=True)
    gate_grad = jnp.where(chosen, gate_grad, 0.0)
    mean = jnp.sum(gates * gate_grad, axis=1, keepdims=True)
    logit_grad = (gates * (gate_grad - mean)).astype(bf16)
    fed_grad = times_transposed(logit_grad, router_ref[...]) + total[:, :features]
    scaled, inverse = norm_rows(middle_ref[...])
    back = norm_back(scaled, inverse, fed_grad * gain_ref[...])
    middle_grad = upstream_ref[...].astype(f32) + back
    middle_grad_ref[...] = middle_grad
    branch_ref[...] = middle_grad.astype(bf16)
    router_grad = contract_rows(logit_grad, fed_ref[...])
    gain_grad = jnp.sum(fed_grad * scaled, axis=0, keepdims=True)

    @pl.when(step == 0)
    def _():
        router_grad_ref[...] = router_grad
        gain_grad_ref[...] = gain_grad

    @pl.when(step > 0)
    def _():
        router_grad_ref[...] += router_grad
        gain_grad_ref[...] += gain_grad


def fed_grads(arrived, fed, middle, upstream, chosen, router, gain):
    length, features = fed.shape
    rows = length // 4
    split = lambda array: pl.BlockSpec((rows, array.shape[1]), lambda i: (i, 0))
    shapes = [
        jax.ShapeDtypeStruct((length, features), f32),
        jax.ShapeDtypeStruct((length, features), bf16),
        jax.ShapeDtypeStruct((LANES, features), f32),
        jax.ShapeDtypeStruct((1, features), f32),
    ]
    operands = [*arrived, fed, middle, upstream, chosen, router, gain]
    return pl.pallas_call(
        fed_grad_kernel,
        grid=(4,),
        in_specs=[split(a) for a in operands[:-2]] + [whole(router), whole(gain)],
        out_specs=[split(shapes[0]), split(shapes[1]), whole(shapes[2]), whole(shapes[3])],
        out_shape=shapes,
        compiler_params=pltpu.CompilerParams(vmem_limit_bytes=VMEM),
        cost_estimate=cost(1e8, 2e7),
    )(*operands)


def expert_grad_kernel(places_ref, *refs):
    slots = (len(refs) - 1) // 4
    fed, upstream, pair, gated = (refs[i * slots : (i + 1) * slots] for i in range(4))
    out_ref = refs[-1]
    inner = outer = None
    for k in range(slots):
        add_inner = contract_rows(fed[k][...], pair[k][0])
        add_outer = contract_rows(upstream[k][0], gated[k][0])
        inner = add_inner if inner is None else inner + add_inner
        outer = add_outer if outer is None else outer + add_outer
    out_ref[0, :, : 2 * FF] = inner.astype(out_ref.dtype)
    out_ref[0, :, 2 * FF :] = outer.astype(out_ref.dtype)


def expert_grads(places, fed, upstream, pairs, gated):
    length, features = fed[0].shape
    slots, count = len(pairs), pairs[0].shape[0]
    rows = features // 2
    column = pl.BlockSpec((length, rows), lambda e, i, at: (0, i))
    there = lambda k: pl.BlockSpec((1, length, rows), lambda e, i, at: (at[k], 0, i))
    each = lambda width: pl.BlockSpec((1, length, width), lambda e, i, at: (e, 0, 0))
    return pl.pallas_call(
        expert_grad_kernel,
        grid_spec=pltpu.PrefetchScalarGridSpec(
            num_scalar_prefetch=1,
            grid=(count, features // rows),
            in_specs=[column] * slots
            + [there(k) for k in range(slots)]
            + [each(2 * FF)] * slots
            + [each(FF)] * slots,
            out_specs=pl.BlockSpec((1, rows, 3 * FF), lambda e, i, at: (e, i, 0)),
        ),
        out_shape=jax.ShapeDtypeStruct((count, features, 3 * FF), bf16),
        compiler_params=pltpu.CompilerParams(vmem_limit_bytes=VMEM),
        cost_estimate=cost(6 * slots * count * length * features * FF, 8e7),
    )(places, *fed, *[upstream] * slots, *pairs, *gated)


def exchange(value, k):
    return lax.ppermute(value, "shard", [(i, i ^ k) for i in range(4)])


def inside(place):
    return (place == 1) | (place == 2)


def sources(place, count):
    if count != 4:
        return [place ^ k for k in range(count)]
    middle = inside(place)
    order = ((1, 3), (2, 1), (3, 2))
    return [place] + [place ^ jnp.where(middle, mid, out) for out, mid in order]


def after(value, *earlier):
    return lax.optimization_barrier((value, earlier))[0]


def line_gather(rows, place, count):
    if count != 4:
        everything = lax.all_gather(rows, "shard", axis=0)
        for source in sources(place, count):
            yield (pick(everything, source),) * 2
            yield
        return
    middle = inside(place)
    near = exchange(rows, 1)
    across = lax.ppermute(rows, "shard", [(1, 2), (2, 1)])
    made = yield rows, rows
    yield
    near_on, across_on = after((near, across), made)
    second_inside = lax.ppermute(near_on, "shard", [(1, 2), (2, 1)])
    second_outside = lax.ppermute(across_on, "shard", [(1, 0), (2, 3)])
    yield across, near
    yield
    third_outside = lax.ppermute(second_inside, "shard", [(1, 0), (2, 3)])
    yield near, second_outside
    yield
    yield second_inside, third_outside
    yield


def scatter_all(parts, place, count):
    stacked = jnp.stack(parts)
    ordered = jnp.stack([pick(stacked, place ^ d) for d in range(count)])
    return lax.psum_scatter(ordered, "shard", scatter_dimension=0, tiled=False)


def line_send(part, k):
    ways = {
        1: ([(0, 1), (3, 2)], [(1, 2), (2, 1)]),
        2: ([(0, 2), (3, 1)], [(1, 0), (2, 3)]),
        3: ([(0, 3), (3, 0)], [(1, 3), (2, 0)]),
    }
    return [lax.ppermute(part, "shard", way) for way in ways[k]]


def total_of(kept, arrived):
    total = kept.astype(f32)
    for part in arrived:
        total = total + part.astype(f32)
    return total


def hop(value, bit):
    return lax.ppermute(value, "rep", [(i, i ^ bit) for i in range(8)])


def pick(stacked, index, axis=0):
    return lax.dynamic_index_in_dim(stacked, index, axis, False)


def gather_near(mine):
    return jnp.stack([exchange(mine, k) for k in range(1, 4)])


def send_pairs(near):
    return [hop(near, 2 * m) for m in range(1, 4)]


def join_pairs(local, parts, core, spot, earlier=()):
    own = jnp.stack(
        [
            jnp.concatenate([local(spot ^ m, core)[None], part])
            for m, part in enumerate(parts)
        ]
    )
    own = after(own, *earlier)
    return own, hop(own, 1)


def join_chip(term, special):
    kept, given = term
    return (kept.astype(f32) + hop(given, 1).astype(f32)).astype(bf16) if special else kept


def place_kernel(at_ref, own_ref, other_ref, attend_ref, output_ref):
    half = own_ref.shape[1]
    query, key = QUERY_HEADS * HEAD_WIDTH, KEY_VALUE_HEADS * HEAD_WIDTH
    for m in range(PAIRS):
        pair = at_ref[0] ^ m
        for side, ref in enumerate((own_ref, other_ref)):
            rows = pl.ds(pl.multiple_of((at_ref[1] ^ side) * half, half), half)
            start = 0
            for out_ref, base, width in (
                (attend_ref, 0, PAIR_QUERY),
                (attend_ref, query, PAIR_KEY),
                (attend_ref, query + key, PAIR_KEY),
                (output_ref, 0, PAIR_QUERY),
            ):
                columns = pl.ds(pl.multiple_of(base + pair * width, LANES), width)
                out_ref[rows, columns] = ref[m, :, start : start + width].astype(f32)
                start += width


def finish_pairs(plane, core, spot):
    piece = plane[0].astype(f32)
    for k in range(1, 4):
        piece = piece + exchange(plane[k], k).astype(f32)
    piece = piece.astype(plane.dtype)
    mine = jnp.stack([piece] + [hop(piece, 2 * m) for m in range(1, 4)])
    other = hop(mine, 1)
    rows = 2 * piece.shape[0]
    return pl.pallas_call(
        place_kernel,
        grid_spec=pltpu.PrefetchScalarGridSpec(
            num_scalar_prefetch=1,
            grid=(1,),
            in_specs=[whole(mine), whole(other)],
            out_specs=[
                pl.BlockSpec((rows, PAIRS * PAIR_WIDTH), lambda i, at: (0, 0)),
                pl.BlockSpec((rows, PAIRS * PAIR_QUERY), lambda i, at: (0, 0)),
            ],
        ),
        out_shape=[
            jax.ShapeDtypeStruct((rows, PAIRS * PAIR_WIDTH), f32),
            jax.ShapeDtypeStruct((rows, PAIRS * PAIR_QUERY), f32),
        ],
        compiler_params=pltpu.CompilerParams(vmem_limit_bytes=VMEM),
        cost_estimate=cost(1e6, 1e7),
    )(jnp.stack([spot, core]).astype(jnp.int32), mine, other)


def reduce_terms(terms):
    part = lax.psum_scatter(terms, "shard", scatter_dimension=1, tiled=False)
    return lax.psum(part, "rep")


def body(
    inputs,
    query_key_value_weight,
    output_weight,
    attention_gain,
    feed_gain,
    router_weight,
    expert_weight,
    routes,
    cotangent,
    *,
    places,
    ranks,
):
    length, features = inputs.shape
    own = query_key_value_weight.shape[0]
    local = expert_weight.shape[0]
    query_width = QUERY_HEADS * HEAD_WIDTH
    key_width = KEY_VALUE_HEADS * HEAD_WIDTH
    place, rank = lax.axis_index("shard"), lax.axis_index("rep")

    special = places == 4 and ranks == 8
    half = own // 2
    base, core, spot = (place, rank % 2, rank // 2) if special else (0, 0, 0)

    projection = query_key_value_weight

    def projection_share(pair, side):
        rows = lax.dynamic_slice_in_dim(projection, side * half, half, 0)
        return jnp.concatenate(
            [
                lax.dynamic_slice_in_dim(rows, pair * PAIR_QUERY, PAIR_QUERY, 1),
                lax.dynamic_slice_in_dim(rows, query_width + pair * PAIR_KEY, PAIR_KEY, 1),
                lax.dynamic_slice_in_dim(
                    rows, query_width + key_width + pair * PAIR_KEY, PAIR_KEY, 1
                ),
            ],
            axis=1,
        )

    def output_share(pair, side):
        return lax.dynamic_slice(
            output_weight, (side * half, pair * PAIR_QUERY), (half, PAIR_QUERY)
        )

    chosen_own = jnp.sum(
        (routes[:, :, None] == jnp.arange(EXPERTS, dtype=jnp.int32)).astype(f32), axis=1
    )
    small = jnp.concatenate(
        [
            attention_gain.reshape(-1),
            feed_gain.reshape(-1),
            router_weight.reshape(-1),
            chosen_own.astype(bf16).reshape(-1),
        ]
    )
    if special:
        extra = -(-small.size // (16 * PAIR_WIDTH)) * 16
        below = jnp.pad(small, (0, extra * PAIR_WIDTH - small.size)).reshape(extra, PAIR_WIDTH)
        near = gather_near(jnp.concatenate([projection_share(spot, core), below]))
        projection_near = near[:, :half]
        small_slots = jnp.concatenate(
            [small[None], near[:, half:].reshape(3, -1)[:, : small.size]]
        )
        small_all = jnp.stack([pick(small_slots, place ^ k) for k in range(4)])
        projection_sent = send_pairs(projection_near)
        output_near = gather_near(after(output_share(spot, core), projection_near))
        cotangent_sent = after(cotangent, projection_near)
    else:
        gathered = lax.all_gather(projection, "shard", axis=0)
        gathered_output = lax.all_gather(output_weight, "shard", axis=0)
        columns = jnp.concatenate(
            [
                gathered[:, :, :query_width].reshape(places, own, PAIRS, PAIR_QUERY),
                gathered[:, :, query_width : query_width + key_width].reshape(
                    places, own, PAIRS, PAIR_KEY
                ),
                gathered[:, :, query_width + key_width :].reshape(places, own, PAIRS, PAIR_KEY),
            ],
            axis=3,
        ).transpose(2, 0, 1, 3)
        attend_columns = (columns[:, :, :half], columns[:, :, half:])
        columns = gathered_output.reshape(places, own, PAIRS, PAIR_QUERY).transpose(2, 0, 1, 3)
        output_columns = (columns[:, :, :half], columns[:, :, half:])
        small_all = lax.all_gather(small, "shard", axis=0)
        cotangent_sent = cotangent

    upstream_all = lax.all_gather(cotangent_sent, "shard", axis=0)

    tables = rotary_tables(length, PAIR_QUERY + PAIR_KEY)
    residual = inputs.astype(f32)
    scaled_in, inverse_in = norm_rows(residual)
    attention_scale = small_all[:, :own].reshape(features).astype(f32)
    feed_scale = small_all[:, own : 2 * own].reshape(features).astype(f32)
    router_full = small_all[:, 2 * own : (2 + EXPERTS) * own].reshape(features, EXPERTS)
    chosen_all = small_all[:, (2 + EXPERTS) * own :].reshape(places, length, EXPERTS).astype(f32)
    normed = (scaled_in * attention_scale).astype(bf16)
    where = jnp.stack([base, core]).astype(jnp.int32)

    def attention():
        if special:
            attend_weights = join_pairs(
                projection_share, [projection_near] + projection_sent, core, spot
            )
            output_sent = send_pairs(after(output_near, attend_weights))
        else:
            attend_weights = attend_columns
        kept = attend_forward(where, normed, attend_weights, tables)
        if special:
            output_weights = join_pairs(
                output_share, [output_near] + output_sent, core, spot, [kept[0]]
            )
        else:
            output_weights = output_columns
        rows = middle_rows(where, kept[0], output_weights, inputs, feed_scale[None])
        return (*attend_weights, *output_weights, *kept, *rows)

    always = routes[0, 0] >= 0

    def apart(function, shapes):
        empty = lambda: tuple(jnp.zeros(*shape) for shape in shapes)
        return lax.cond(always, function, empty)

    share = (PAIRS, places, half)
    own_a, other_a, own_o, other_o, mixed, qkv, lse, middle, fed = apart(
        attention,
        [((*share, PAIR_WIDTH), bf16)] * 2
        + [((*share, PAIR_QUERY), bf16)] * 2
        + [
            ((PAIRS, length, PAIR_QUERY), bf16),
            ((PAIRS, length, PAIR_WIDTH), bf16),
            ((PAIRS, 8, length), f32),
            ((length, features), f32),
            ((length, features), bf16),
        ],
    )
    attend_weights, output_weights = (own_a, other_a), (own_o, other_o)
    router_wide = jnp.pad(router_full, ((0, 0), (0, LANES - EXPERTS)))
    chosen_wide = jnp.pad(chosen_all, ((0, 0), (0, 0), (0, LANES - EXPERTS)))
    rows, pair_grads, gated = [], [], []
    combined = places
    order = sources(place, places)
    middle_place = inside(place).astype(jnp.int32)
    fed_slots, rows_come, arriving = [], [], line_gather(fed, place, places)
    for k, source in enumerate(order):
        index = jnp.zeros_like(source) if k == 0 else source
        at = jnp.stack([place * local, index, source, middle_place]).astype(jnp.int32)
        rows_up = cotangent[None] if k == 0 else upstream_all
        fed_k, row, combined, *kept = expert_slot(
            at, next(arriving), rows_up, chosen_wide, router_wide, expert_weight, combined
        )
        for held, value in zip((fed_slots, rows, pair_grads, gated), (fed_k, row, *kept)):
            held.append(value)
        arriving.send((row, upstream_all))
        if special and k:
            rows_come += line_send(row, k)
    expert_term = expert_grads(
        jnp.stack(order).astype(jnp.int32),
        fed_slots,
        upstream_all,
        pair_grads,
        gated,
    )
    expert_total = lax.psum(expert_term, "rep").astype(f32)

    if special:
        arrived = [rows[0], *rows_come]
    else:
        arrived = [scatter_all(rows, place, places)]
    arrived = after(arrived, expert_term)

    combined = lax.all_to_all(after(combined, arrived), "shard", 0, 0)

    def rest():
        chosen = jnp.pad(chosen_own, ((0, 0), (0, LANES - EXPERTS)))
        middle_grad, branch_grad, router_term, feed_term = fed_grads(
            arrived, fed, middle, cotangent, chosen, router_wide, feed_scale[None]
        )
        normed_grad = jnp.zeros((length, features), f32)
        terms, chips = [None] * PAIRS, [None] * PAIRS
        steps = (3, 1, 2, 0)
        for i, m in enumerate(steps):
            ready = [chips[steps[i - 2]]] if i >= 2 else []
            own_term, other_term, normed_grad = attend_backward(
                where,
                m,
                after(branch_grad, *ready),
                output_weights,
                (mixed, qkv, lse),
                normed,
                attend_weights,
                tables,
                normed_grad,
            )
            terms[m] = (own_term, other_term)
            if i >= 1:
                chips[steps[i - 1]] = join_chip(terms[steps[i - 1]], special)
        if special:
            chips[0] = join_chip(terms[0], special)
            part = half // 2
            upper, lower = (lambda c: c[:, :part]), (lambda c: c[:, part:])
            add = lambda a, b: a.astype(f32) + b.astype(f32)
            over_x = hop(jnp.stack([upper(chips[1]), upper(chips[3])]), 2)
            over_y = hop(jnp.stack([lower(chips[2]), lower(chips[3])]), 4)
            upper_y = hop(add(upper(chips[2]), over_x[1]).astype(bf16), 4)
            lower_x = hop(add(lower(chips[1]), over_y[1]).astype(bf16), 2)
            plane = jnp.concatenate(
                [
                    add(upper(chips[0]), over_x[0]) + upper_y.astype(f32),
                    add(lower(chips[0]), over_y[0]) + lower_x.astype(f32),
                ],
                axis=1,
            )
            attend_total, output_total = finish_pairs(plane.astype(bf16), core, spot)
        else:
            stacked = jnp.stack([jnp.stack(term) for term in terms])
            weight_sums = reduce_terms(stacked.transpose(0, 2, 1, 3, 4))
            weight_sums = weight_sums.reshape(PAIRS, own, -1).transpose(1, 0, 2).astype(f32)
            attend_total = jnp.concatenate(
                [
                    weight_sums[:, :, :PAIR_QUERY].reshape(own, query_width),
                    weight_sums[:, :, PAIR_QUERY : PAIR_QUERY + PAIR_KEY].reshape(own, key_width),
                    weight_sums[:, :, PAIR_QUERY + PAIR_KEY : PAIR_WIDTH].reshape(own, key_width),
                ],
                axis=1,
            )
            output_total = weight_sums[:, :, PAIR_WIDTH:].reshape(own, query_width)

        attention_term = jnp.sum(normed_grad * scaled_in, axis=0)
        input_grad = (
            middle_grad + norm_back(scaled_in, inverse_in, normed_grad * attention_scale)
        ).astype(bf16)

        small_terms = jnp.concatenate(
            [attention_term[None], feed_term, router_term[:EXPERTS]], axis=0
        )
        if special:
            for axis, bit in (("rep", 1), ("rep", 2), ("rep", 4), ("shard", 1), ("shard", 2)):
                size = 8 if axis == "rep" else 4
                pairs = [(i, i ^ bit) for i in range(size)]
                small_terms = small_terms + lax.ppermute(small_terms, axis, pairs)
        else:
            small_terms = lax.psum(small_terms, ("rep", "shard"))
        small_sums = lax.dynamic_slice_in_dim(small_terms, place * own, own, 1)
        return (
            input_grad,
            attend_total,
            output_total,
            small_sums[0],
            small_sums[1],
            small_sums[2:].T,
        )

    shapes = (
        ((length, features), bf16),
        (query_key_value_weight.shape, f32),
        (output_weight.shape, f32),
        ((own,), f32),
        ((own,), f32),
        ((own, EXPERTS), f32),
    )
    grads = apart(rest, shapes)
    activations = (middle + jnp.sum(combined.astype(f32), axis=0)).astype(bf16)
    return (activations, *grads, expert_total)


def solution(mesh):
    in_specs = (
        P(("rep", "shard"), None),
        P("shard", None),
        P("shard", None),
        P("shard"),
        P("shard"),
        P("shard", None),
        P("shard", None, None),
        P(("rep", "shard"), None),
        P(("rep", "shard"), None),
    )
    out_specs = (
        P(("rep", "shard"), None),
        P(("rep", "shard"), None),
        P("shard", None),
        P("shard", None),
        P("shard"),
        P("shard"),
        P("shard", None),
        P("shard", None, None),
    )
    run = functools.partial(body, places=mesh.shape["shard"], ranks=mesh.shape["rep"])
    return jax.shard_map(run, mesh=mesh, in_specs=in_specs, out_specs=out_specs, check_vma=False)
```

```python
import functools

import jax
import jax.numpy as jnp
from jax import lax
from jax.experimental import pallas as pl
from jax.experimental.pallas import tpu as pltpu
from jax.sharding import PartitionSpec as P

QUERY_HEADS = 24
KEY_VALUE_HEADS = 8
HEAD_WIDTH = 64
FF = 512
EXPERTS = 16

EPSILON = 1e-06
MASKED = -1e30

GROUP = QUERY_HEADS // KEY_VALUE_HEADS
PAIRS = KEY_VALUE_HEADS // 2
PAIR_QUERY = 2 * GROUP * HEAD_WIDTH
PAIR_KEY = 2 * HEAD_WIDTH
PAIR_WIDTH = PAIR_QUERY + 2 * PAIR_KEY
BLOCK = 256
LANES = 128
VMEM = 60 * 2**20


def cost(flops, moved):
    return pl.CostEstimate(flops=int(flops), bytes_accessed=int(moved), transcendentals=0)

bf16 = jnp.bfloat16
f32 = jnp.float32


def dot(left, right):
    return jnp.dot(left, right, preferred_element_type=f32)


def contract_rows(left, right):
    return lax.dot_general(left, right, (((0,), (0,)), ((), ())), preferred_element_type=f32)


def times_transposed(left, right):
    return lax.dot_general(left, right, (((1,), (1,)), ((), ())), preferred_element_type=f32)


def norm_rows(value_rows):
    inverse = lax.rsqrt(jnp.mean(value_rows * value_rows, axis=-1, keepdims=True) + EPSILON)
    return (value_rows * inverse, inverse)


def norm_back(scaled, inverse, upstream):
    return inverse * (upstream - scaled * jnp.mean(upstream * scaled, axis=-1, keepdims=True))


def rotary_tables(length, width):
    half = HEAD_WIDTH // 2
    frequency = 10000.0 ** (-2.0 * jnp.arange(half, dtype=f32) / HEAD_WIDTH)
    angles = jnp.arange(length, dtype=f32)[:, None] * frequency[None, :]
    cosine, sine = jnp.cos(angles), jnp.sin(angles)
    heads = width // HEAD_WIDTH
    return (
        jnp.tile(jnp.concatenate([cosine, cosine], axis=1), (1, heads)),
        jnp.tile(jnp.concatenate([-sine, sine], axis=1), (1, heads)),
    )


def rotate(values, cosine, sine):
    width = values.shape[1]
    half = HEAD_WIDTH // 2
    lane = lax.broadcasted_iota(jnp.int32, values.shape, 1)
    swapped = jnp.where(
        lane % HEAD_WIDTH < half,
        pltpu.roll(values, width - half, 1),
        pltpu.roll(values, half, 1),
    )
    return values * cosine + swapped * sine


def causal_block():
    shape = (BLOCK, BLOCK)
    return lax.broadcasted_iota(jnp.int32, shape, 0) <= lax.broadcasted_iota(jnp.int32, shape, 1)


def stack_rows(parts):
    return parts[0] if len(parts) == 1 else jnp.concatenate(parts, axis=0)


def natural(at_ref, own_ref, other_ref, held_ref):
    shards, half = own_ref.shape[1:3]
    for k in range(shards):
        for side, ref in enumerate((own_ref, other_ref)):
            start = (at_ref[0] ^ k) * (2 * half) + (at_ref[1] ^ side) * half
            held_ref[pl.ds(pl.multiple_of(start, half), half), :] = ref[0, k]


def attend_forward_kernel(
    at_ref, normed_ref, own_ref, other_ref, cosine_ref, sine_ref, mixed_ref, qkv_ref, lse_ref, weight_ref
):
    length = normed_ref.shape[0]
    natural(at_ref, own_ref, other_ref, weight_ref)
    keep = causal_block()
    projected = dot(normed_ref[...], weight_ref[...])
    rotated = rotate(projected[:, : PAIR_QUERY + PAIR_KEY], cosine_ref[...], sine_ref[...])
    query = (rotated[:, :PAIR_QUERY] * HEAD_WIDTH**-0.5).astype(bf16)
    key = rotated[:, PAIR_QUERY:].astype(bf16)
    value = projected[:, PAIR_QUERY + PAIR_KEY :].astype(bf16)
    qkv_ref[0, :, :PAIR_QUERY] = query
    qkv_ref[0, :, PAIR_QUERY : PAIR_QUERY + PAIR_KEY] = key
    qkv_ref[0, :, PAIR_QUERY + PAIR_KEY :] = value
    value_columns = value.T
    outs = []
    for head in range(2 * GROUP):
        kv = (head // GROUP) * HEAD_WIDTH
        columns = []
        for block in range(length // BLOCK):
            start, stop = block * BLOCK, (block + 1) * BLOCK
            scores = times_transposed(
                key[:stop, kv : kv + HEAD_WIDTH],
                query[start:stop, head * HEAD_WIDTH : (head + 1) * HEAD_WIDTH],
            )
            parts = [scores[:start]] if block else []
            scores = stack_rows(parts + [jnp.where(keep, scores[start:], MASKED)])
            top = jnp.max(scores, axis=0, keepdims=True)
            powers = jnp.exp(scores - top)
            total = jnp.sum(powers, axis=0, keepdims=True)
            probability = (powers * (1.0 / total)).astype(bf16)
            columns.append(dot(value_columns[kv : kv + HEAD_WIDTH, :stop], probability))
            lse_ref[0, head, start:stop] = (top + jnp.log(total))[0]
        outs.append(jnp.concatenate(columns, axis=1))
    mixed_ref[0] = jnp.concatenate(outs, axis=0).T.astype(bf16)


def whole(array):
    return pl.BlockSpec(array.shape, lambda *_: (0,) * array.ndim)


def entry(array, index=None):
    rest = (0,) * (array.ndim - 1)
    return pl.BlockSpec(
        (1,) + array.shape[1:], lambda p, at: ((p if index is None else index),) + rest
    )


def attend_forward(at, normed, weights, tables):
    length, features = normed.shape
    shapes = [
        jax.ShapeDtypeStruct((PAIRS, length, PAIR_QUERY), bf16),
        jax.ShapeDtypeStruct((PAIRS, length, PAIR_WIDTH), bf16),
        jax.ShapeDtypeStruct((PAIRS, 8, length), f32),
    ]
    return pl.pallas_call(
        attend_forward_kernel,
        grid_spec=pltpu.PrefetchScalarGridSpec(
            num_scalar_prefetch=1,
            grid=(PAIRS,),
            in_specs=[whole(normed)] + [entry(w) for w in weights] + [whole(t) for t in tables],
            out_specs=[entry(shape) for shape in shapes],
            scratch_shapes=[pltpu.VMEM((features, PAIR_WIDTH), bf16)],
        ),
        out_shape=shapes,
        compiler_params=pltpu.CompilerParams(vmem_limit_bytes=VMEM),
        cost_estimate=cost(2e10, 2e7),
    )(at, normed, *weights, *tables)


def middle_kernel(
    at_ref, mixed_ref, own_ref, other_ref, input_ref, gain_ref, middle_ref, fed_ref, weight_ref
):
    step = pl.program_id(0)
    natural(at_ref, own_ref, other_ref, weight_ref)
    added = times_transposed(mixed_ref[0], weight_ref[...])

    @pl.when(step == 0)
    def _():
        middle_ref[...] = input_ref[...].astype(f32) + added

    @pl.when(step > 0)
    def _():
        middle_ref[...] += added

    @pl.when(step == pl.num_programs(0) - 1)
    def _():
        fed_ref[...] = (norm_rows(middle_ref[...])[0] * gain_ref[...]).astype(bf16)


def middle_rows(at, mixed, weights, inputs, gain):
    length, features = inputs.shape
    shapes = [jax.ShapeDtypeStruct((length, features), kind) for kind in (f32, bf16)]
    return pl.pallas_call(
        middle_kernel,
        grid_spec=pltpu.PrefetchScalarGridSpec(
            num_scalar_prefetch=1,
            grid=(PAIRS,),
            in_specs=[entry(mixed)] + [entry(w) for w in weights] + [whole(inputs), whole(gain)],
            out_specs=[whole(shape) for shape in shapes],
            scratch_shapes=[pltpu.VMEM((features, PAIR_QUERY), bf16)],
        ),
        out_shape=shapes,
        compiler_params=pltpu.CompilerParams(vmem_limit_bytes=VMEM),
        cost_estimate=cost(2.4e9, 1e7),
    )(at, mixed, *weights, inputs, gain)


def attend_backward_kernel(
    at_ref,
    branch_ref,
    own_output_ref,
    other_output_ref,
    mixed_ref,
    qkv_ref,
    lse_ref,
    normed_ref,
    own_weight_ref,
    other_weight_ref,
    cosine_ref,
    sine_ref,
    total_ref,
    own_term_ref,
    other_term_ref,
    grad_ref,
    output_ref,
    weight_ref,
    term_ref,
):
    length = branch_ref.shape[0]
    natural(at_ref, own_output_ref, other_output_ref, output_ref)
    natural(at_ref, own_weight_ref, other_weight_ref, weight_ref)
    keep = causal_block()
    blocks = length // BLOCK
    mixed_grad = dot(branch_ref[...], output_ref[...]).astype(bf16)
    query = qkv_ref[0, :, :PAIR_QUERY]
    key = qkv_ref[0, :, PAIR_QUERY : PAIR_QUERY + PAIR_KEY]
    value = qkv_ref[0, :, PAIR_QUERY + PAIR_KEY :]
    scaled_key = (key.astype(f32) * HEAD_WIDTH**-0.5).T.astype(bf16)
    query_grads, key_grads, value_grads = [], [], []
    for side in range(2):
        kv = side * HEAD_WIDTH
        key_part = key[:, kv : kv + HEAD_WIDTH]
        value_part = value[:, kv : kv + HEAD_WIDTH]
        key_grad, value_grad = [None] * blocks, [None] * blocks
        for head in range(side * GROUP, (side + 1) * GROUP):
            column = head * HEAD_WIDTH
            columns = []
            for block in range(blocks):
                start, stop = block * BLOCK, (block + 1) * BLOCK
                query_rows = query[start:stop, column : column + HEAD_WIDTH]
                upstream = mixed_grad[start:stop, column : column + HEAD_WIDTH]
                scores = times_transposed(key_part[:stop], query_rows)
                prob_grad = times_transposed(value_part[:stop], upstream)
                probability = jnp.exp(scores - lse_ref[0, head, start:stop][None, :])
                parts = [probability[:start]] if block else []
                probability = stack_rows(parts + [jnp.where(keep, probability[start:], 0.0)])
                shift = jnp.sum(probability * prob_grad, axis=0, keepdims=True)
                score_grad = (probability * (prob_grad - shift)).astype(bf16)
                value_add = dot(probability.astype(bf16), upstream)
                key_add = dot(score_grad, query_rows)
                for j in range(block + 1):
                    rows = slice(j * BLOCK, (j + 1) * BLOCK)
                    value_grad[j] = (
                        value_add[rows] if value_grad[j] is None else value_grad[j] + value_add[rows]
                    )
                    key_grad[j] = (
                        key_add[rows] if key_grad[j] is None else key_grad[j] + key_add[rows]
                    )
                columns.append(dot(scaled_key[kv : kv + HEAD_WIDTH, :stop], score_grad))
            query_grads.append(jnp.concatenate(columns, axis=1))
        key_grads.append(stack_rows(key_grad))
        value_grads.append(stack_rows(value_grad))
    turned = rotate(
        jnp.concatenate([jnp.concatenate(query_grads, axis=0).T] + key_grads, axis=1),
        cosine_ref[...],
        -sine_ref[...],
    )
    projected_grad = jnp.concatenate([turned] + value_grads, axis=1).astype(bf16)
    term_ref[:, :PAIR_WIDTH] = contract_rows(normed_ref[...], projected_grad).astype(bf16)
    term_ref[:, PAIR_WIDTH:] = contract_rows(branch_ref[...], mixed_ref[0]).astype(bf16)
    shards, half = own_weight_ref.shape[1:3]
    for k in range(shards):
        for side, ref in enumerate((own_term_ref, other_term_ref)):
            start = (at_ref[0] ^ k) * (2 * half) + (at_ref[1] ^ side) * half
            ref[k] = term_ref[pl.ds(pl.multiple_of(start, half), half), :]
    grad_ref[...] = total_ref[...] + times_transposed(projected_grad, weight_ref[...])


def attend_backward(at, m, branch_grad, output, saved, normed, weights, tables, total):
    length, features = branch_grad.shape
    shards, half = weights[0].shape[1:3]
    width = PAIR_WIDTH + PAIR_QUERY
    term = jax.ShapeDtypeStruct((shards, half, width), bf16)
    shapes = [term, term, jax.ShapeDtypeStruct((length, features), f32)]
    ones = [*output, *saved]
    operands = [branch_grad, *ones, normed, *weights, *tables, total]
    specs = [whole(branch_grad)] + [entry(one, m) for one in ones] + [whole(normed)]
    specs += [entry(w, m) for w in weights] + [whole(t) for t in tables] + [whole(total)]
    return pl.pallas_call(
        attend_backward_kernel,
        grid_spec=pltpu.PrefetchScalarGridSpec(
            num_scalar_prefetch=1,
            grid=(1,),
            in_specs=specs,
            out_specs=[whole(shape) for shape in shapes],
            scratch_shapes=[
                pltpu.VMEM((features, PAIR_QUERY), bf16),
                pltpu.VMEM((features, PAIR_WIDTH), bf16),
                pltpu.VMEM((features, width), bf16),
            ],
        ),
        out_shape=shapes,
        input_output_aliases={len(operands): 2},
        compiler_params=pltpu.CompilerParams(vmem_limit_bytes=VMEM),
        cost_estimate=cost(9e9, 1.5e7),
    )(at, *operands)


def expert_kernel(
    sequences,
    table_ref,
    inner_ref,
    outer_ref,
    upstream_ref,
    chosen_ref,
    router_ref,
    weight_ref,
    *refs,
):
    (
        fed_ref,
        row_ref,
        combined_ref,
        pair_ref,
        gated_ref,
        gates_ref,
        gate_grad_ref,
        row_total,
        combined_total,
    ) = refs[-9:]
    step, steps = pl.program_id(0), pl.num_programs(0)
    index = table_ref[sequences + 1] + step
    lane = lax.broadcasted_iota(jnp.int32, gates_ref.shape, 1)

    @pl.when(step == 0)
    def _():
        @pl.when(table_ref[sequences + 2] > 0)
        def _():
            fed_ref[...] = inner_ref[...]

        @pl.when(table_ref[sequences + 2] == 0)
        def _():
            fed_ref[...] = outer_ref[...]

        logits = dot(fed_ref[...], router_ref[...])
        chosen = chosen_ref[0] > 0.0
        logits = jnp.where(chosen, logits, MASKED)
        powers = jnp.where(chosen, jnp.exp(logits - jnp.max(logits, axis=1, keepdims=True)), 0.0)
        gates_ref[...] = powers / jnp.sum(powers, axis=1, keepdims=True)
        gate_grad_ref[...] = jnp.zeros_like(gate_grad_ref)

    gate = jnp.sum(jnp.where(lane == index, gates_ref[...], 0.0), axis=1, keepdims=True)
    gate_grad = None
    width = FF // 2
    for start in range(0, FF, width):
        stop = start + width
        gate_part = dot(fed_ref[...], weight_ref[0, :, start:stop])
        up_part = dot(fed_ref[...], weight_ref[0, :, FF + start : FF + stop])
        raw_grad = dot(upstream_ref[0], weight_ref[0, :, 2 * FF + start : 2 * FF + stop])
        sigma = jax.nn.sigmoid(gate_part)
        activated = gate_part * sigma
        hidden = activated * up_part
        part = jnp.sum(hidden * raw_grad, axis=1, keepdims=True)
        gate_grad = part if gate_grad is None else gate_grad + part
        hidden_grad = gate * raw_grad
        slope = sigma * (1.0 + gate_part * (1.0 - sigma))
        pair_ref[0, :, start:stop] = (hidden_grad * up_part * slope).astype(bf16)
        pair_ref[0, :, FF + start : FF + stop] = (hidden_grad * activated).astype(bf16)
        gated_ref[0, :, start:stop] = (gate * hidden).astype(bf16)
    gate_grad_ref[...] += jnp.where(lane == index, gate_grad, 0.0)
    combined = times_transposed(gated_ref[0], weight_ref[0, :, 2 * FF :])
    row = times_transposed(pair_ref[0], weight_ref[0, :, : 2 * FF])

    @pl.when(step == 0)
    def _():
        combined_total[...] = combined
        row_total[...] = row

    @pl.when(step > 0)
    def _():
        combined_total[...] += combined
        row_total[...] += row

    @pl.when(step == steps - 1)
    def _():
        features = row_total.shape[1]
        row_ref[:, :features] = row_total[...].astype(bf16)
        high = gate_grad_ref[...].astype(bf16)
        low = gate_grad_ref[...] - high.astype(f32)
        row_ref[:, features:] = (high.astype(f32) + pltpu.roll(low, LANES // 2, 1)).astype(bf16)
        combined_ref[0] = combined_total[...].astype(bf16)


def expert_slot(at, k, choices, upstream, chosen, router, weights, combined):
    length, features = choices[0].shape
    count = weights.shape[0]
    held = [] if isinstance(combined, int) else [combined]
    sequences = combined if isinstance(combined, int) else combined.shape[0]
    full = lambda *shape: pl.BlockSpec(shape, lambda e, at: (0,) * len(shape))
    each = lambda *shape: pl.BlockSpec((1,) + shape, lambda e, at: (e,) + (0,) * len(shape))
    there = lambda i, *shape: pl.BlockSpec(
        (1,) + shape, lambda e, at: (at[i],) + (0,) * len(shape)
    )
    return pl.pallas_call(
        functools.partial(expert_kernel, sequences),
        grid_spec=pltpu.PrefetchScalarGridSpec(
            num_scalar_prefetch=1,
            grid=(count,),
            in_specs=[
                full(length, features),
                full(length, features),
                there(sequences + 3 + k, length, features),
                there(k, length, LANES),
                full(features, LANES),
                each(features, 3 * FF),
            ]
            + [pl.BlockSpec(memory_space=pl.ANY)] * len(held),
            out_specs=[
                full(length, features),
                full(length, features + LANES),
                there(k, length, features),
                each(length, 2 * FF),
                each(length, FF),
            ],
            scratch_shapes=[
                pltpu.VMEM((length, LANES), f32),
                pltpu.VMEM((length, LANES), f32),
                pltpu.VMEM((length, features), f32),
                pltpu.VMEM((length, features), f32),
            ],
        ),
        out_shape=[
            jax.ShapeDtypeStruct((length, features), bf16),
            jax.ShapeDtypeStruct((length, features + LANES), bf16),
            jax.ShapeDtypeStruct((sequences, length, features), bf16),
            jax.ShapeDtypeStruct((count, length, 2 * FF), bf16),
            jax.ShapeDtypeStruct((count, length, FF), bf16),
        ],
        input_output_aliases={7: 2} if held else {},
        compiler_params=pltpu.CompilerParams(vmem_limit_bytes=VMEM),
        cost_estimate=cost(12 * count * length * features * FF, 3.2e7),
    )(at, *choices, upstream, chosen, router, weights, *held)


def fed_grad_kernel(*refs):
    arrived = refs[:-10]
    (
        fed_ref,
        middle_ref,
        upstream_ref,
        chosen_ref,
        router_ref,
        gain_ref,
        middle_grad_ref,
        branch_ref,
        router_grad_ref,
        gain_grad_ref,
    ) = refs[-10:]
    step = pl.program_id(0)
    total = arrived[0][...].astype(f32)
    for ref in arrived[1:]:
        total = total + ref[...].astype(f32)
    features = fed_ref.shape[1]
    parts = total[:, features:]
    gate_grad = parts + pltpu.roll(parts, LANES // 2, 1)
    chosen = chosen_ref[...] > 0.0
    logits = jnp.where(chosen, dot(fed_ref[...], router_ref[...]), MASKED)
    powers = jnp.where(chosen, jnp.exp(logits - jnp.max(logits, axis=1, keepdims=True)), 0.0)
    gates = powers / jnp.sum(powers, axis=1, keepdims=True)
    gate_grad = jnp.where(chosen, gate_grad, 0.0)
    mean = jnp.sum(gates * gate_grad, axis=1, keepdims=True)
    logit_grad = (gates * (gate_grad - mean)).astype(bf16)
    fed_grad = times_transposed(logit_grad, router_ref[...]) + total[:, :features]
    scaled, inverse = norm_rows(middle_ref[...])
    back = norm_back(scaled, inverse, fed_grad * gain_ref[...])
    middle_grad = upstream_ref[...].astype(f32) + back
    middle_grad_ref[...] = middle_grad
    branch_ref[...] = middle_grad.astype(bf16)
    router_grad = contract_rows(logit_grad, fed_ref[...])
    gain_grad = jnp.sum(fed_grad * scaled, axis=0, keepdims=True)

    @pl.when(step == 0)
    def _():
        router_grad_ref[...] = router_grad
        gain_grad_ref[...] = gain_grad

    @pl.when(step > 0)
    def _():
        router_grad_ref[...] += router_grad
        gain_grad_ref[...] += gain_grad


def fed_grads(arrived, fed, middle, upstream, chosen, router, gain):
    length, features = fed.shape
    rows = length // 4
    split = lambda array: pl.BlockSpec((rows, array.shape[1]), lambda i: (i, 0))
    shapes = [
        jax.ShapeDtypeStruct((length, features), f32),
        jax.ShapeDtypeStruct((length, features), bf16),
        jax.ShapeDtypeStruct((LANES, features), f32),
        jax.ShapeDtypeStruct((1, features), f32),
    ]
    operands = [*arrived, fed, middle, upstream, chosen, router, gain]
    return pl.pallas_call(
        fed_grad_kernel,
        grid=(4,),
        in_specs=[split(a) for a in operands[:-2]] + [whole(router), whole(gain)],
        out_specs=[split(shapes[0]), split(shapes[1]), whole(shapes[2]), whole(shapes[3])],
        out_shape=shapes,
        compiler_params=pltpu.CompilerParams(vmem_limit_bytes=VMEM),
        cost_estimate=cost(1e8, 2e7),
    )(*operands)


def expert_grad_kernel(places_ref, *refs):
    slots = (len(refs) - 1) // 4
    fed, upstream, pair, gated = (refs[i * slots : (i + 1) * slots] for i in range(4))
    out_ref = refs[-1]
    inner = outer = None
    for k in range(slots):
        add_inner = contract_rows(fed[k][...], pair[k][0])
        add_outer = contract_rows(upstream[k][0], gated[k][0])
        inner = add_inner if inner is None else inner + add_inner
        outer = add_outer if outer is None else outer + add_outer
    out_ref[0, :, : 2 * FF] = inner.astype(out_ref.dtype)
    out_ref[0, :, 2 * FF :] = outer.astype(out_ref.dtype)


def expert_grads(places, fed, upstream, pairs, gated):
    length, features = fed[0].shape
    slots, count = len(pairs), pairs[0].shape[0]
    rows = features // 2
    column = pl.BlockSpec((length, rows), lambda e, i, at: (0, i))
    there = lambda k: pl.BlockSpec((1, length, rows), lambda e, i, at: (at[k], 0, i))
    each = lambda width: pl.BlockSpec((1, length, width), lambda e, i, at: (e, 0, 0))
    return pl.pallas_call(
        expert_grad_kernel,
        grid_spec=pltpu.PrefetchScalarGridSpec(
            num_scalar_prefetch=1,
            grid=(count, features // rows),
            in_specs=[column] * slots
            + [there(k) for k in range(slots)]
            + [each(2 * FF)] * slots
            + [each(FF)] * slots,
            out_specs=pl.BlockSpec((1, rows, 3 * FF), lambda e, i, at: (e, i, 0)),
        ),
        out_shape=jax.ShapeDtypeStruct((count, features, 3 * FF), bf16),
        compiler_params=pltpu.CompilerParams(vmem_limit_bytes=VMEM),
        cost_estimate=cost(6 * slots * count * length * features * FF, 8e7),
    )(places, *fed, *[upstream] * slots, *pairs, *gated)


def exchange(value, k):
    return lax.ppermute(value, "shard", [(i, i ^ k) for i in range(4)])


def inside(place):
    return (place == 1) | (place == 2)


def sources(place, count):
    if count != 4:
        return [place ^ k for k in range(count)]
    middle = inside(place)
    order = ((1, 3), (2, 1), (3, 2))
    return [place] + [place ^ jnp.where(middle, mid, out) for out, mid in order]


def after(value, *earlier):
    return lax.optimization_barrier((value, earlier))[0]


def line_gather(rows, place, count):
    if count != 4:
        everything = lax.all_gather(rows, "shard", axis=0)
        for source in sources(place, count):
            yield (pick(everything, source),) * 2
            yield
        return
    middle = inside(place)
    near = exchange(rows, 1)
    across = lax.ppermute(rows, "shard", [(1, 2), (2, 1)])
    made = yield rows, rows
    yield
    near_on, across_on = after((near, across), made)
    second_inside = lax.ppermute(near_on, "shard", [(1, 2), (2, 1)])
    second_outside = lax.ppermute(across_on, "shard", [(1, 0), (2, 3)])
    yield across, near
    yield
    third_outside = lax.ppermute(second_inside, "shard", [(1, 0), (2, 3)])
    yield near, second_outside
    yield
    yield second_inside, third_outside
    yield


def scatter_all(parts, place, count):
    stacked = jnp.stack(parts)
    ordered = jnp.stack([pick(stacked, place ^ d) for d in range(count)])
    return lax.psum_scatter(ordered, "shard", scatter_dimension=0, tiled=False)


def line_send(part, k):
    ways = {
        1: ([(0, 1), (3, 2)], [(1, 2), (2, 1)]),
        2: ([(0, 2), (3, 1)], [(1, 0), (2, 3)]),
        3: ([(0, 3), (3, 0)], [(1, 3), (2, 0)]),
    }
    return [lax.ppermute(part, "shard", way) for way in ways[k]]


def total_of(kept, arrived):
    total = kept.astype(f32)
    for part in arrived:
        total = total + part.astype(f32)
    return total


def hop(value, bit):
    return lax.ppermute(value, "rep", [(i, i ^ bit) for i in range(8)])


def pick(stacked, index, axis=0):
    return lax.dynamic_index_in_dim(stacked, index, axis, False)


def gather_near(mine):
    return jnp.stack([exchange(mine, k) for k in range(1, 4)])


def send_pairs(near):
    return [hop(near, 2 * m) for m in range(1, 4)]


def join_pairs(own, parts, earlier=()):
    own = jnp.concatenate([own[:, None], jnp.stack(parts)], axis=1)
    own = after(own, *earlier)
    return own, hop(own, 1)


def join_chip(term, special):
    kept, given = term
    return (kept.astype(f32) + hop(given, 1).astype(f32)).astype(bf16) if special else kept


def place_kernel(at_ref, own_ref, other_ref, attend_ref, output_ref):
    half = own_ref.shape[1]
    query, key = QUERY_HEADS * HEAD_WIDTH, KEY_VALUE_HEADS * HEAD_WIDTH
    for m in range(PAIRS):
        pair = at_ref[0] ^ m
        for side, ref in enumerate((own_ref, other_ref)):
            rows = pl.ds(pl.multiple_of((at_ref[1] ^ side) * half, half), half)
            start = 0
            for out_ref, base, width in (
                (attend_ref, 0, PAIR_QUERY),
                (attend_ref, query, PAIR_KEY),
                (attend_ref, query + key, PAIR_KEY),
                (output_ref, 0, PAIR_QUERY),
            ):
                columns = pl.ds(pl.multiple_of(base + pair * width, LANES), width)
                out_ref[rows, columns] = ref[m, :, start : start + width].astype(f32)
                start += width


def finish_pairs(plane, core, spot):
    piece = plane[0].astype(f32)
    for k in range(1, 4):
        piece = piece + exchange(plane[k], k).astype(f32)
    piece = piece.astype(plane.dtype)
    mine = jnp.stack([piece] + [hop(piece, 2 * m) for m in range(1, 4)])
    other = hop(mine, 1)
    rows = 2 * piece.shape[0]
    return pl.pallas_call(
        place_kernel,
        grid_spec=pltpu.PrefetchScalarGridSpec(
            num_scalar_prefetch=1,
            grid=(1,),
            in_specs=[whole(mine), whole(other)],
            out_specs=[
                pl.BlockSpec((rows, PAIRS * PAIR_WIDTH), lambda i, at: (0, 0)),
                pl.BlockSpec((rows, PAIRS * PAIR_QUERY), lambda i, at: (0, 0)),
            ],
        ),
        out_shape=[
            jax.ShapeDtypeStruct((rows, PAIRS * PAIR_WIDTH), f32),
            jax.ShapeDtypeStruct((rows, PAIRS * PAIR_QUERY), f32),
        ],
        compiler_params=pltpu.CompilerParams(vmem_limit_bytes=VMEM),
        cost_estimate=cost(1e6, 1e7),
    )(jnp.stack([spot, core]).astype(jnp.int32), mine, other)


def reduce_terms(terms):
    part = lax.psum_scatter(terms, "shard", scatter_dimension=1, tiled=False)
    return lax.psum(part, "rep")


def body(
    inputs,
    query_key_value_weight,
    output_weight,
    attention_gain,
    feed_gain,
    router_weight,
    expert_weight,
    routes,
    cotangent,
    *,
    places,
    ranks,
):
    length, features = inputs.shape
    own = query_key_value_weight.shape[0]
    local = expert_weight.shape[0]
    query_width = QUERY_HEADS * HEAD_WIDTH
    key_width = KEY_VALUE_HEADS * HEAD_WIDTH
    place, rank = lax.axis_index("shard"), lax.axis_index("rep")

    special = places == 4 and ranks == 8
    half = own // 2
    base, core, spot = (place, rank % 2, rank // 2) if special else (0, 0, 0)

    projection = query_key_value_weight

    def projection_share(pair, side):
        rows = lax.dynamic_slice_in_dim(projection, side * half, half, 0)
        return jnp.concatenate(
            [
                lax.dynamic_slice_in_dim(rows, pair * PAIR_QUERY, PAIR_QUERY, 1),
                lax.dynamic_slice_in_dim(rows, query_width + pair * PAIR_KEY, PAIR_KEY, 1),
                lax.dynamic_slice_in_dim(
                    rows, query_width + key_width + pair * PAIR_KEY, PAIR_KEY, 1
                ),
            ],
            axis=1,
        )

    def output_share(pair, side):
        return lax.dynamic_slice(
            output_weight, (side * half, pair * PAIR_QUERY), (half, PAIR_QUERY)
        )

    chosen_own = jnp.sum(
        (routes[:, :, None] == jnp.arange(EXPERTS, dtype=jnp.int32)).astype(f32), axis=1
    )
    small = jnp.concatenate(
        [
            attention_gain.reshape(-1),
            feed_gain.reshape(-1),
            router_weight.reshape(-1),
            chosen_own.astype(bf16).reshape(-1),
        ]
    )
    if special:
        projection_own = jnp.stack([projection_share(spot ^ m, core) for m in range(PAIRS)])
        output_own = jnp.stack([output_share(spot ^ m, core) for m in range(PAIRS)])
        projection_near = gather_near(projection_own[0])
        projection_near, projection_own, output_own = after(
            (projection_near, projection_own, output_own)
        )
        projection_sent = send_pairs(projection_near)
        extra = -(-small.size // (16 * PAIR_QUERY)) * 16
        below = jnp.pad(small, (0, extra * PAIR_QUERY - small.size)).reshape(extra, PAIR_QUERY)
        near = jnp.concatenate([output_own[0], below])
        near = gather_near(after(near, projection_near))
        output_near = near[:, :half]
        small_slots = jnp.concatenate(
            [small[None], near[:, half:].reshape(3, -1)[:, : small.size]]
        )
        small_all = jnp.stack([pick(small_slots, place ^ k) for k in range(4)])
        cotangent_sent = after(cotangent, projection_near)
    else:
        gathered = lax.all_gather(projection, "shard", axis=0)
        gathered_output = lax.all_gather(output_weight, "shard", axis=0)
        columns = jnp.concatenate(
            [
                gathered[:, :, :query_width].reshape(places, own, PAIRS, PAIR_QUERY),
                gathered[:, :, query_width : query_width + key_width].reshape(
                    places, own, PAIRS, PAIR_KEY
                ),
                gathered[:, :, query_width + key_width :].reshape(places, own, PAIRS, PAIR_KEY),
            ],
            axis=3,
        ).transpose(2, 0, 1, 3)
        attend_columns = (columns[:, :, :half], columns[:, :, half:])
        columns = gathered_output.reshape(places, own, PAIRS, PAIR_QUERY).transpose(2, 0, 1, 3)
        output_columns = (columns[:, :, :half], columns[:, :, half:])
        small_all = lax.all_gather(small, "shard", axis=0)
        cotangent_sent = cotangent

    upstream_all = lax.all_gather(cotangent_sent, "shard", axis=0)

    tables = rotary_tables(length, PAIR_QUERY + PAIR_KEY)
    residual = inputs.astype(f32)
    scaled_in, inverse_in = norm_rows(residual)
    attention_scale = small_all[:, :own].reshape(features).astype(f32)
    feed_scale = small_all[:, own : 2 * own].reshape(features).astype(f32)
    normed = (scaled_in * attention_scale).astype(bf16)
    where = jnp.stack([base, core]).astype(jnp.int32)

    def attention():
        if special:
            attend_weights = join_pairs(projection_own, [projection_near] + projection_sent)
            output_sent = send_pairs(after(output_near, attend_weights))
        else:
            attend_weights = attend_columns
        kept = attend_forward(where, normed, attend_weights, tables)
        if special:
            output_weights = join_pairs(output_own, [output_near] + output_sent, [kept[0]])
        else:
            output_weights = output_columns
        rows = middle_rows(where, kept[0], output_weights, inputs, feed_scale[None])
        return (*attend_weights, *output_weights, *kept, *rows)

    always = routes[0, 0] >= 0

    def apart(function, shapes):
        empty = lambda: tuple(jnp.zeros(*shape) for shape in shapes)
        return lax.cond(always, function, empty)

    share = (PAIRS, places, half)
    own_a, other_a, own_o, other_o, mixed, qkv, lse, middle, fed = apart(
        attention,
        [((*share, PAIR_WIDTH), bf16)] * 2
        + [((*share, PAIR_QUERY), bf16)] * 2
        + [
            ((PAIRS, length, PAIR_QUERY), bf16),
            ((PAIRS, length, PAIR_WIDTH), bf16),
            ((PAIRS, 8, length), f32),
            ((length, features), f32),
            ((length, features), bf16),
        ],
    )
    attend_weights, output_weights = (own_a, other_a), (own_o, other_o)
    small_late = after(small_all, fed)
    router_full = small_late[:, 2 * own : (2 + EXPERTS) * own].reshape(features, EXPERTS)
    chosen_all = small_late[:, (2 + EXPERTS) * own :].reshape(places, length, EXPERTS).astype(f32)
    router_wide = jnp.pad(router_full, ((0, 0), (0, LANES - EXPERTS)))
    chosen_wide = jnp.pad(chosen_all, ((0, 0), (0, 0), (0, LANES - EXPERTS)))
    rows, pair_grads, gated = [], [], []
    combined = places
    order = sources(place, places)
    entries = [*order, core, place * local, inside(place), 0, *order[1:]]
    table = jnp.stack([jnp.asarray(e, jnp.int32) for e in entries])
    fed_slots, rows_come, arriving = [], [], line_gather(fed, place, places)
    for k, source in enumerate(order):
        rows_up = cotangent[None] if k == 0 else upstream_all
        fed_k, row, combined, *kept = expert_slot(
            table, k, next(arriving), rows_up, chosen_wide, router_wide, expert_weight, combined
        )
        for held, value in zip((fed_slots, rows, pair_grads, gated), (fed_k, row, *kept)):
            held.append(value)
        arriving.send((row, upstream_all))
        if special and k:
            rows_come += line_send(row, k)
    expert_term = expert_grads(
        table,
        fed_slots,
        upstream_all,
        pair_grads,
        gated,
    )
    expert_total = lax.psum(expert_term, "rep").astype(f32)

    if special:
        arrived = [rows[0], *rows_come]
    else:
        arrived = [scatter_all(rows, place, places)]
    arrived = after(arrived, expert_term)

    combined = lax.all_to_all(after(combined, arrived), "shard", 0, 0)

    def rest():
        chosen = jnp.pad(chosen_own, ((0, 0), (0, LANES - EXPERTS)))
        middle_grad, branch_grad, router_term, feed_term = fed_grads(
            arrived, fed, middle, cotangent, chosen, router_wide, feed_scale[None]
        )
        normed_grad = jnp.zeros((length, features), f32)
        terms, chips = [None] * PAIRS, [None] * PAIRS
        steps = (3, 1, 2, 0)
        for i, m in enumerate(steps):
            ready = [chips[steps[i - 2]]] if i >= 2 else []
            own_term, other_term, normed_grad = attend_backward(
                where,
                m,
                after(branch_grad, *ready),
                output_weights,
                (mixed, qkv, lse),
                normed,
                attend_weights,
                tables,
                normed_grad,
            )
            terms[m] = (own_term, other_term)
            if i >= 1:
                chips[steps[i - 1]] = join_chip(terms[steps[i - 1]], special)
        if special:
            chips[0] = join_chip(terms[0], special)
            part = half // 2
            upper, lower = (lambda c: c[:, :part]), (lambda c: c[:, part:])
            add = lambda a, b: a.astype(f32) + b.astype(f32)
            over_x = hop(jnp.stack([upper(chips[1]), upper(chips[3])]), 2)
            over_y = hop(jnp.stack([lower(chips[2]), lower(chips[3])]), 4)
            upper_y = hop(add(upper(chips[2]), over_x[1]).astype(bf16), 4)
            lower_x = hop(add(lower(chips[1]), over_y[1]).astype(bf16), 2)
            plane = jnp.concatenate(
                [
                    add(upper(chips[0]), over_x[0]) + upper_y.astype(f32),
                    add(lower(chips[0]), over_y[0]) + lower_x.astype(f32),
                ],
                axis=1,
            )
            attend_total, output_total = finish_pairs(plane.astype(bf16), core, spot)
        else:
            stacked = jnp.stack([jnp.stack(term) for term in terms])
            weight_sums = reduce_terms(stacked.transpose(0, 2, 1, 3, 4))
            weight_sums = weight_sums.reshape(PAIRS, own, -1).transpose(1, 0, 2).astype(f32)
            attend_total = jnp.concatenate(
                [
                    weight_sums[:, :, :PAIR_QUERY].reshape(own, query_width),
                    weight_sums[:, :, PAIR_QUERY : PAIR_QUERY + PAIR_KEY].reshape(own, key_width),
                    weight_sums[:, :, PAIR_QUERY + PAIR_KEY : PAIR_WIDTH].reshape(own, key_width),
                ],
                axis=1,
            )
            output_total = weight_sums[:, :, PAIR_WIDTH:].reshape(own, query_width)

        attention_term = jnp.sum(normed_grad * scaled_in, axis=0)
        input_grad = (
            middle_grad + norm_back(scaled_in, inverse_in, normed_grad * attention_scale)
        ).astype(bf16)

        small_terms = jnp.concatenate(
            [attention_term[None], feed_term, router_term[:EXPERTS]], axis=0
        )
        if special:
            for axis, bit in (("rep", 1), ("rep", 2), ("rep", 4), ("shard", 1), ("shard", 2)):
                size = 8 if axis == "rep" else 4
                pairs = [(i, i ^ bit) for i in range(size)]
                small_terms = small_terms + lax.ppermute(small_terms, axis, pairs)
        else:
            small_terms = lax.psum(small_terms, ("rep", "shard"))
        small_sums = lax.dynamic_slice_in_dim(small_terms, place * own, own, 1)
        return (
            input_grad,
            attend_total,
            output_total,
            small_sums[0],
            small_sums[1],
            small_sums[2:].T,
        )

    shapes = (
        ((length, features), bf16),
        (query_key_value_weight.shape, f32),
        (output_weight.shape, f32),
        ((own,), f32),
        ((own,), f32),
        ((own, EXPERTS), f32),
    )
    grads = apart(rest, shapes)
    activations = (middle + jnp.sum(combined.astype(f32), axis=0)).astype(bf16)
    return (activations, *grads, expert_total)


def solution(mesh):
    in_specs = (
        P(("rep", "shard"), None),
        P("shard", None),
        P("shard", None),
        P("shard"),
        P("shard"),
        P("shard", None),
        P("shard", None, None),
        P(("rep", "shard"), None),
        P(("rep", "shard"), None),
    )
    out_specs = (
        P(("rep", "shard"), None),
        P(("rep", "shard"), None),
        P("shard", None),
        P("shard", None),
        P("shard"),
        P("shard"),
        P("shard", None),
        P("shard", None, None),
    )
    run = functools.partial(body, places=mesh.shape["shard"], ranks=mesh.shape["rep"])
    return jax.shard_map(run, mesh=mesh, in_specs=in_specs, out_specs=out_specs, check_vma=False)
```

```python
import functools

import jax
import jax.numpy as jnp
from jax import lax
from jax.experimental import pallas as pl
from jax.experimental.pallas import tpu as pltpu
from jax.sharding import PartitionSpec as P

QUERY_HEADS = 24
KEY_VALUE_HEADS = 8
HEAD_WIDTH = 64
FF = 512
EXPERTS = 16

EPSILON = 1e-06
MASKED = -1e30

GROUP = QUERY_HEADS // KEY_VALUE_HEADS
PAIRS = KEY_VALUE_HEADS // 2
PAIR_QUERY = 2 * GROUP * HEAD_WIDTH
PAIR_KEY = 2 * HEAD_WIDTH
PAIR_WIDTH = PAIR_QUERY + 2 * PAIR_KEY
BLOCK = 256
LANES = 128
VMEM = 60 * 2**20


def cost(flops, moved):
    return pl.CostEstimate(flops=int(flops), bytes_accessed=int(moved), transcendentals=0)

bf16 = jnp.bfloat16
f32 = jnp.float32


def dot(left, right):
    return jnp.dot(left, right, preferred_element_type=f32)


def contract_rows(left, right):
    return lax.dot_general(left, right, (((0,), (0,)), ((), ())), preferred_element_type=f32)


def times_transposed(left, right):
    return lax.dot_general(left, right, (((1,), (1,)), ((), ())), preferred_element_type=f32)


def norm_rows(value_rows):
    inverse = lax.rsqrt(jnp.mean(value_rows * value_rows, axis=-1, keepdims=True) + EPSILON)
    return (value_rows * inverse, inverse)


def norm_back(scaled, inverse, upstream):
    return inverse * (upstream - scaled * jnp.mean(upstream * scaled, axis=-1, keepdims=True))


def rotary_tables(length, width):
    half = HEAD_WIDTH // 2
    frequency = 10000.0 ** (-2.0 * jnp.arange(half, dtype=f32) / HEAD_WIDTH)
    angles = jnp.arange(length, dtype=f32)[:, None] * frequency[None, :]
    cosine, sine = jnp.cos(angles), jnp.sin(angles)
    heads = width // HEAD_WIDTH
    return (
        jnp.tile(jnp.concatenate([cosine, cosine], axis=1), (1, heads)),
        jnp.tile(jnp.concatenate([-sine, sine], axis=1), (1, heads)),
    )


def rotate(values, cosine, sine):
    width = values.shape[1]
    half = HEAD_WIDTH // 2
    lane = lax.broadcasted_iota(jnp.int32, values.shape, 1)
    swapped = jnp.where(
        lane % HEAD_WIDTH < half,
        pltpu.roll(values, width - half, 1),
        pltpu.roll(values, half, 1),
    )
    return values * cosine + swapped * sine


def causal_block():
    shape = (BLOCK, BLOCK)
    return lax.broadcasted_iota(jnp.int32, shape, 0) <= lax.broadcasted_iota(jnp.int32, shape, 1)


def stack_rows(parts):
    return parts[0] if len(parts) == 1 else jnp.concatenate(parts, axis=0)


def natural(at_ref, own_ref, other_ref, held_ref):
    shards, half = own_ref.shape[1:3]
    for k in range(shards):
        for side, ref in enumerate((own_ref, other_ref)):
            start = (at_ref[0] ^ k) * (2 * half) + (at_ref[1] ^ side) * half
            held_ref[pl.ds(pl.multiple_of(start, half), half), :] = ref[0, k]


def attend_forward_kernel(
    at_ref, normed_ref, own_ref, other_ref, cosine_ref, sine_ref, mixed_ref, qkv_ref, lse_ref, weight_ref
):
    length = normed_ref.shape[0]
    natural(at_ref, own_ref, other_ref, weight_ref)
    keep = causal_block()
    projected = dot(normed_ref[...], weight_ref[...])
    rotated = rotate(projected[:, : PAIR_QUERY + PAIR_KEY], cosine_ref[...], sine_ref[...])
    query = (rotated[:, :PAIR_QUERY] * HEAD_WIDTH**-0.5).astype(bf16)
    key = rotated[:, PAIR_QUERY:].astype(bf16)
    value = projected[:, PAIR_QUERY + PAIR_KEY :].astype(bf16)
    qkv_ref[0, :, :PAIR_QUERY] = query
    qkv_ref[0, :, PAIR_QUERY : PAIR_QUERY + PAIR_KEY] = key
    qkv_ref[0, :, PAIR_QUERY + PAIR_KEY :] = value
    value_columns = value.T
    outs = []
    for head in range(2 * GROUP):
        kv = (head // GROUP) * HEAD_WIDTH
        columns = []
        for block in range(length // BLOCK):
            start, stop = block * BLOCK, (block + 1) * BLOCK
            scores = times_transposed(
                key[:stop, kv : kv + HEAD_WIDTH],
                query[start:stop, head * HEAD_WIDTH : (head + 1) * HEAD_WIDTH],
            )
            parts = [scores[:start]] if block else []
            scores = stack_rows(parts + [jnp.where(keep, scores[start:], MASKED)])
            top = jnp.max(scores, axis=0, keepdims=True)
            powers = jnp.exp(scores - top)
            total = jnp.sum(powers, axis=0, keepdims=True)
            probability = (powers * (1.0 / total)).astype(bf16)
            columns.append(dot(value_columns[kv : kv + HEAD_WIDTH, :stop], probability))
            lse_ref[0, head, start:stop] = (top + jnp.log(total))[0]
        outs.append(jnp.concatenate(columns, axis=1))
    mixed_ref[0] = jnp.concatenate(outs, axis=0).T.astype(bf16)


def whole(array):
    return pl.BlockSpec(array.shape, lambda *_: (0,) * array.ndim)


def entry(array, index=None):
    rest = (0,) * (array.ndim - 1)
    return pl.BlockSpec(
        (1,) + array.shape[1:], lambda p, at: ((p if index is None else index),) + rest
    )


def attend_forward(at, normed, weights, tables):
    length, features = normed.shape
    shapes = [
        jax.ShapeDtypeStruct((PAIRS, length, PAIR_QUERY), bf16),
        jax.ShapeDtypeStruct((PAIRS, length, PAIR_WIDTH), bf16),
        jax.ShapeDtypeStruct((PAIRS, 8, length), f32),
    ]
    return pl.pallas_call(
        attend_forward_kernel,
        grid_spec=pltpu.PrefetchScalarGridSpec(
            num_scalar_prefetch=1,
            grid=(PAIRS,),
            in_specs=[whole(normed)] + [entry(w) for w in weights] + [whole(t) for t in tables],
            out_specs=[entry(shape) for shape in shapes],
            scratch_shapes=[pltpu.VMEM((features, PAIR_WIDTH), bf16)],
        ),
        out_shape=shapes,
        compiler_params=pltpu.CompilerParams(vmem_limit_bytes=VMEM),
        cost_estimate=cost(2e10, 2e7),
    )(at, normed, *weights, *tables)


def middle_kernel(
    at_ref, mixed_ref, own_ref, other_ref, input_ref, gain_ref, middle_ref, fed_ref, weight_ref
):
    step = pl.program_id(0)
    natural(at_ref, own_ref, other_ref, weight_ref)
    added = times_transposed(mixed_ref[0], weight_ref[...])

    @pl.when(step == 0)
    def _():
        middle_ref[...] = input_ref[...].astype(f32) + added

    @pl.when(step > 0)
    def _():
        middle_ref[...] += added

    @pl.when(step == pl.num_programs(0) - 1)
    def _():
        fed_ref[...] = (norm_rows(middle_ref[...])[0] * gain_ref[...]).astype(bf16)


def middle_rows(at, mixed, weights, inputs, gain):
    length, features = inputs.shape
    shapes = [jax.ShapeDtypeStruct((length, features), kind) for kind in (f32, bf16)]
    return pl.pallas_call(
        middle_kernel,
        grid_spec=pltpu.PrefetchScalarGridSpec(
            num_scalar_prefetch=1,
            grid=(PAIRS,),
            in_specs=[entry(mixed)] + [entry(w) for w in weights] + [whole(inputs), whole(gain)],
            out_specs=[whole(shape) for shape in shapes],
            scratch_shapes=[pltpu.VMEM((features, PAIR_QUERY), bf16)],
        ),
        out_shape=shapes,
        compiler_params=pltpu.CompilerParams(vmem_limit_bytes=VMEM),
        cost_estimate=cost(2.4e9, 1e7),
    )(at, mixed, *weights, inputs, gain)


def attend_backward_kernel(
    at_ref,
    branch_ref,
    own_output_ref,
    other_output_ref,
    mixed_ref,
    qkv_ref,
    lse_ref,
    normed_ref,
    own_weight_ref,
    other_weight_ref,
    cosine_ref,
    sine_ref,
    total_ref,
    own_term_ref,
    other_term_ref,
    grad_ref,
    output_ref,
    weight_ref,
    term_ref,
):
    length = branch_ref.shape[0]
    natural(at_ref, own_output_ref, other_output_ref, output_ref)
    natural(at_ref, own_weight_ref, other_weight_ref, weight_ref)
    keep = causal_block()
    blocks = length // BLOCK
    mixed_grad = dot(branch_ref[...], output_ref[...]).astype(bf16)
    query = qkv_ref[0, :, :PAIR_QUERY]
    key = qkv_ref[0, :, PAIR_QUERY : PAIR_QUERY + PAIR_KEY]
    value = qkv_ref[0, :, PAIR_QUERY + PAIR_KEY :]
    scaled_key = (key.astype(f32) * HEAD_WIDTH**-0.5).T.astype(bf16)
    query_grads, key_grads, value_grads = [], [], []
    for side in range(2):
        kv = side * HEAD_WIDTH
        key_part = key[:, kv : kv + HEAD_WIDTH]
        value_part = value[:, kv : kv + HEAD_WIDTH]
        key_grad, value_grad = [None] * blocks, [None] * blocks
        for head in range(side * GROUP, (side + 1) * GROUP):
            column = head * HEAD_WIDTH
            columns = []
            for block in range(blocks):
                start, stop = block * BLOCK, (block + 1) * BLOCK
                query_rows = query[start:stop, column : column + HEAD_WIDTH]
                upstream = mixed_grad[start:stop, column : column + HEAD_WIDTH]
                scores = times_transposed(key_part[:stop], query_rows)
                prob_grad = times_transposed(value_part[:stop], upstream)
                probability = jnp.exp(scores - lse_ref[0, head, start:stop][None, :])
                parts = [probability[:start]] if block else []
                probability = stack_rows(parts + [jnp.where(keep, probability[start:], 0.0)])
                shift = jnp.sum(probability * prob_grad, axis=0, keepdims=True)
                score_grad = (probability * (prob_grad - shift)).astype(bf16)
                value_add = dot(probability.astype(bf16), upstream)
                key_add = dot(score_grad, query_rows)
                for j in range(block + 1):
                    rows = slice(j * BLOCK, (j + 1) * BLOCK)
                    value_grad[j] = (
                        value_add[rows] if value_grad[j] is None else value_grad[j] + value_add[rows]
                    )
                    key_grad[j] = (
                        key_add[rows] if key_grad[j] is None else key_grad[j] + key_add[rows]
                    )
                columns.append(dot(scaled_key[kv : kv + HEAD_WIDTH, :stop], score_grad))
            query_grads.append(jnp.concatenate(columns, axis=1))
        key_grads.append(stack_rows(key_grad))
        value_grads.append(stack_rows(value_grad))
    turned = rotate(
        jnp.concatenate([jnp.concatenate(query_grads, axis=0).T] + key_grads, axis=1),
        cosine_ref[...],
        -sine_ref[...],
    )
    projected_grad = jnp.concatenate([turned] + value_grads, axis=1).astype(bf16)
    term_ref[:, :PAIR_WIDTH] = contract_rows(normed_ref[...], projected_grad).astype(bf16)
    term_ref[:, PAIR_WIDTH:] = contract_rows(branch_ref[...], mixed_ref[0]).astype(bf16)
    shards, half = own_weight_ref.shape[1:3]
    for k in range(shards):
        for side, ref in enumerate((own_term_ref, other_term_ref)):
            start = (at_ref[0] ^ k) * (2 * half) + (at_ref[1] ^ side) * half
            ref[k] = term_ref[pl.ds(pl.multiple_of(start, half), half), :]
    grad_ref[...] = total_ref[...] + times_transposed(projected_grad, weight_ref[...])


def attend_backward(at, m, branch_grad, output, saved, normed, weights, tables, total):
    length, features = branch_grad.shape
    shards, half = weights[0].shape[1:3]
    width = PAIR_WIDTH + PAIR_QUERY
    term = jax.ShapeDtypeStruct((shards, half, width), bf16)
    shapes = [term, term, jax.ShapeDtypeStruct((length, features), f32)]
    ones = [*output, *saved]
    operands = [branch_grad, *ones, normed, *weights, *tables, total]
    specs = [whole(branch_grad)] + [entry(one, m) for one in ones] + [whole(normed)]
    specs += [entry(w, m) for w in weights] + [whole(t) for t in tables] + [whole(total)]
    return pl.pallas_call(
        attend_backward_kernel,
        grid_spec=pltpu.PrefetchScalarGridSpec(
            num_scalar_prefetch=1,
            grid=(1,),
            in_specs=specs,
            out_specs=[whole(shape) for shape in shapes],
            scratch_shapes=[
                pltpu.VMEM((features, PAIR_QUERY), bf16),
                pltpu.VMEM((features, PAIR_WIDTH), bf16),
                pltpu.VMEM((features, width), bf16),
            ],
        ),
        out_shape=shapes,
        input_output_aliases={len(operands): 2},
        compiler_params=pltpu.CompilerParams(vmem_limit_bytes=VMEM),
        cost_estimate=cost(9e9, 1.5e7),
    )(at, *operands)


def expert_kernel(
    sequences,
    whole_slot,
    table_ref,
    inner_ref,
    outer_ref,
    upstream_ref,
    chosen_ref,
    router_ref,
    weight_ref,
    *refs,
):
    (fed_ref, row_ref, pair_ref, gated_ref, back_ref, *refs) = refs[-10 if whole_slot else -8 :]
    if whole_slot:
        combined_ref, gates_ref, gate_grad_ref, row_total, combined_total = refs
    else:
        gates_ref, gate_grad_ref, row_total = refs
    step, steps = pl.program_id(0), pl.num_programs(0)
    index = table_ref[sequences + 1] + step
    lane = lax.broadcasted_iota(jnp.int32, gates_ref.shape, 1)

    @pl.when(step == 0)
    def _():
        @pl.when(table_ref[sequences + 2] > 0)
        def _():
            fed_ref[...] = inner_ref[...]

        @pl.when(table_ref[sequences + 2] == 0)
        def _():
            fed_ref[...] = outer_ref[...]

        logits = dot(fed_ref[...], router_ref[...])
        chosen = chosen_ref[0] > 0.0
        logits = jnp.where(chosen, logits, MASKED)
        powers = jnp.where(chosen, jnp.exp(logits - jnp.max(logits, axis=1, keepdims=True)), 0.0)
        gates_ref[...] = powers / jnp.sum(powers, axis=1, keepdims=True)
        gate_grad_ref[...] = jnp.zeros_like(gate_grad_ref)

    gate = jnp.sum(jnp.where(lane == index, gates_ref[...], 0.0), axis=1, keepdims=True)
    gate_grad = None
    width = FF // 2
    for start in range(0, FF, width):
        stop = start + width
        gate_part = dot(fed_ref[...], weight_ref[0, :, start:stop])
        up_part = dot(fed_ref[...], weight_ref[0, :, FF + start : FF + stop])
        raw_grad = dot(upstream_ref[0], weight_ref[0, :, 2 * FF + start : 2 * FF + stop])
        sigma = jax.nn.sigmoid(gate_part)
        activated = gate_part * sigma
        hidden = activated * up_part
        part = jnp.sum(hidden * raw_grad, axis=1, keepdims=True)
        gate_grad = part if gate_grad is None else gate_grad + part
        hidden_grad = gate * raw_grad
        slope = sigma * (1.0 + gate_part * (1.0 - sigma))
        pair_ref[0, :, start:stop] = (hidden_grad * up_part * slope).astype(bf16)
        pair_ref[0, :, FF + start : FF + stop] = (hidden_grad * activated).astype(bf16)
        gated_ref[0, :, start:stop] = (gate * hidden).astype(bf16)
    gate_grad_ref[...] += jnp.where(lane == index, gate_grad, 0.0)
    sums = [(row_total, times_transposed(pair_ref[0], weight_ref[0, :, : 2 * FF]))]
    if whole_slot:
        sums.append((combined_total, times_transposed(gated_ref[0], weight_ref[0, :, 2 * FF :])))

    @pl.when(step == 0)
    def _():
        for total, added in sums:
            total[...] = added

    @pl.when(step > 0)
    def _():
        for total, added in sums:
            total[...] += added

    @pl.when(step == steps - 1)
    def _():
        row_ref[...] = row_total[...].astype(bf16)
        back_ref[0] = gate_grad_ref[...].T[:EXPERTS]
        if whole_slot:
            combined_ref[0] = combined_total[...].astype(bf16)


def expert_slot(at, k, choices, upstream, chosen, router, weights, gate_grads, combined, sequences):
    length, features = choices[0].shape
    count = weights.shape[0]
    whole_slot = k < sequences - 1
    held = [] if gate_grads is None else [gate_grads, combined][: 1 + whole_slot]
    full = lambda *shape: pl.BlockSpec(shape, lambda e, at: (0,) * len(shape))
    each = lambda *shape: pl.BlockSpec((1,) + shape, lambda e, at: (e,) + (0,) * len(shape))
    there = lambda i, *shape: pl.BlockSpec(
        (1,) + shape, lambda e, at: (at[i],) + (0,) * len(shape)
    )
    rows = pltpu.VMEM((length, features), f32)
    gates = pltpu.VMEM((length, LANES), f32)
    out_specs = [
        full(length, features),
        full(length, features),
        each(length, 2 * FF),
        each(length, FF),
        there(k, EXPERTS, length),
    ]
    out_shape = [
        jax.ShapeDtypeStruct((length, features), bf16),
        jax.ShapeDtypeStruct((length, features), bf16),
        jax.ShapeDtypeStruct((count, length, 2 * FF), bf16),
        jax.ShapeDtypeStruct((count, length, FF), bf16),
        jax.ShapeDtypeStruct((sequences, EXPERTS, length), f32),
    ]
    if whole_slot:
        out_specs.append(there(k, length, features))
        out_shape.append(jax.ShapeDtypeStruct((sequences, length, features), bf16))
    return pl.pallas_call(
        functools.partial(expert_kernel, sequences, whole_slot),
        grid_spec=pltpu.PrefetchScalarGridSpec(
            num_scalar_prefetch=1,
            grid=(count,),
            in_specs=[
                full(length, features),
                full(length, features),
                there(sequences + 3 + k, length, features),
                there(k, length, LANES),
                full(features, LANES),
                each(features, 3 * FF),
            ]
            + [pl.BlockSpec(memory_space=pl.ANY)] * len(held),
            out_specs=out_specs,
            scratch_shapes=[gates, gates, rows] + [rows] * whole_slot,
        ),
        out_shape=out_shape,
        input_output_aliases={7 + i: 4 + i for i in range(len(held))},
        compiler_params=pltpu.CompilerParams(vmem_limit_bytes=VMEM),
        cost_estimate=cost(12 * count * length * features * FF, 3.2e7),
    )(at, *choices, upstream, chosen, router, weights, *held)


def combine_kernel(table_ref, gated_ref, weight_ref, _, combined_ref, total_ref):
    step = pl.program_id(0)
    added = times_transposed(gated_ref[0], weight_ref[0])

    @pl.when(step == 0)
    def _():
        total_ref[...] = added

    @pl.when(step > 0)
    def _():
        total_ref[...] += added

    @pl.when(step == pl.num_programs(0) - 1)
    def _():
        combined_ref[0] = total_ref[...].astype(bf16)


def combine_slot(at, k, gated, weights, combined):
    count, length, _ = gated.shape
    features = weights.shape[1]
    return pl.pallas_call(
        combine_kernel,
        grid_spec=pltpu.PrefetchScalarGridSpec(
            num_scalar_prefetch=1,
            grid=(count,),
            in_specs=[
                pl.BlockSpec((1, length, FF), lambda e, at: (e, 0, 0)),
                pl.BlockSpec((1, features, FF), lambda e, at: (e, 0, 2)),
                pl.BlockSpec(memory_space=pl.ANY),
            ],
            out_specs=pl.BlockSpec((1, length, features), lambda e, at: (at[k], 0, 0)),
            scratch_shapes=[pltpu.VMEM((length, features), f32)],
        ),
        out_shape=jax.ShapeDtypeStruct(combined.shape, bf16),
        input_output_aliases={3: 0},
        compiler_params=pltpu.CompilerParams(vmem_limit_bytes=VMEM),
        cost_estimate=cost(2 * count * length * features * FF, 1e7),
    )(at, gated, weights, combined)


def fed_grad_kernel(*refs):
    arrived = refs[:-11]
    (
        back_ref,
        fed_ref,
        middle_ref,
        upstream_ref,
        chosen_ref,
        router_ref,
        gain_ref,
        middle_grad_ref,
        branch_ref,
        router_grad_ref,
        gain_grad_ref,
    ) = refs[-11:]
    step = pl.program_id(0)
    total = arrived[0][...].astype(f32)
    for ref in arrived[1:]:
        total = total + ref[...].astype(f32)
    columns = back_ref[0]
    for i in range(1, back_ref.shape[0]):
        columns = columns + back_ref[i]
    empty = jnp.zeros((LANES - EXPERTS, columns.shape[1]), f32)
    gate_grad = jnp.concatenate([columns, empty], axis=0).T
    chosen = chosen_ref[...] > 0.0
    logits = jnp.where(chosen, dot(fed_ref[...], router_ref[...]), MASKED)
    powers = jnp.where(chosen, jnp.exp(logits - jnp.max(logits, axis=1, keepdims=True)), 0.0)
    gates = powers / jnp.sum(powers, axis=1, keepdims=True)
    gate_grad = jnp.where(chosen, gate_grad, 0.0)
    mean = jnp.sum(gates * gate_grad, axis=1, keepdims=True)
    logit_grad = (gates * (gate_grad - mean)).astype(bf16)
    fed_grad = times_transposed(logit_grad, router_ref[...]) + total
    scaled, inverse = norm_rows(middle_ref[...])
    back = norm_back(scaled, inverse, fed_grad * gain_ref[...])
    middle_grad = upstream_ref[...].astype(f32) + back
    middle_grad_ref[...] = middle_grad
    branch_ref[...] = middle_grad.astype(bf16)
    router_grad = contract_rows(logit_grad, fed_ref[...])
    gain_grad = jnp.sum(fed_grad * scaled, axis=0, keepdims=True)

    @pl.when(step == 0)
    def _():
        router_grad_ref[...] = router_grad
        gain_grad_ref[...] = gain_grad

    @pl.when(step > 0)
    def _():
        router_grad_ref[...] += router_grad
        gain_grad_ref[...] += gain_grad


def fed_grads(arrived, gate_grads, fed, middle, upstream, chosen, router, gain):
    length, features = fed.shape
    rows = length // 4
    split = lambda array: pl.BlockSpec((rows, array.shape[1]), lambda i: (i, 0))
    shapes = [
        jax.ShapeDtypeStruct((length, features), f32),
        jax.ShapeDtypeStruct((length, features), bf16),
        jax.ShapeDtypeStruct((LANES, features), f32),
        jax.ShapeDtypeStruct((1, features), f32),
    ]
    operands = [*arrived, gate_grads, fed, middle, upstream, chosen, router, gain]
    columns = pl.BlockSpec((*gate_grads.shape[:2], rows), lambda i: (0, 0, i))
    specs = [split(a) for a in arrived] + [columns] + [split(a) for a in operands[-6:-2]]
    return pl.pallas_call(
        fed_grad_kernel,
        grid=(4,),
        in_specs=specs + [whole(router), whole(gain)],
        out_specs=[split(shapes[0]), split(shapes[1]), whole(shapes[2]), whole(shapes[3])],
        out_shape=shapes,
        compiler_params=pltpu.CompilerParams(vmem_limit_bytes=VMEM),
        cost_estimate=cost(1e8, 2e7),
    )(*operands)


def expert_grad_kernel(places_ref, *refs):
    slots = (len(refs) - 1) // 4
    fed, upstream, pair, gated = (refs[i * slots : (i + 1) * slots] for i in range(4))
    out_ref = refs[-1]
    inner = outer = None
    for k in range(slots):
        add_inner = contract_rows(fed[k][...], pair[k][0])
        add_outer = contract_rows(upstream[k][0], gated[k][0])
        inner = add_inner if inner is None else inner + add_inner
        outer = add_outer if outer is None else outer + add_outer
    out_ref[0, :, : 2 * FF] = inner.astype(out_ref.dtype)
    out_ref[0, :, 2 * FF :] = outer.astype(out_ref.dtype)


def expert_grads(places, fed, upstream, pairs, gated):
    length, features = fed[0].shape
    slots, count = len(pairs), pairs[0].shape[0]
    rows = features // 2
    column = pl.BlockSpec((length, rows), lambda e, i, at: (0, i))
    there = lambda k: pl.BlockSpec((1, length, rows), lambda e, i, at: (at[k], 0, i))
    each = lambda width: pl.BlockSpec((1, length, width), lambda e, i, at: (e, 0, 0))
    return pl.pallas_call(
        expert_grad_kernel,
        grid_spec=pltpu.PrefetchScalarGridSpec(
            num_scalar_prefetch=1,
            grid=(count, features // rows),
            in_specs=[column] * slots
            + [there(k) for k in range(slots)]
            + [each(2 * FF)] * slots
            + [each(FF)] * slots,
            out_specs=pl.BlockSpec((1, rows, 3 * FF), lambda e, i, at: (e, i, 0)),
        ),
        out_shape=jax.ShapeDtypeStruct((count, features, 3 * FF), bf16),
        compiler_params=pltpu.CompilerParams(vmem_limit_bytes=VMEM),
        cost_estimate=cost(6 * slots * count * length * features * FF, 8e7),
    )(places, *fed, *[upstream] * slots, *pairs, *gated)


def exchange(value, k):
    return lax.ppermute(value, "shard", [(i, i ^ k) for i in range(4)])


def inside(place):
    return (place == 1) | (place == 2)


def sources(place, count):
    if count != 4:
        return [place ^ k for k in range(count)]
    middle = inside(place)
    order = ((1, 3), (2, 1), (3, 2))
    return [place] + [place ^ jnp.where(middle, mid, out) for out, mid in order]


def after(value, *earlier):
    return lax.optimization_barrier((value, earlier))[0]


def line_gather(rows, place, count):
    if count != 4:
        everything = lax.all_gather(rows, "shard", axis=0)
        for source in sources(place, count):
            yield (pick(everything, source),) * 2
            yield
        return
    middle = inside(place)
    near = exchange(rows, 1)
    across = lax.ppermute(rows, "shard", [(1, 2), (2, 1)])
    made = yield rows, rows
    yield
    near_on, across_on = after((near, across), made)
    second_inside = lax.ppermute(near_on, "shard", [(1, 2), (2, 1)])
    second_outside = lax.ppermute(across_on, "shard", [(1, 0), (2, 3)])
    yield across, near
    yield
    third_outside = lax.ppermute(second_inside, "shard", [(1, 0), (2, 3)])
    yield near, second_outside
    yield
    yield second_inside, third_outside
    yield


def scatter_all(parts, place, count):
    stacked = jnp.stack(parts)
    ordered = jnp.stack([pick(stacked, place ^ d) for d in range(count)])
    return lax.psum_scatter(ordered, "shard", scatter_dimension=0, tiled=False)


def line_send(part, k):
    ways = {
        1: ([(0, 1), (3, 2)], [(1, 2), (2, 1)]),
        2: ([(0, 2), (3, 1)], [(1, 0), (2, 3)]),
        3: ([(0, 3), (3, 0)], [(1, 3), (2, 0)]),
    }
    return [lax.ppermute(part, "shard", way) for way in ways[k]]


def total_of(kept, arrived):
    total = kept.astype(f32)
    for part in arrived:
        total = total + part.astype(f32)
    return total


def hop(value, bit):
    return lax.ppermute(value, "rep", [(i, i ^ bit) for i in range(8)])


def pick(stacked, index, axis=0):
    return lax.dynamic_index_in_dim(stacked, index, axis, False)


def gather_near(mine):
    return jnp.stack([exchange(mine, k) for k in range(1, 4)])


def send_pairs(near):
    return [hop(near, 2 * m) for m in range(1, 4)]


def join_pairs(own, parts, earlier=()):
    own = jnp.concatenate([own[:, None], jnp.stack(parts)], axis=1)
    own = after(own, *earlier)
    return own, hop(own, 1)


def join_chip(term, special):
    kept, given = term
    return (kept.astype(f32) + hop(given, 1).astype(f32)).astype(bf16) if special else kept


def place_kernel(at_ref, own_ref, other_ref, attend_ref, output_ref):
    half = own_ref.shape[1]
    query, key = QUERY_HEADS * HEAD_WIDTH, KEY_VALUE_HEADS * HEAD_WIDTH
    for m in range(PAIRS):
        pair = at_ref[0] ^ m
        for side, ref in enumerate((own_ref, other_ref)):
            rows = pl.ds(pl.multiple_of((at_ref[1] ^ side) * half, half), half)
            start = 0
            for out_ref, base, width in (
                (attend_ref, 0, PAIR_QUERY),
                (attend_ref, query, PAIR_KEY),
                (attend_ref, query + key, PAIR_KEY),
                (output_ref, 0, PAIR_QUERY),
            ):
                columns = pl.ds(pl.multiple_of(base + pair * width, LANES), width)
                out_ref[rows, columns] = ref[m, :, start : start + width].astype(f32)
                start += width


def finish_pairs(plane, core, spot):
    piece = plane[0].astype(f32)
    for k in range(1, 4):
        piece = piece + exchange(plane[k], k).astype(f32)
    piece = piece.astype(plane.dtype)
    mine = jnp.stack([piece] + [hop(piece, 2 * m) for m in range(1, 4)])
    other = hop(mine, 1)
    rows = 2 * piece.shape[0]
    return pl.pallas_call(
        place_kernel,
        grid_spec=pltpu.PrefetchScalarGridSpec(
            num_scalar_prefetch=1,
            grid=(1,),
            in_specs=[whole(mine), whole(other)],
            out_specs=[
                pl.BlockSpec((rows, PAIRS * PAIR_WIDTH), lambda i, at: (0, 0)),
                pl.BlockSpec((rows, PAIRS * PAIR_QUERY), lambda i, at: (0, 0)),
            ],
        ),
        out_shape=[
            jax.ShapeDtypeStruct((rows, PAIRS * PAIR_WIDTH), f32),
            jax.ShapeDtypeStruct((rows, PAIRS * PAIR_QUERY), f32),
        ],
        compiler_params=pltpu.CompilerParams(vmem_limit_bytes=VMEM),
        cost_estimate=cost(1e6, 1e7),
    )(jnp.stack([spot, core]).astype(jnp.int32), mine, other)


def reduce_terms(terms):
    part = lax.psum_scatter(terms, "shard", scatter_dimension=1, tiled=False)
    return lax.psum(part, "rep")


def body(
    inputs,
    query_key_value_weight,
    output_weight,
    attention_gain,
    feed_gain,
    router_weight,
    expert_weight,
    routes,
    cotangent,
    *,
    places,
    ranks,
):
    length, features = inputs.shape
    own = query_key_value_weight.shape[0]
    local = expert_weight.shape[0]
    query_width = QUERY_HEADS * HEAD_WIDTH
    key_width = KEY_VALUE_HEADS * HEAD_WIDTH
    place, rank = lax.axis_index("shard"), lax.axis_index("rep")

    special = places == 4 and ranks == 8
    half = own // 2
    base, core, spot = (place, rank % 2, rank // 2) if special else (0, 0, 0)

    projection = query_key_value_weight

    def projection_share(pair, side):
        rows = lax.dynamic_slice_in_dim(projection, side * half, half, 0)
        return jnp.concatenate(
            [
                lax.dynamic_slice_in_dim(rows, pair * PAIR_QUERY, PAIR_QUERY, 1),
                lax.dynamic_slice_in_dim(rows, query_width + pair * PAIR_KEY, PAIR_KEY, 1),
                lax.dynamic_slice_in_dim(
                    rows, query_width + key_width + pair * PAIR_KEY, PAIR_KEY, 1
                ),
            ],
            axis=1,
        )

    def output_share(pair, side):
        return lax.dynamic_slice(
            output_weight, (side * half, pair * PAIR_QUERY), (half, PAIR_QUERY)
        )

    chosen_own = jnp.sum(
        (routes[:, :, None] == jnp.arange(EXPERTS, dtype=jnp.int32)).astype(f32), axis=1
    )
    small = jnp.concatenate(
        [
            attention_gain.reshape(-1),
            feed_gain.reshape(-1),
            router_weight.reshape(-1),
            chosen_own.astype(bf16).reshape(-1),
        ]
    )
    if special:
        projection_own = jnp.stack([projection_share(spot ^ m, core) for m in range(PAIRS)])
        output_own = jnp.stack([output_share(spot ^ m, core) for m in range(PAIRS)])
        projection_near = gather_near(projection_own[0])
        projection_near, projection_own, output_own = after(
            (projection_near, projection_own, output_own)
        )
        projection_sent = send_pairs(projection_near)
        extra = -(-small.size // (16 * PAIR_QUERY)) * 16
        below = jnp.pad(small, (0, extra * PAIR_QUERY - small.size)).reshape(extra, PAIR_QUERY)
        near = jnp.concatenate([output_own[0], below])
        near = gather_near(after(near, projection_near))
        output_near = near[:, :half]
        small_slots = jnp.concatenate(
            [small[None], near[:, half:].reshape(3, -1)[:, : small.size]]
        )
        small_all = jnp.stack([pick(small_slots, place ^ k) for k in range(4)])
        cotangent_sent = after(cotangent, projection_near)
    else:
        gathered = lax.all_gather(projection, "shard", axis=0)
        gathered_output = lax.all_gather(output_weight, "shard", axis=0)
        columns = jnp.concatenate(
            [
                gathered[:, :, :query_width].reshape(places, own, PAIRS, PAIR_QUERY),
                gathered[:, :, query_width : query_width + key_width].reshape(
                    places, own, PAIRS, PAIR_KEY
                ),
                gathered[:, :, query_width + key_width :].reshape(places, own, PAIRS, PAIR_KEY),
            ],
            axis=3,
        ).transpose(2, 0, 1, 3)
        attend_columns = (columns[:, :, :half], columns[:, :, half:])
        columns = gathered_output.reshape(places, own, PAIRS, PAIR_QUERY).transpose(2, 0, 1, 3)
        output_columns = (columns[:, :, :half], columns[:, :, half:])
        small_all = lax.all_gather(small, "shard", axis=0)
        cotangent_sent = cotangent

    upstream_all = lax.all_gather(cotangent_sent, "shard", axis=0)

    tables = rotary_tables(length, PAIR_QUERY + PAIR_KEY)
    residual = inputs.astype(f32)
    scaled_in, inverse_in = norm_rows(residual)
    attention_scale = small_all[:, :own].reshape(features).astype(f32)
    feed_scale = small_all[:, own : 2 * own].reshape(features).astype(f32)
    normed = (scaled_in * attention_scale).astype(bf16)
    where = jnp.stack([base, core]).astype(jnp.int32)

    def attention():
        if special:
            attend_weights = join_pairs(projection_own, [projection_near] + projection_sent)
            output_sent = send_pairs(after(output_near, attend_weights))
        else:
            attend_weights = attend_columns
        kept = attend_forward(where, normed, attend_weights, tables)
        if special:
            output_weights = join_pairs(output_own, [output_near] + output_sent, [kept[0]])
        else:
            output_weights = output_columns
        rows = middle_rows(where, kept[0], output_weights, inputs, feed_scale[None])
        return (*attend_weights, *output_weights, *kept, *rows)

    always = routes[0, 0] >= 0

    def apart(function, shapes):
        empty = lambda: tuple(jnp.zeros(*shape) for shape in shapes)
        return lax.cond(always, function, empty)

    share = (PAIRS, places, half)
    own_a, other_a, own_o, other_o, mixed, qkv, lse, middle, fed = apart(
        attention,
        [((*share, PAIR_WIDTH), bf16)] * 2
        + [((*share, PAIR_QUERY), bf16)] * 2
        + [
            ((PAIRS, length, PAIR_QUERY), bf16),
            ((PAIRS, length, PAIR_WIDTH), bf16),
            ((PAIRS, 8, length), f32),
            ((length, features), f32),
            ((length, features), bf16),
        ],
    )
    attend_weights, output_weights = (own_a, other_a), (own_o, other_o)
    small_late = after(small_all, fed)
    router_full = small_late[:, 2 * own : (2 + EXPERTS) * own].reshape(features, EXPERTS)
    chosen_all = small_late[:, (2 + EXPERTS) * own :].reshape(places, length, EXPERTS).astype(f32)
    router_wide = jnp.pad(router_full, ((0, 0), (0, LANES - EXPERTS)))
    chosen_wide = jnp.pad(chosen_all, ((0, 0), (0, 0), (0, LANES - EXPERTS)))
    rows, pair_grads, gated = [], [], []
    combined = gate_grads = None
    order = sources(place, places)
    entries = [*order, core, place * local, inside(place), 0, *order[1:]]
    table = jnp.stack([jnp.asarray(e, jnp.int32) for e in entries])
    fed_slots, rows_come, arriving = [], [], line_gather(fed, place, places)
    for k, source in enumerate(order):
        rows_up = cotangent[None] if k == 0 else upstream_all
        fed_k, row, pair_k, gated_k, gate_grads, *buffer = expert_slot(
            table,
            k,
            next(arriving),
            rows_up,
            chosen_wide,
            router_wide,
            expert_weight,
            gate_grads,
            combined,
            places,
        )
        combined = buffer[0] if buffer else combined
        for held, value in zip((fed_slots, rows, pair_grads, gated), (fed_k, row, pair_k, gated_k)):
            held.append(value)
        arriving.send((row, upstream_all))
        if special and k:
            rows_come += line_send(row, k)
    expert_term = expert_grads(
        table,
        fed_slots,
        upstream_all,
        pair_grads,
        gated,
    )
    expert_total = lax.psum(expert_term, "rep").astype(f32)

    if special:
        arrived = [rows[0], *rows_come]
    else:
        arrived = [scatter_all(rows, place, places)]
    arrived = after(arrived, expert_term)

    combined = combine_slot(
        table, places - 1, after(gated[-1], expert_term), expert_weight, combined
    )
    gate_grads = lax.all_to_all(gate_grads, "shard", 0, 0)
    combined = lax.all_to_all(after(combined, arrived), "shard", 0, 0)

    def rest():
        chosen = jnp.pad(chosen_own, ((0, 0), (0, LANES - EXPERTS)))
        middle_grad, branch_grad, router_term, feed_term = fed_grads(
            arrived, gate_grads, fed, middle, cotangent, chosen, router_wide, feed_scale[None]
        )
        normed_grad = jnp.zeros((length, features), f32)
        terms, chips = [None] * PAIRS, [None] * PAIRS
        steps = (3, 1, 2, 0)
        for i, m in enumerate(steps):
            ready = [chips[steps[i - 2]]] if i >= 2 else []
            own_term, other_term, normed_grad = attend_backward(
                where,
                m,
                after(branch_grad, *ready),
                output_weights,
                (mixed, qkv, lse),
                normed,
                attend_weights,
                tables,
                normed_grad,
            )
            terms[m] = (own_term, other_term)
            if i >= 1:
                chips[steps[i - 1]] = join_chip(terms[steps[i - 1]], special)
        if special:
            chips[0] = join_chip(terms[0], special)
            part = half // 2
            upper, lower = (lambda c: c[:, :part]), (lambda c: c[:, part:])
            add = lambda a, b: a.astype(f32) + b.astype(f32)
            over_x = hop(jnp.stack([upper(chips[1]), upper(chips[3])]), 2)
            over_y = hop(jnp.stack([lower(chips[2]), lower(chips[3])]), 4)
            upper_y = hop(add(upper(chips[2]), over_x[1]).astype(bf16), 4)
            lower_x = hop(add(lower(chips[1]), over_y[1]).astype(bf16), 2)
            plane = jnp.concatenate(
                [
                    add(upper(chips[0]), over_x[0]) + upper_y.astype(f32),
                    add(lower(chips[0]), over_y[0]) + lower_x.astype(f32),
                ],
                axis=1,
            )
            attend_total, output_total = finish_pairs(plane.astype(bf16), core, spot)
        else:
            stacked = jnp.stack([jnp.stack(term) for term in terms])
            weight_sums = reduce_terms(stacked.transpose(0, 2, 1, 3, 4))
            weight_sums = weight_sums.reshape(PAIRS, own, -1).transpose(1, 0, 2).astype(f32)
            attend_total = jnp.concatenate(
                [
                    weight_sums[:, :, :PAIR_QUERY].reshape(own, query_width),
                    weight_sums[:, :, PAIR_QUERY : PAIR_QUERY + PAIR_KEY].reshape(own, key_width),
                    weight_sums[:, :, PAIR_QUERY + PAIR_KEY : PAIR_WIDTH].reshape(own, key_width),
                ],
                axis=1,
            )
            output_total = weight_sums[:, :, PAIR_WIDTH:].reshape(own, query_width)

        attention_term = jnp.sum(normed_grad * scaled_in, axis=0)
        input_grad = (
            middle_grad + norm_back(scaled_in, inverse_in, normed_grad * attention_scale)
        ).astype(bf16)

        small_terms = jnp.concatenate(
            [attention_term[None], feed_term, router_term[:EXPERTS]], axis=0
        )
        if special:
            for axis, bit in (("rep", 1), ("rep", 2), ("rep", 4), ("shard", 1), ("shard", 2)):
                size = 8 if axis == "rep" else 4
                pairs = [(i, i ^ bit) for i in range(size)]
                small_terms = small_terms + lax.ppermute(small_terms, axis, pairs)
        else:
            small_terms = lax.psum(small_terms, ("rep", "shard"))
        small_sums = lax.dynamic_slice_in_dim(small_terms, place * own, own, 1)
        return (
            input_grad,
            attend_total,
            output_total,
            small_sums[0],
            small_sums[1],
            small_sums[2:].T,
        )

    shapes = (
        ((length, features), bf16),
        (query_key_value_weight.shape, f32),
        (output_weight.shape, f32),
        ((own,), f32),
        ((own,), f32),
        ((own, EXPERTS), f32),
    )
    grads = apart(rest, shapes)
    activations = (middle + jnp.sum(combined.astype(f32), axis=0)).astype(bf16)
    return (activations, *grads, expert_total)


def solution(mesh):
    in_specs = (
        P(("rep", "shard"), None),
        P("shard", None),
        P("shard", None),
        P("shard"),
        P("shard"),
        P("shard", None),
        P("shard", None, None),
        P(("rep", "shard"), None),
        P(("rep", "shard"), None),
    )
    out_specs = (
        P(("rep", "shard"), None),
        P(("rep", "shard"), None),
        P("shard", None),
        P("shard", None),
        P("shard"),
        P("shard"),
        P("shard", None),
        P("shard", None, None),
    )
    run = functools.partial(body, places=mesh.shape["shard"], ranks=mesh.shape["rep"])
    return jax.shard_map(run, mesh=mesh, in_specs=in_specs, out_specs=out_specs, check_vma=False)
```
